32 devices in a mesh: dp: 8 (over y, x, core), vox: 4 (over z).
Axes of the slice: x: 2, y: 2, z: 4, core: 2. Of those that a mesh axis runs over, the one named last changes fastest.
Arguments:
- kernels: bfloat16 [384, 16384], P('dp', 'vox'), may hold values from -0.046875 to 0.046875
- observed: float32 [8, 384], P(None, 'dp'), may hold values from -6 to 6
- initial: float32 [8, 16384], P(None, 'vox'), may hold values from -6 to 6
- threshold: float32 [8, 16, 2], replicated, may hold values from 0.05 to 0.5
Outputs:
- coefficients: float32 [8, 16384], P(None, 'vox')
- residual: float32 [8, 384], P(None, 'dp')
The draws below stay inside these ranges and needn't reach their ends.
All inputs are finite; a program needn't handle non-finite values.
Results may differ from the reference program's by a relative error of at most 0.0043.
Values may be sent and summed in bfloat16 or wider, within the bound.
No kernel may reach another device: no remote copies, remote signals or barrier semaphores. Data moves between devices by JAX's collectives and lax.ppermute only.
A program may use at most 64 MiB of HBM per device.

```python
import math
import jax
import jax.numpy as jnp
from jax import lax

LAYERS = 16
CELLS_DEV = 256
MODELS = 8
ITERS = 2
VOXELS = 16384
ROWS = 384
N_VOX = 4


def level_of(key, dims, cuts, least, top_value):
    def one(dim, shards_of):
        draws = jax.random.uniform(jax.random.fold_in(jax.random.fold_in(key, 6), dim), (shards_of,), jnp.float32, least / len(cuts), top_value / len(cuts))
        return jnp.repeat(jnp.exp(draws), dims[dim] // shards_of).reshape((-1,) + (1,) * (len(dims) - dim - 1))

    level = one(*cuts[0])
    for cut in cuts[1:]:
        level = level * one(*cut)
    return level


def scatter_about(key, dims, width, reach, pieces=(), kind=jnp.bfloat16):
    array = width * jax.random.normal(key, dims, jnp.float32)
    if pieces:
        array = array * level_of(key, dims, pieces, -0.22, 0.18)
    return jnp.clip(array, -reach, reach).astype(kind)


def setup_inputs(seed: int = 0) -> dict:
    splits = jax.random.split(jax.random.key(seed), 5)
    kernels = scatter_about(splits[0], (ROWS, VOXELS), VOXELS ** -0.5, 0.046875, ((0, 8), (1, 4)))
    observed = scatter_about(splits[1], (MODELS, ROWS), 1.0, 6.0, ((1, 8),), jnp.float32)
    initial = scatter_about(splits[2], (MODELS, VOXELS), 1.0, 6.0, ((1, 4),), jnp.float32)
    threshold = jnp.clip(jnp.exp(jax.random.uniform(splits[3], (MODELS, LAYERS, 2), jnp.float32, math.log(0.05), math.log(0.5))), 0.05, 0.5)
    return dict(kernels=kernels, observed=observed, initial=initial, threshold=threshold)


step_size = 0.5


def to_curve(flat_model):
    models_count = flat_model.shape[0]
    half_cells = CELLS_DEV // 2
    arranged = flat_model.reshape(models_count, N_VOX, LAYERS, 2, half_cells)
    arranged = jnp.transpose(arranged, (0, 2, 3, 1, 4))
    return arranged.reshape(models_count, LAYERS, 2, N_VOX * half_cells)


def from_curve(arranged):
    models_count = arranged.shape[0]
    half_cells = CELLS_DEV // 2
    spread = arranged.reshape(models_count, LAYERS, 2, N_VOX, half_cells)
    spread = jnp.transpose(spread, (0, 3, 1, 2, 4))
    return spread.reshape(models_count, N_VOX * LAYERS * CELLS_DEV)


def forward_wave(arranged):
    even_part = arranged[:, :, 0, :]
    odd_part = arranged[:, :, 1, :]
    detail = odd_part - 0.5 * (even_part + jnp.roll(even_part, -1, axis=-1))
    smooth = even_part + 0.25 * (jnp.roll(detail, 1, axis=-1) + detail)
    return jnp.stack([smooth, detail], axis=2)


def inverse_wave(arranged):
    smooth = arranged[:, :, 0, :]
    detail = arranged[:, :, 1, :]
    even_part = smooth - 0.25 * (jnp.roll(detail, 1, axis=-1) + detail)
    odd_part = detail + 0.5 * (even_part + jnp.roll(even_part, -1, axis=-1))
    return jnp.stack([even_part, odd_part], axis=2)


def shrink(values, thresholds):
    return jnp.sign(values) * jnp.maximum(jnp.abs(values) - thresholds, 0.0)


def reference(kernels, observed, initial, threshold):
    thresholds = threshold[:, :, :, None]
    wavelets = to_curve(initial)
    voxel_model = from_curve(inverse_wave(wavelets)).astype(jnp.bfloat16)
    residual = observed
    for iteration in range(ITERS):
        predicted = lax.dot_general(voxel_model, kernels, (((1,), (1,)), ((), ())), preferred_element_type=jnp.float32)
        residual = observed - predicted
        gradient = jnp.dot(residual.astype(jnp.bfloat16), kernels, preferred_element_type=jnp.float32)
        updated = wavelets + step_size * forward_wave(to_curve(gradient))
        wavelets = shrink(updated, thresholds)
        if iteration + 1 < ITERS:
            voxel_model = from_curve(inverse_wave(wavelets)).astype(jnp.bfloat16)
    return from_curve(wavelets), residual
```

```python
import functools

import jax
import jax.numpy as jnp
from jax import lax
from jax.experimental import pallas as pl
from jax.experimental.pallas import tpu as pltpu
from jax.sharding import PartitionSpec as P

step_size = 0.5
LANES = 128
F32 = jnp.float32
BF16 = jnp.bfloat16

E_LAST, E_FIRST, E_SECOND, O_LAST, O_FIRST = range(5)
KINDS = 5


def lanes_of(shape):
    return lax.broadcasted_iota(jnp.int32, shape, len(shape) - 1)


def turned(x, by):
    return pltpu.roll(x, by % LANES, x.ndim - 1)


def shifted_in(x, by, edge):
    free = 0 if by == 1 else LANES - 1
    return jnp.where(lanes_of(x.shape) == free, edge, turned(x, by))


def column(x, lane):
    return jnp.broadcast_to(x[:, lane : lane + 1], x.shape)


def edge_tile(pair_of, layers, base):
    tile = None
    for layer in reversed(range(layers)):
        even, odd = pair_of(layer)
        lane = lanes_of(even.shape)
        fresh = jnp.where((lane >= LANES - 1) | (lane <= 1), even, turned(odd, 3))
        if tile is None:
            tile = jnp.zeros_like(fresh)
        tile = jnp.where((lane >= LANES - 1) | (lane <= 3), fresh, turned(tile, KINDS))
    lane = lanes_of(tile.shape)
    tile = turned(tile, base + 1)
    return jnp.where((lane >= base) & (lane < base + KINDS * layers), tile, 0.0)


def kind_lane(lane, base, kind):
    return lax.rem(lane - base + KINDS * LANES, KINDS) == kind


def shrink(values, cutoff):
    return values - jnp.clip(values, -cutoff, cutoff)


def layer_tiles(ref, layer):
    start = layer * 2 * LANES
    return ref[:, start : start + LANES], ref[:, start + LANES : start + 2 * LANES]


def nt_dot(a, b):
    return lax.dot_general(a, b, (((1,), (1,)), ((), ())), preferred_element_type=F32)


def first_kernel(layers, wave_ref, k_ref, packet_ref, tile):
    rows = k_ref.shape[0]
    models = wave_ref.shape[0]
    parts = []
    for layer in range(layers):
        smooth, detail = layer_tiles(wave_ref, layer)
        even = smooth - 0.25 * (shifted_in(detail, 1, 0.0) + detail)
        odd = detail + 0.5 * (even + shifted_in(even, -1, 0.0))
        parts += [even, odd]
    model = jnp.concatenate(parts, axis=1).astype(BF16)
    tile[...] = edge_tile(lambda l: layer_tiles(wave_ref, l), layers, rows)
    tile[:, :rows] = nt_dot(model, k_ref[...])
    whole = tile[...]
    high = whole.astype(BF16).astype(F32)
    packet_ref[rows:, :] = jnp.concatenate([high, whole - high], axis=0).astype(BF16)
    edges = edge_tile(lambda l: tuple(t.astype(F32) for t in layer_tiles(k_ref, l)), layers, rows)
    packet_ref[:rows, :] = edges.astype(BF16)


def second_kernel(layers, n_vox, *refs):
    (observed_ref, *packets, out_ref, halo_ref, held) = refs
    models, rows = observed_ref.shape
    me = lax.axis_index("vox")
    for distance, packet in enumerate(packets):
        held[me ^ distance] = packet[...]
    lane = lanes_of((models, LANES))

    def edge_values(which):
        both = held[which, rows:, :].astype(F32)
        return both[:models] + both[models:]

    def mixed(from_left, from_right):
        at = lanes_of(from_left.shape)
        left = kind_lane(at, rows, E_LAST) | kind_lane(at, rows, O_LAST)
        return jnp.where(left, from_left, from_right)

    edge = [edge_values(z) for z in range(n_vox)]
    terms, columns = [], []
    for z in range(n_vox):
        before, after = edge[z - 1], edge[(z + 1) % n_vox]
        last = turned(before, E_FIRST - O_LAST)
        last_odd = turned(before, O_FIRST - O_LAST)
        next_smooth = turned(after, O_LAST - E_FIRST)
        next_detail = turned(after, O_LAST - O_FIRST)
        next_even = next_smooth - 0.25 * (edge[z] + next_detail)
        term = jnp.where(
            kind_lane(lane, rows, E_FIRST),
            -0.25 * last,
            jnp.where(
                kind_lane(lane, rows, O_FIRST),
                -0.125 * last_odd,
                jnp.where(kind_lane(lane, rows, O_LAST), 0.5 * next_even, 0.0),
            ),
        )
        inside = (lane >= rows) & (lane < rows + KINDS * layers)
        terms.append(jnp.where(inside, term, 0.0).astype(BF16))
        columns.append(held[z, :rows, :])
    predicted = nt_dot(jnp.concatenate(terms, axis=1), jnp.concatenate(columns, axis=1))
    shares = edge[0]
    for z in range(1, n_vox):
        shares = shares + edge[z]
    predicted = predicted + shares[:, :rows]
    left, right = lax.rem(me + n_vox - 1, n_vox), lax.rem(me + 1, n_vox)
    out_ref[:rows, :] = mixed(held[left, :rows, :].astype(F32), held[right, :rows, :].astype(F32))
    out_ref[rows:, :] = jnp.zeros((2 * models, LANES), F32)
    out_ref[rows : rows + models, :rows] = observed_ref[...] - predicted
    out_ref[rows + models :, :rows] = observed_ref[...]
    halo_ref[...] = mixed(edge_values(left), edge_values(right))


def back_projected(residual, k_ref, halo_columns, g_ref):
    width = k_ref.shape[1]
    sent = residual.astype(BF16)
    g_ref[:, :width] = jnp.dot(sent, k_ref[...], preferred_element_type=F32).astype(BF16)
    g_ref[:, width:] = jnp.dot(sent, halo_columns, preferred_element_type=F32).astype(BF16)


def third_kernel(mine_ref, other_ref, k_ref, g_ref, columns_ref, observed_ref, held, lhs):
    core = lax.rem(lax.axis_index("dp"), 2)
    models = g_ref.shape[0]
    rows = mine_ref.shape[0] - 2 * models
    held[core] = mine_ref[...]
    held[1 - core] = other_ref[...]
    lhs[...] = jnp.zeros_like(lhs)
    observed_ref[...] = jnp.zeros_like(observed_ref)
    for c in range(2):
        lhs[:, c * rows : (c + 1) * rows] = held[c, rows : rows + models, :rows]
        observed_ref[:, c * rows : (c + 1) * rows] = held[c, rows + models :, :rows]
    columns = jnp.concatenate([held[c, :rows, :] for c in range(2)], axis=0).astype(BF16)
    columns_ref[...] = columns
    back_projected(lhs[:, : 2 * rows], k_ref, columns, g_ref)


def tree_sum(values):
    while len(values) > 1:
        values = [a + b for a, b in zip(values[::2], values[1::2])]
    return values[0]


def stepped_layer(layer, base, gradient, wave_ref, cut_ref, halo, full):
    even, odd = gradient(layer)
    edge = gradient(None)
    lane = base + KINDS * layer

    def at(tile, kind):
        return column(tile, lane + kind)

    cut_s, cut_d = column(cut_ref, 2 * layer), column(cut_ref, 2 * layer + 1)
    smooth, detail = layer_tiles(wave_ref, layer)
    even_next = at(edge, E_FIRST)
    detail_g = odd - 0.5 * (even + shifted_in(even, -1, even_next))
    before_g = at(edge, O_LAST) - 0.5 * (at(edge, E_LAST) + column(even, 0))
    smooth_g = even + 0.25 * (shifted_in(detail_g, 1, before_g) + detail_g)
    smooth = shrink(smooth + step_size * smooth_g, cut_s)
    detail = shrink(detail + step_size * detail_g, cut_d)
    if not full:
        return smooth, detail
    after_g = at(edge, O_FIRST) - 0.5 * (even_next + at(edge, E_SECOND))
    next_g = even_next + 0.25 * (column(detail_g, LANES - 1) + after_g)
    before = shrink(at(halo, O_LAST) + step_size * before_g, cut_d)
    next_s = shrink(at(halo, E_FIRST) + step_size * next_g, cut_s)
    after = shrink(at(halo, O_FIRST) + step_size * after_g, cut_d)
    return smooth, detail, before, next_s, after


def gradient_reader(refs):
    width = refs[0].shape[1]

    def read(layer):
        if layer is None:
            return tree_sum([r[:, width - LANES :].astype(F32) for r in refs])
        start = 2 * LANES * layer
        return tuple(
            tree_sum([r[:, s : s + LANES].astype(F32) for r in refs]) for s in (start, start + LANES)
        )

    return functools.lru_cache(None)(read)


def fourth_kernel(layers, base, wave_ref, cut_ref, halo_ref, k_ref, *refs):
    *g_refs, new_ref, pred_ref = refs
    gradient = gradient_reader(g_refs)
    cut, halo = cut_ref[...], halo_ref[...]
    parts = []
    for layer in range(layers):
        smooth, detail, before, next_s, after = stepped_layer(layer, base, gradient, wave_ref, cut, halo, True)
        start = 2 * LANES * layer
        new_ref[:, start : start + LANES] = smooth
        new_ref[:, start + LANES : start + 2 * LANES] = detail
        even = smooth - 0.25 * (shifted_in(detail, 1, before) + detail)
        even_next = next_s - 0.25 * (column(detail, LANES - 1) + after)
        odd = detail + 0.5 * (even + shifted_in(even, -1, even_next))
        parts += [even, odd]
    model = jnp.concatenate(parts, axis=1).astype(BF16)
    pred_ref[...] = jnp.zeros_like(pred_ref)
    pred_ref[:, : k_ref.shape[0]] = nt_dot(model, k_ref[...])


def fifth_kernel(k_ref, columns_ref, observed_ref, *refs):
    *shares, g_ref, residual_ref = refs
    core = lax.rem(lax.axis_index("dp"), 2)
    rows = residual_ref.shape[1]
    residual = observed_ref[...] - tree_sum([s[...] for s in shares])
    back_projected(residual[:, : 2 * rows], k_ref, columns_ref[...], g_ref)
    residual_ref[...] = jnp.where(core == 0, residual[:, :rows], residual[:, rows : 2 * rows])


def sixth_kernel(layers, base, wave_ref, cut_ref, *refs):
    *g_refs, new_ref = refs
    gradient = gradient_reader(g_refs)
    cut = cut_ref[...]
    for layer in range(layers):
        smooth, detail = stepped_layer(layer, base, gradient, wave_ref, cut, None, False)
        start = 2 * LANES * layer
        new_ref[:, start : start + LANES] = smooth
        new_ref[:, start + LANES : start + 2 * LANES] = detail


def from_partner(x, axis, distance):
    return lax.ppermute(x, axis, [(i, i ^ distance) for i in range(lax.axis_size(axis))])


def shares_of(x, axis, lowest):
    size = lax.axis_size(axis) // lowest
    while size > 4:
        parts = [x] + [from_partner(x, axis, lowest * d) for d in range(1, 4)]
        x = tree_sum([p.astype(F32) for p in parts]).astype(x.dtype)
        lowest, size = lowest * 4, size // 4
    return [x] + [from_partner(x, axis, lowest * d) for d in range(1, size)]


def call(kernel, out_shape, scratch=(), *args):
    return pl.pallas_call(
        kernel,
        out_shape=out_shape,
        in_specs=[pl.BlockSpec(memory_space=pltpu.VMEM)] * len(args),
        out_specs=jax.tree.map(lambda _: pl.BlockSpec(memory_space=pltpu.VMEM), out_shape),
        scratch_shapes=list(scratch),
    )(*args)


def body(kernels, observed, initial, threshold):
    models, width = initial.shape
    rows = kernels.shape[0]
    layers = threshold.shape[1]
    n_vox = lax.axis_size("vox")
    assert width == 2 * layers * LANES and rows + KINDS * layers <= LANES and 2 * rows <= LANES
    shape = jax.ShapeDtypeStruct
    cut = threshold.reshape(models, layers * 2)
    cut = jnp.pad(cut, ((0, 0), (0, LANES - 2 * layers)))

    packet_rows = rows + 2 * models
    packet = call(
        functools.partial(first_kernel, layers),
        shape((packet_rows, LANES), BF16),
        [pltpu.VMEM((models, LANES), F32)],
        initial,
        kernels,
    )
    packets = [packet] + [from_partner(packet, "vox", d) for d in range(1, n_vox)]

    other = from_partner(kernels, "dp", 1)
    first_core = lax.rem(lax.axis_index("dp"), 2) == 0
    both = jnp.where(first_core, jnp.concatenate([kernels, other]), jnp.concatenate([other, kernels]))

    mine, halo = call(
        functools.partial(second_kernel, layers, n_vox),
        (shape((packet_rows, LANES), F32), shape((models, LANES), F32)),
        [pltpu.VMEM((n_vox, packet_rows, LANES), BF16)],
        observed,
        *packets,
    )
    theirs = from_partner(mine, "dp", 1)
    g, columns, observed_both = call(
        third_kernel,
        (
            shape((models, width + LANES), BF16),
            shape((2 * rows, LANES), BF16),
            shape((models, LANES), F32),
        ),
        [pltpu.VMEM((2, packet_rows, LANES), F32), pltpu.VMEM((models, LANES), F32)],
        mine,
        theirs,
        both,
    )
    wavelets, predicted = call(
        functools.partial(fourth_kernel, layers, rows),
        (shape((models, width), F32), shape((models, LANES), F32)),
        (),
        initial,
        cut,
        halo,
        both,
        *shares_of(g, "dp", 2),
    )
    g, residual = call(
        fifth_kernel,
        (shape((models, width + LANES), BF16), shape((models, rows), F32)),
        (),
        both,
        columns,
        observed_both,
        *shares_of(predicted, "vox", 1),
    )
    coefficients = call(
        functools.partial(sixth_kernel, layers, rows),
        shape((models, width), F32),
        (),
        wavelets,
        cut,
        *shares_of(g, "dp", 2),
    )
    return coefficients, residual


def solution(mesh):
    return jax.shard_map(
        body,
        mesh=mesh,
        in_specs=(P("dp", "vox"), P(None, "dp"), P(None, "vox"), P()),
        out_specs=(P(None, "vox"), P(None, "dp")),
        check_vma=False,
    )
```

```python
import functools

import jax
import jax.numpy as jnp
from jax import lax
from jax.experimental import pallas as pl
from jax.experimental.pallas import tpu as pltpu
from jax.sharding import PartitionSpec as P

step_size = 0.5
LANES = 128
F32 = jnp.float32
BF16 = jnp.bfloat16

E_LAST, E_FIRST, E_SECOND, O_LAST, O_FIRST = range(5)
KINDS = 5


def lanes_of(shape):
    return lax.broadcasted_iota(jnp.int32, shape, len(shape) - 1)


def turned(x, by):
    return pltpu.roll(x, by % LANES, x.ndim - 1)


def shifted_in(x, by, edge):
    free = 0 if by == 1 else LANES - 1
    return jnp.where(lanes_of(x.shape) == free, edge, turned(x, by))


def column(x, lane):
    return jnp.broadcast_to(x[:, lane : lane + 1], x.shape)


def edge_tile(pair_of, layers, base):
    tile = None
    for layer in range(layers):
        even, odd = pair_of(layer)
        start = base + KINDS * layer
        lane = lanes_of(even.shape)
        if tile is None:
            tile = jnp.zeros_like(even)
        tile = jnp.where((lane >= start) & (lane < start + 3), turned(even, start + 1), tile)
        tile = jnp.where((lane >= start + 3) & (lane < start + 5), turned(odd, start + 4), tile)
    return tile


def kind_lane(lane, base, kind):
    return lax.rem(lane - base + KINDS * LANES, KINDS) == kind


def shrink(values, cutoff):
    return values - jnp.clip(values, -cutoff, cutoff)


def layer_tiles(ref, layer):
    start = layer * 2 * LANES
    return ref[:, start : start + LANES], ref[:, start + LANES : start + 2 * LANES]


def stacked(ref, layers):
    tiles = [layer_tiles(ref, layer) for layer in range(layers)]
    return tuple(jnp.concatenate([t[p] for t in tiles], axis=0).astype(F32) for p in range(2))


def stacked_lane(tile, lanes):
    return jnp.concatenate([tile[:, lane : lane + 1] for lane in lanes], axis=0)


def unstacked(even, odd, models):
    rows = [slice(start, start + models) for start in range(0, even.shape[0], models)]
    return jnp.concatenate([t[r] for r in rows for t in (even, odd)], axis=1)


def nt_dot(a, b):
    return lax.dot_general(a, b, (((1,), (1,)), ((), ())), preferred_element_type=F32)


def inverse_wave(smooth, detail, before, next_even_of):
    even = smooth - 0.25 * (shifted_in(detail, 1, before) + detail)
    odd = detail + 0.5 * (even + shifted_in(even, -1, next_even_of(detail)))
    return even, odd


def first_kernel(layers, wave_ref, k_ref, packet_ref, tile):
    rows = k_ref.shape[0]
    models = wave_ref.shape[0]
    even, odd = inverse_wave(*stacked(wave_ref, layers), 0.0, lambda detail: 0.0)
    tile[...] = edge_tile(lambda l: layer_tiles(wave_ref, l), layers, rows)
    edges = edge_tile(lambda l: tuple(t.astype(F32) for t in layer_tiles(k_ref, l)), layers, rows)
    packet_ref[:rows, :] = edges.astype(BF16)
    tile[:, :rows] = nt_dot(unstacked(even, odd, models).astype(BF16), k_ref[...])
    whole = tile[...]
    high = whole.astype(BF16).astype(F32)
    packet_ref[rows:, :] = jnp.concatenate([high, whole - high], axis=0).astype(BF16)


def second_kernel(layers, n_vox, *refs):
    (observed_ref, *packets, out_ref, halo_ref, held) = refs
    models, rows = observed_ref.shape
    me = lax.axis_index("vox")
    for distance, packet in enumerate(packets):
        held[me ^ distance] = packet[...]
    lane = lanes_of((models, LANES))

    def edge_values(which):
        both = held[which, rows:, :].astype(F32)
        return both[:models] + both[models:]

    def mixed(from_left, from_right):
        at = lanes_of(from_left.shape)
        left = kind_lane(at, rows, E_LAST) | kind_lane(at, rows, O_LAST)
        return jnp.where(left, from_left, from_right)

    edge = [edge_values(z) for z in range(n_vox)]
    terms, columns = [], []
    for z in range(n_vox):
        before, after = edge[z - 1], edge[(z + 1) % n_vox]
        last = turned(before, E_FIRST - O_LAST)
        last_odd = turned(before, O_FIRST - O_LAST)
        next_smooth = turned(after, O_LAST - E_FIRST)
        next_detail = turned(after, O_LAST - O_FIRST)
        next_even = next_smooth - 0.25 * (edge[z] + next_detail)
        term = jnp.where(
            kind_lane(lane, rows, E_FIRST),
            -0.25 * last,
            jnp.where(
                kind_lane(lane, rows, O_FIRST),
                -0.125 * last_odd,
                jnp.where(kind_lane(lane, rows, O_LAST), 0.5 * next_even, 0.0),
            ),
        )
        inside = (lane >= rows) & (lane < rows + KINDS * layers)
        terms.append(jnp.where(inside, term, 0.0).astype(BF16))
        columns.append(held[z, :rows, :])
    predicted = nt_dot(jnp.concatenate(terms, axis=1), jnp.concatenate(columns, axis=1))
    shares = edge[0]
    for z in range(1, n_vox):
        shares = shares + edge[z]
    predicted = predicted + shares[:, :rows]
    left, right = lax.rem(me + n_vox - 1, n_vox), lax.rem(me + 1, n_vox)
    out_ref[:rows, :] = mixed(held[left, :rows, :].astype(F32), held[right, :rows, :].astype(F32))
    out_ref[rows:, :] = jnp.zeros((2 * models, LANES), F32)
    out_ref[rows : rows + models, :rows] = observed_ref[...] - predicted
    out_ref[rows + models :, :rows] = observed_ref[...]
    halo_ref[...] = mixed(edge_values(left), edge_values(right))


def in_core_order(mine, other, work):
    core = lax.rem(lax.axis_index("dp"), 2)

    @pl.when(core == 0)
    def _():
        work(mine, other)

    @pl.when(core == 1)
    def _():
        work(other, mine)


def back_projected(mine, other, g_ref):
    width = mine[1].shape[1]

    def work(*cores):
        sent = [residual.astype(BF16) for residual, _, _ in cores]
        g_ref[:, :width] = sum(
            jnp.dot(r, k[...], preferred_element_type=F32) for r, (_, k, _) in zip(sent, cores)
        ).astype(BF16)
        g_ref[:, width:] = sum(
            jnp.dot(r, h[...].astype(BF16), preferred_element_type=F32) for r, (_, _, h) in zip(sent, cores)
        ).astype(BF16)

    in_core_order(mine, other, work)


def third_kernel(mine_ref, other_ref, k_ref, k_other_ref, g_ref):
    rows = k_ref.shape[0]
    models = g_ref.shape[0]

    def core(ref, k):
        return ref[rows : rows + models, :rows], k, ref.at[:rows]

    back_projected(core(mine_ref, k_ref), core(other_ref, k_other_ref), g_ref)


def tree_sum(values):
    while len(values) > 1:
        values = [a + b for a, b in zip(values[::2], values[1::2])]
    return values[0]


def stepped(layers, base, wave_ref, cut_ref, g_refs, halo_ref=None):
    models, width = wave_ref.shape
    gradients = [stacked(g, layers) for g in g_refs]
    even, odd = (tree_sum([g[p] for g in gradients]) for p in range(2))
    edge = tree_sum([g[:, width:].astype(F32) for g in g_refs])
    cut_s, cut_d = (stacked_lane(cut_ref[:, p, :], range(layers)) for p in range(2))

    def at(tile, kind):
        return stacked_lane(tile, [base + KINDS * layer + kind for layer in range(layers)])

    even_next = at(edge, E_FIRST)
    detail_g = odd - 0.5 * (even + shifted_in(even, -1, even_next))
    before_g = at(edge, O_LAST) - 0.5 * (at(edge, E_LAST) + even[:, :1])
    smooth_g = even + 0.25 * (shifted_in(detail_g, 1, before_g) + detail_g)
    smooth, detail = stacked(wave_ref, layers)
    smooth = shrink(smooth + step_size * smooth_g, cut_s)
    detail = shrink(detail + step_size * detail_g, cut_d)
    if halo_ref is None:
        return smooth, detail
    halo = halo_ref[...]
    after_g = at(edge, O_FIRST) - 0.5 * (even_next + at(edge, E_SECOND))
    next_g = even_next + 0.25 * (detail_g[:, LANES - 1 :] + after_g)
    before = shrink(at(halo, O_LAST) + step_size * before_g, cut_d)
    next_smooth = shrink(at(halo, E_FIRST) + step_size * next_g, cut_s)
    after = shrink(at(halo, O_FIRST) + step_size * after_g, cut_d)
    return smooth, detail, before, next_smooth, after


def fourth_kernel(layers, base, wave_ref, cut_ref, halo_ref, k_ref, k_other_ref, *refs):
    *g_refs, new_ref, pred_ref = refs
    models = wave_ref.shape[0]
    rows = k_ref.shape[0]
    smooth, detail, before, next_smooth, after = stepped(layers, base, wave_ref, cut_ref, g_refs, halo_ref)
    new_ref[...] = unstacked(smooth, detail, models)

    def next_even_of(detail):
        return next_smooth - 0.25 * (detail[:, LANES - 1 :] + after)

    model = unstacked(*inverse_wave(smooth, detail, before, next_even_of), models).astype(BF16)
    pred_ref[...] = jnp.zeros_like(pred_ref)
    pred_ref[:, :rows] = nt_dot(model, k_ref[...])
    pred_ref[:, rows : 2 * rows] = nt_dot(model, k_other_ref[...])


def fifth_kernel(mine_ref, other_ref, k_ref, k_other_ref, *refs):
    *shares, g_ref, residual_ref = refs
    models, rows = residual_ref.shape
    predicted = tree_sum([s[...] for s in shares])

    def core(ref, k, start):
        residual = ref[rows + models :, :rows] - predicted[:, start : start + rows]
        return residual, k, ref.at[:rows]

    mine = core(mine_ref, k_ref, 0)
    residual_ref[...] = mine[0]
    back_projected(mine, core(other_ref, k_other_ref, rows), g_ref)


def sixth_kernel(layers, base, wave_ref, cut_ref, *refs):
    *g_refs, new_ref = refs
    new_ref[...] = unstacked(*stepped(layers, base, wave_ref, cut_ref, g_refs), wave_ref.shape[0])


def from_partner(x, axis, distance):
    return lax.ppermute(x, axis, [(i, i ^ distance) for i in range(lax.axis_size(axis))])


def shares_of(x, axis, lowest):
    size = lax.axis_size(axis) // lowest
    while size > 4:
        parts = [x] + [from_partner(x, axis, lowest * d) for d in range(1, 4)]
        x = tree_sum([p.astype(F32) for p in parts]).astype(x.dtype)
        lowest, size = lowest * 4, size // 4
    return [x] + [from_partner(x, axis, lowest * d) for d in range(1, size)]


def call(kernel, out_shape, *args, scratch=()):
    return pl.pallas_call(
        kernel,
        out_shape=out_shape,
        in_specs=[pl.BlockSpec(memory_space=pltpu.VMEM)] * len(args),
        out_specs=jax.tree.map(lambda _: pl.BlockSpec(memory_space=pltpu.VMEM), out_shape),
        scratch_shapes=list(scratch),
    )(*[pltpu.with_memory_space_constraint(arg, pltpu.VMEM) for arg in args])


def body(kernels, observed, initial, threshold):
    models, width = initial.shape
    rows = kernels.shape[0]
    layers = threshold.shape[1]
    n_vox = lax.axis_size("vox")
    assert width == 2 * layers * LANES and rows + KINDS * layers <= LANES and 2 * rows <= LANES
    cut = jnp.swapaxes(threshold, 1, 2)
    packet_rows = rows + 2 * models

    packet = call(
        functools.partial(first_kernel, layers),
        pltpu.VMEM((packet_rows, LANES), BF16),
        initial,
        kernels,
        scratch=[pltpu.VMEM((models, LANES), F32)],
    )
    packets = [packet] + [from_partner(packet, "vox", d) for d in range(1, n_vox)]
    k_other = from_partner(kernels, "dp", 1)
    mine, halo = call(
        functools.partial(second_kernel, layers, n_vox),
        (pltpu.VMEM((packet_rows, LANES), F32), pltpu.VMEM((models, LANES), F32)),
        observed,
        *packets,
        scratch=[pltpu.VMEM((n_vox, packet_rows, LANES), BF16)],
    )
    other = from_partner(mine, "dp", 1)
    g = call(third_kernel, pltpu.VMEM((models, width + LANES), BF16), mine, other, kernels, k_other)
    wavelets, predicted = call(
        functools.partial(fourth_kernel, layers, rows),
        (pltpu.VMEM((models, width), F32), pltpu.VMEM((models, LANES), F32)),
        initial,
        cut,
        halo,
        kernels,
        k_other,
        *shares_of(g, "dp", 2),
    )
    g, residual = call(
        fifth_kernel,
        (pltpu.VMEM((models, width + LANES), BF16), jax.ShapeDtypeStruct((models, rows), F32)),
        mine,
        other,
        kernels,
        k_other,
        *shares_of(predicted, "vox", 1),
    )
    coefficients = call(
        functools.partial(sixth_kernel, layers, rows),
        jax.ShapeDtypeStruct((models, width), F32),
        wavelets,
        cut,
        *shares_of(g, "dp", 2),
    )
    return coefficients, residual


def solution(mesh):
    return jax.shard_map(
        body,
        mesh=mesh,
        in_specs=(P("dp", "vox"), P(None, "dp"), P(None, "vox"), P()),
        out_specs=(P(None, "vox"), P(None, "dp")),
        check_vma=False,
    )
```

```python
import functools

import jax
import jax.numpy as jnp
from jax import lax
from jax.experimental import pallas as pl
from jax.experimental.pallas import tpu as pltpu
from jax.sharding import PartitionSpec as P

step_size = 0.5
LANES = 128
F32 = jnp.float32
BF16 = jnp.bfloat16

E_LAST, E_FIRST, E_SECOND, O_LAST, O_FIRST = range(5)
E_NEXT, D_BEFORE, S_NEXT, D_LAST, D_NEXT = range(5)
KINDS = 5


def lanes_of(shape):
    return lax.broadcasted_iota(jnp.int32, shape, len(shape) - 1)


def turned(x, by):
    return pltpu.roll(x, by % LANES, x.ndim - 1)


def shifted_in(x, by, edge):
    free = 0 if by == 1 else LANES - 1
    return jnp.where(lanes_of(x.shape) == free, edge, turned(x, by))


def edge_tile(pair_of, layers, base):
    tile = None
    for layer in range(layers):
        even, odd = pair_of(layer)
        start = base + KINDS * layer
        lane = lanes_of(even.shape)
        if tile is None:
            tile = jnp.zeros_like(even)
        tile = jnp.where((lane >= start) & (lane < start + 3), turned(even, start + 1), tile)
        tile = jnp.where((lane >= start + 3) & (lane < start + 5), turned(odd, start + 4), tile)
    return tile


def kind_lane(lane, base, kind):
    return lax.rem(lane - base + KINDS * LANES, KINDS) == kind


def shrink(values, cutoff):
    return values - jnp.clip(values, -cutoff, cutoff)


def layer_tiles(ref, layer):
    start = layer * 2 * LANES
    return ref[:, start : start + LANES], ref[:, start + LANES : start + 2 * LANES]


def stacked(ref, layers):
    tiles = [layer_tiles(ref, layer) for layer in range(layers)]
    return tuple(jnp.concatenate([t[p] for t in tiles], axis=0).astype(F32) for p in range(2))


def unstacked(even, odd, models):
    rows = [slice(start, start + models) for start in range(0, even.shape[0], models)]
    return jnp.concatenate([t[r] for r in rows for t in (even, odd)], axis=1)


def nt_dot(a, b):
    return lax.dot_general(a, b, (((1,), (1,)), ((), ())), preferred_element_type=F32)


def inverse_wave(smooth, detail, edge):
    even = smooth - 0.25 * (shifted_in(detail, 1, edge) + detail)
    odd = detail + 0.5 * (even + shifted_in(even, -1, edge))
    return even, odd


def forward_wave(even, odd):
    detail = odd - 0.5 * (even + shifted_in(even, -1, 0.0))
    smooth = even + 0.25 * (shifted_in(detail, 1, 0.0) + detail)
    return smooth, detail


def by_kind(lane, base, *values):
    kind = lax.rem(lane - base + KINDS * LANES, KINDS)
    result = values[0]
    for k, value in enumerate(values[1:], 1):
        result = jnp.where(kind == k, value, result)
    return result


def first_kernel(layers, wave_hbm, k_hbm, packet_ref, wave_ref, k_ref, tile, arrived):
    loads = [
        pltpu.make_async_copy(wave_hbm, wave_ref, arrived.at[0]),
        pltpu.make_async_copy(k_hbm, k_ref, arrived.at[1]),
    ]
    for load in loads:
        load.start()
    rows = k_ref.shape[0]
    models = wave_ref.shape[0]
    loads[0].wait()
    even, odd = inverse_wave(*stacked(wave_ref, layers), 0.0)
    model = unstacked(even, odd, models).astype(BF16)
    tile[...] = edge_tile(lambda l: layer_tiles(wave_ref, l), layers, rows)
    loads[1].wait()
    edges = edge_tile(lambda l: tuple(t.astype(F32) for t in layer_tiles(k_ref, l)), layers, rows)
    packet_ref[:rows, :] = edges.astype(BF16)
    tile[:, :rows] = nt_dot(model, k_ref[...])
    whole = tile[...]
    high = whole.astype(BF16).astype(F32)
    packet_ref[rows:, :] = jnp.concatenate([high, whole - high], axis=0).astype(BF16)


def preparing_kernel(layers, base, k_ref, k_other_ref, threshold_ref, kw_ref, kw_other_ref, cut_ref, cut_halo_ref):
    rows = k_ref.shape[0]
    models, width = cut_ref.shape
    for source, target in ((k_ref, kw_ref), (k_other_ref, kw_other_ref)):
        target[...] = unstacked(*forward_wave(*stacked(source, layers)), rows).astype(BF16)
    lane = lanes_of((models, LANES))
    halo = jnp.zeros((models, LANES), F32)
    for layer in range(layers):
        smooth, detail = (
            jnp.broadcast_to(threshold_ref[:, p, layer : layer + 1], (models, LANES)) for p in range(2)
        )
        start = 2 * LANES * layer
        cut_ref[:, start : start + LANES] = smooth
        cut_ref[:, start + LANES : start + 2 * LANES] = detail
        start = base + KINDS * layer
        here = (lane >= start) & (lane < start + KINDS)
        halo = jnp.where(here, jnp.where(lane == start + S_NEXT, smooth, detail), halo)
    cut_halo_ref[...] = halo


def second_kernel(layers, n_vox, *refs):
    (observed_ref, *packets, out_ref, halo_ref, held) = refs
    models, rows = observed_ref.shape
    me = lax.axis_index("vox")
    for distance, packet in enumerate(packets):
        held[me ^ distance] = packet[...]
    left, right = lax.rem(me + n_vox - 1, n_vox), lax.rem(me + 1, n_vox)
    lane = lanes_of((models, LANES))
    inside = (lane >= rows) & (lane < rows + KINDS * layers)

    def edge_values(which):
        both = held[which, rows:, :].astype(F32)
        return both[:models] + both[models:]

    edge = [edge_values(z) for z in range(n_vox)]
    terms, columns = [], []
    for z in range(n_vox):
        before, after = edge[z - 1], edge[(z + 1) % n_vox]
        next_smooth = turned(after, O_LAST - E_FIRST)
        next_detail = turned(after, O_LAST - O_FIRST)
        next_even = next_smooth - 0.25 * (edge[z] + next_detail)
        term = by_kind(
            lane,
            rows,
            0.0,
            -0.25 * turned(before, E_FIRST - O_LAST),
            0.0,
            0.5 * next_even,
            -0.125 * turned(before, O_FIRST - O_LAST),
        )
        terms.append(jnp.where(inside, term, 0.0).astype(BF16))
        columns.append(held[z, :rows, :])
    predicted = nt_dot(jnp.concatenate(terms, axis=1), jnp.concatenate(columns, axis=1))
    shares = edge[0]
    for z in range(1, n_vox):
        shares = shares + edge[z]
    predicted = predicted + shares[:, :rows]

    before, own, after = (held[z, :rows, :].astype(F32) for z in (left, me, right))
    details = by_kind(
        lanes_of(own.shape),
        rows,
        0.0,
        0.0,
        0.0,
        own - 0.5 * (turned(own, O_LAST - E_LAST) + turned(after, O_LAST - E_FIRST)),
        after - 0.5 * (turned(after, O_FIRST - E_FIRST) + turned(after, O_FIRST - E_SECOND)),
    )
    out_ref[:rows, :] = by_kind(
        lanes_of(own.shape),
        rows,
        turned(after, E_NEXT - E_FIRST),
        turned(before, D_BEFORE - O_LAST) - 0.5 * (turned(before, D_BEFORE - E_LAST) + own),
        turned(after, S_NEXT - E_FIRST) + 0.25 * (turned(details, S_NEXT - D_LAST) + turned(details, S_NEXT - D_NEXT)),
        details,
        details,
    )
    out_ref[rows:, :] = jnp.zeros((2 * models, LANES), F32)
    out_ref[rows : rows + models, :rows] = observed_ref[...] - predicted
    out_ref[rows + models :, :rows] = observed_ref[...]
    before, own, after = (edge_values(z) for z in (left, me, right))
    halo_ref[...] = by_kind(
        lane, rows, 0.0, turned(before, D_BEFORE - O_LAST), turned(after, S_NEXT - E_FIRST), own, after
    )


def in_core_order(mine, other, work):
    core = lax.rem(lax.axis_index("dp"), 2)

    @pl.when(core == 0)
    def _():
        work(mine, other)

    @pl.when(core == 1)
    def _():
        work(other, mine)


def back_projected(mine, other, g_ref):
    width = mine[1].shape[1]

    def work(*cores):
        sent = [residual.astype(BF16) for residual, _, _ in cores]
        g_ref[:, :width] = sum(
            jnp.dot(r, k[...], preferred_element_type=F32) for r, (_, k, _) in zip(sent, cores)
        ).astype(BF16)
        g_ref[:, width:] = sum(
            jnp.dot(r, h[...].astype(BF16), preferred_element_type=F32) for r, (_, _, h) in zip(sent, cores)
        ).astype(BF16)

    in_core_order(mine, other, work)


def third_kernel(mine_ref, other_ref, kw_ref, kw_other_ref, g_ref):
    rows = kw_ref.shape[0]
    models = g_ref.shape[0]

    def core(ref, k):
        return ref[rows : rows + models, :rows], k, ref.at[:rows]

    back_projected(core(mine_ref, kw_ref), core(other_ref, kw_other_ref), g_ref)


def tree_sum(values):
    while len(values) > 1:
        values = [a + b for a, b in zip(values[::2], values[1::2])]
    return values[0]


def at_ends(tile, layers, base):
    return jnp.concatenate([turned(tile, -(base + KINDS * layer + 1)) for layer in range(layers)], axis=0)


def stepped(layers, base, wave_ref, cut_ref, g_refs):
    width = wave_ref.shape[1]
    gradients = [stacked(g, layers) for g in g_refs]
    smooth_g, detail_g = (tree_sum([g[p] for g in gradients]) for p in range(2))
    edge = tree_sum([g[:, width:].astype(F32) for g in g_refs])
    ends = at_ends(edge, layers, base)
    lane = lanes_of(ends.shape)
    smooth_g += jnp.where(lane == 0, 0.25 * ends, jnp.where(lane == LANES - 1, -0.125 * ends, 0.0))
    detail_g += jnp.where(lane == LANES - 1, -0.5 * ends, 0.0)
    smooth, detail = (
        shrink(w + step_size * g, cut)
        for w, g, cut in zip(stacked(wave_ref, layers), (smooth_g, detail_g), stacked(cut_ref, layers))
    )
    return smooth, detail, edge


def fourth_kernel(layers, base, wave_ref, cut_ref, halo_ref, cut_halo_ref, k_ref, k_other_ref, *refs):
    *g_refs, new_ref, pred_ref = refs
    models = wave_ref.shape[0]
    rows = k_ref.shape[0]
    smooth, detail, edge = stepped(layers, base, wave_ref, cut_ref, g_refs)
    new_ref[...] = unstacked(smooth, detail, models)
    halo = shrink(halo_ref[...] + step_size * edge, cut_halo_ref[...])
    next_even = turned(halo, E_NEXT - S_NEXT) - 0.25 * (turned(halo, E_NEXT - D_LAST) + turned(halo, E_NEXT - D_NEXT))
    ends = at_ends(by_kind(lanes_of(halo.shape), base, next_even, halo), layers, base)
    model = unstacked(*inverse_wave(smooth, detail, ends), models).astype(BF16)
    pred_ref[...] = jnp.zeros_like(pred_ref)
    pred_ref[:, :rows] = nt_dot(model, k_ref[...])
    pred_ref[:, rows : 2 * rows] = nt_dot(model, k_other_ref[...])


def fifth_kernel(mine_ref, other_ref, kw_ref, kw_other_ref, *refs):
    *shares, g_ref, residual_ref = refs
    models, rows = residual_ref.shape
    predicted = tree_sum([s[...] for s in shares])

    def core(ref, k, start):
        residual = ref[rows + models :, :rows] - predicted[:, start : start + rows]
        return residual, k, ref.at[:rows]

    mine = core(mine_ref, kw_ref, 0)
    residual_ref[...] = mine[0]
    back_projected(mine, core(other_ref, kw_other_ref, rows), g_ref)


def sixth_kernel(layers, base, wave_ref, cut_ref, *refs):
    *g_refs, new_ref = refs
    smooth, detail, _ = stepped(layers, base, wave_ref, cut_ref, g_refs)
    new_ref[...] = unstacked(smooth, detail, wave_ref.shape[0])


def from_partner(x, axis, distance):
    return lax.ppermute(x, axis, [(i, i ^ distance) for i in range(lax.axis_size(axis))])


def shares_of(x, axis, lowest):
    size = lax.axis_size(axis) // lowest
    while size > 4:
        parts = [x] + [from_partner(x, axis, lowest * d) for d in range(1, 4)]
        x = tree_sum([p.astype(F32) for p in parts]).astype(x.dtype)
        lowest, size = lowest * 4, size // 4
    return [x] + [from_partner(x, axis, lowest * d) for d in range(1, size)]


def call(kernel, out_shape, *args, scratch=(), space=pltpu.VMEM):
    return pl.pallas_call(
        kernel,
        out_shape=out_shape,
        in_specs=[pl.BlockSpec(memory_space=space)] * len(args),
        out_specs=jax.tree.map(lambda _: pl.BlockSpec(memory_space=pltpu.VMEM), out_shape),
        scratch_shapes=list(scratch),
    )(*[pltpu.with_memory_space_constraint(arg, space) for arg in args])


def body(kernels, observed, initial, threshold):
    models, width = initial.shape
    rows = kernels.shape[0]
    layers = threshold.shape[1]
    n_vox = lax.axis_size("vox")
    assert width == 2 * layers * LANES and rows + KINDS * layers <= LANES and 2 * rows <= LANES
    packet_rows = rows + 2 * models
    g_shape = pltpu.VMEM((models, width + LANES), BF16)

    packet, wavelets, k_mine = call(
        functools.partial(first_kernel, layers),
        (pltpu.VMEM((packet_rows, LANES), BF16), pltpu.VMEM((models, width), F32), pltpu.VMEM((rows, width), BF16)),
        initial,
        kernels,
        scratch=[pltpu.VMEM((models, LANES), F32), pltpu.SemaphoreType.DMA((2,))],
        space=pltpu.HBM,
    )
    packets = [packet] + [from_partner(packet, "vox", d) for d in range(1, n_vox)]
    k_other = from_partner(k_mine, "dp", 1)
    kw, kw_other, cut, cut_halo = call(
        functools.partial(preparing_kernel, layers, rows),
        (
            pltpu.VMEM((rows, width), BF16),
            pltpu.VMEM((rows, width), BF16),
            pltpu.VMEM((models, width), F32),
            pltpu.VMEM((models, LANES), F32),
        ),
        k_mine,
        k_other,
        jnp.swapaxes(threshold, 1, 2),
    )
    mine, halo = call(
        functools.partial(second_kernel, layers, n_vox),
        (pltpu.VMEM((packet_rows, LANES), F32), pltpu.VMEM((models, LANES), F32)),
        observed,
        *packets,
        scratch=[pltpu.VMEM((n_vox, packet_rows, LANES), BF16)],
    )
    other = from_partner(mine, "dp", 1)
    g = call(third_kernel, g_shape, mine, other, kw, kw_other)
    wavelets, predicted = call(
        functools.partial(fourth_kernel, layers, rows),
        (pltpu.VMEM((models, width), F32), pltpu.VMEM((models, LANES), F32)),
        wavelets,
        cut,
        halo,
        cut_halo,
        k_mine,
        k_other,
        *shares_of(g, "dp", 2),
    )
    g, residual = call(
        fifth_kernel,
        (g_shape, pltpu.VMEM((models, rows), F32)),
        mine,
        other,
        kw,
        kw_other,
        *shares_of(predicted, "vox", 1),
    )
    coefficients = call(
        functools.partial(sixth_kernel, layers, rows),
        jax.ShapeDtypeStruct((models, width), F32),
        wavelets,
        cut,
        *shares_of(g, "dp", 2),
    )
    return coefficients, residual


def solution(mesh):
    return jax.shard_map(
        body,
        mesh=mesh,
        in_specs=(P("dp", "vox"), P(None, "dp"), P(None, "vox"), P()),
        out_specs=(P(None, "vox"), P(None, "dp")),
        check_vma=False,
    )
```

```python
import functools

import jax
import jax.numpy as jnp
from jax import lax
from jax.experimental import pallas as pl
from jax.experimental.pallas import tpu as pltpu
from jax.sharding import PartitionSpec as P

step_size = 0.5
LANES = 128
F32 = jnp.float32
BF16 = jnp.bfloat16

E_LAST, E_FIRST, E_SECOND, O_LAST, O_FIRST = range(5)
E_NEXT, D_BEFORE, S_NEXT, D_LAST, D_NEXT = range(5)
KINDS = 5


def lanes_of(shape):
    return lax.broadcasted_iota(jnp.int32, shape, len(shape) - 1)


def turned(x, by):
    return pltpu.roll(x, by % LANES, x.ndim - 1)


def shifted_in(x, by, edge):
    free = 0 if by == 1 else LANES - 1
    return jnp.where(lanes_of(x.shape) == free, edge, turned(x, by))


def edge_tile(pair_of, layers, base):
    tile = None
    for layer in range(layers):
        even, odd = pair_of(layer)
        start = base + KINDS * layer
        lane = lanes_of(even.shape)
        if tile is None:
            tile = jnp.zeros_like(even)
        tile = jnp.where((lane >= start) & (lane < start + 3), turned(even, start + 1), tile)
        tile = jnp.where((lane >= start + 3) & (lane < start + 5), turned(odd, start + 4), tile)
    return tile


def kind_lane(lane, base, kind):
    return lax.rem(lane - base + KINDS * LANES, KINDS) == kind


def shrink(values, cutoff):
    return values - jnp.clip(values, -cutoff, cutoff)


def layer_tiles(ref, layer):
    start = layer * 2 * LANES
    return ref[:, start : start + LANES], ref[:, start + LANES : start + 2 * LANES]


def stacked(ref, layers):
    tiles = [layer_tiles(ref, layer) for layer in range(layers)]
    return tuple(jnp.concatenate([t[p] for t in tiles], axis=0).astype(F32) for p in range(2))


def unstacked(even, odd, models):
    rows = [slice(start, start + models) for start in range(0, even.shape[0], models)]
    return jnp.concatenate([t[r] for r in rows for t in (even, odd)], axis=1)


def nt_dot(a, b):
    return lax.dot_general(a, b, (((1,), (1,)), ((), ())), preferred_element_type=F32)


def inverse_wave(smooth, detail, edge):
    even = smooth - 0.25 * (shifted_in(detail, 1, edge) + detail)
    odd = detail + 0.5 * (even + shifted_in(even, -1, edge))
    return even, odd


def forward_wave(even, odd):
    detail = odd - 0.5 * (even + shifted_in(even, -1, 0.0))
    smooth = even + 0.25 * (shifted_in(detail, 1, 0.0) + detail)
    return smooth, detail


def by_kind(lane, base, *values):
    kind = lax.rem(lane - base + KINDS * LANES, KINDS)
    result = values[0]
    for k, value in enumerate(values[1:], 1):
        result = jnp.where(kind == k, value, result)
    return result


def first_kernel(layers, wave_hbm, k_hbm, packet_ref, wave_ref, k_ref, tile, arrived):
    loads = [
        pltpu.make_async_copy(wave_hbm, wave_ref, arrived.at[0]),
        pltpu.make_async_copy(k_hbm, k_ref, arrived.at[1]),
    ]
    for load in loads:
        load.start()
    rows = k_ref.shape[0]
    models = wave_ref.shape[0]
    loads[0].wait()
    even, odd = inverse_wave(*stacked(wave_ref, layers), 0.0)
    model = unstacked(even, odd, models).astype(BF16)
    tile[...] = edge_tile(lambda l: layer_tiles(wave_ref, l), layers, rows)
    loads[1].wait()
    edges = edge_tile(lambda l: tuple(t.astype(F32) for t in layer_tiles(k_ref, l)), layers, rows)
    packet_ref[:rows, :] = edges.astype(BF16)
    tile[:, :rows] = nt_dot(model, k_ref[...])
    whole = tile[...]
    high = whole.astype(BF16).astype(F32)
    packet_ref[rows:, :] = jnp.concatenate([high, whole - high], axis=0).astype(BF16)


def preparing_kernel(layers, base, k_ref, k_other_ref, threshold_ref, kw_ref, kw_other_ref, cut_ref, cut_halo_ref):
    rows = k_ref.shape[0]
    models, width = cut_ref.shape
    for source, target in ((k_ref, kw_ref), (k_other_ref, kw_other_ref)):
        target[...] = unstacked(*forward_wave(*stacked(source, layers)), rows).astype(BF16)
    lane = lanes_of((models, LANES))
    halo = jnp.zeros((models, LANES), F32)
    for layer in range(layers):
        smooth, detail = (
            jnp.broadcast_to(threshold_ref[:, p, layer : layer + 1], (models, LANES)) for p in range(2)
        )
        start = 2 * LANES * layer
        cut_ref[:, start : start + LANES] = smooth
        cut_ref[:, start + LANES : start + 2 * LANES] = detail
        start = base + KINDS * layer
        here = (lane >= start) & (lane < start + KINDS)
        halo = jnp.where(here, jnp.where(lane == start + S_NEXT, smooth, detail), halo)
    cut_halo_ref[...] = halo


def second_kernel(layers, n_vox, *refs):
    (observed_ref, *packets, out_ref, halo_ref, held) = refs
    models, rows = observed_ref.shape
    me = lax.axis_index("vox")
    for distance, packet in enumerate(packets):
        held[me ^ distance] = packet[...]
    left, right = lax.rem(me + n_vox - 1, n_vox), lax.rem(me + 1, n_vox)
    lane = lanes_of((models, LANES))
    inside = (lane >= rows) & (lane < rows + KINDS * layers)

    def edge_values(which):
        both = held[which, rows:, :].astype(F32)
        return both[:models] + both[models:]

    edge = [edge_values(z) for z in range(n_vox)]
    terms, columns = [], []
    for z in range(n_vox):
        before, after = edge[z - 1], edge[(z + 1) % n_vox]
        next_smooth = turned(after, O_LAST - E_FIRST)
        next_detail = turned(after, O_LAST - O_FIRST)
        next_even = next_smooth - 0.25 * (edge[z] + next_detail)
        term = by_kind(
            lane,
            rows,
            0.0,
            -0.25 * turned(before, E_FIRST - O_LAST),
            0.0,
            0.5 * next_even,
            -0.125 * turned(before, O_FIRST - O_LAST),
        )
        terms.append(jnp.where(inside, term, 0.0).astype(BF16))
        columns.append(held[z, :rows, :])
    predicted = nt_dot(jnp.concatenate(terms, axis=1), jnp.concatenate(columns, axis=1))
    shares = edge[0]
    for z in range(1, n_vox):
        shares = shares + edge[z]
    predicted = predicted + shares[:, :rows]

    before, own, after = (held[z, :rows, :].astype(F32) for z in (left, me, right))
    details = by_kind(
        lanes_of(own.shape),
        rows,
        0.0,
        0.0,
        0.0,
        own - 0.5 * (turned(own, O_LAST - E_LAST) + turned(after, O_LAST - E_FIRST)),
        after - 0.5 * (turned(after, O_FIRST - E_FIRST) + turned(after, O_FIRST - E_SECOND)),
    )
    out_ref[:rows, :] = by_kind(
        lanes_of(own.shape),
        rows,
        turned(after, E_NEXT - E_FIRST),
        turned(before, D_BEFORE - O_LAST) - 0.5 * (turned(before, D_BEFORE - E_LAST) + own),
        turned(after, S_NEXT - E_FIRST) + 0.25 * (turned(details, S_NEXT - D_LAST) + turned(details, S_NEXT - D_NEXT)),
        details,
        details,
    )
    out_ref[rows:, :] = jnp.zeros((2 * models, LANES), F32)
    out_ref[rows : rows + models, :rows] = observed_ref[...] - predicted
    out_ref[rows + models :, :rows] = observed_ref[...]
    before, own, after = (edge_values(z) for z in (left, me, right))
    halo_ref[...] = by_kind(
        lane, rows, 0.0, turned(before, D_BEFORE - O_LAST), turned(after, S_NEXT - E_FIRST), own, after
    )


def in_core_order(mine, other, work):
    core = lax.rem(lax.axis_index("dp"), 2)

    @pl.when(core == 0)
    def _():
        work(mine, other)

    @pl.when(core == 1)
    def _():
        work(other, mine)


def back_projected(mine, other, g_ref):
    width = mine[1].shape[1]

    def work(*cores):
        sent = [residual.astype(BF16) for residual, _, _ in cores]
        g_ref[:, :width] = sum(
            jnp.dot(r, k[...], preferred_element_type=F32) for r, (_, k, _) in zip(sent, cores)
        ).astype(BF16)
        g_ref[:, width:] = sum(
            jnp.dot(r, h[...].astype(BF16), preferred_element_type=F32) for r, (_, _, h) in zip(sent, cores)
        ).astype(BF16)

    in_core_order(mine, other, work)


def third_kernel(mine_ref, other_ref, kw_ref, kw_other_ref, g_ref):
    rows = kw_ref.shape[0]
    models = g_ref.shape[0]

    def core(ref, k):
        return ref[rows : rows + models, :rows], k, ref.at[:rows]

    back_projected(core(mine_ref, kw_ref), core(other_ref, kw_other_ref), g_ref)


def tree_sum(values):
    while len(values) > 1:
        values = [a + b for a, b in zip(values[::2], values[1::2])]
    return values[0]


def at_ends(tile, layers, base):
    return jnp.concatenate([turned(tile, -(base + KINDS * layer + 1)) for layer in range(layers)], axis=0)


def stepped(layers, base, wave_ref, cut_ref, g_refs):
    width = wave_ref.shape[1]
    gradients = [stacked(g, layers) for g in g_refs]
    smooth_g, detail_g = (tree_sum([g[p] for g in gradients]) for p in range(2))
    edge = tree_sum([g[:, width:].astype(F32) for g in g_refs])
    ends = at_ends(edge, layers, base)
    lane = lanes_of(ends.shape)
    smooth_g += jnp.where(lane == 0, 0.25 * ends, jnp.where(lane == LANES - 1, -0.125 * ends, 0.0))
    detail_g += jnp.where(lane == LANES - 1, -0.5 * ends, 0.0)
    smooth, detail = (
        shrink(w + step_size * g, cut)
        for w, g, cut in zip(stacked(wave_ref, layers), (smooth_g, detail_g), stacked(cut_ref, layers))
    )
    return smooth, detail, edge


def fourth_kernel(layers, base, wave_ref, cut_ref, halo_ref, cut_halo_ref, k_ref, k_other_ref, *refs):
    *g_refs, new_ref, pred_ref = refs
    models = wave_ref.shape[0]
    rows = k_ref.shape[0]
    smooth, detail, edge = stepped(layers, base, wave_ref, cut_ref, g_refs)
    new_ref[...] = unstacked(smooth, detail, models)
    halo = shrink(halo_ref[...] + step_size * edge, cut_halo_ref[...])
    next_even = turned(halo, E_NEXT - S_NEXT) - 0.25 * (turned(halo, E_NEXT - D_LAST) + turned(halo, E_NEXT - D_NEXT))
    ends = at_ends(by_kind(lanes_of(halo.shape), base, next_even, halo), layers, base)
    model = unstacked(*inverse_wave(smooth, detail, ends), models).astype(BF16)
    pred_ref[...] = jnp.zeros_like(pred_ref)

    def work(first, second):
        pred_ref[:, :rows] = nt_dot(model, first[...])
        pred_ref[:, rows : 2 * rows] = nt_dot(model, second[...])

    in_core_order(k_ref, k_other_ref, work)


def fifth_kernel(mine_ref, other_ref, kw_ref, kw_other_ref, *refs):
    *shares, g_ref, residual_ref = refs
    models, rows = residual_ref.shape
    predicted = tree_sum([s[...] for s in shares])
    first, second = predicted[:, :rows], predicted[:, rows : 2 * rows]
    is_first = lax.rem(lax.axis_index("dp"), 2) == 0

    def core(ref, k, predicted):
        return ref[rows + models :, :rows] - predicted, k, ref.at[:rows]

    mine = core(mine_ref, kw_ref, jnp.where(is_first, first, second))
    residual_ref[...] = mine[0]
    back_projected(mine, core(other_ref, kw_other_ref, jnp.where(is_first, second, first)), g_ref)


def sixth_kernel(layers, base, wave_ref, cut_ref, *refs):
    *g_refs, new_ref = refs
    smooth, detail, _ = stepped(layers, base, wave_ref, cut_ref, g_refs)
    new_ref[...] = unstacked(smooth, detail, wave_ref.shape[0])


def from_partner(x, axis, distance):
    return lax.ppermute(x, axis, [(i, i ^ distance) for i in range(lax.axis_size(axis))])


def from_other_core(x, chips, vox):
    n_vox = lax.axis_size("vox")
    places = [(d, z) for d in range(lax.axis_size("dp")) for z in range(n_vox)]
    route = [(d * n_vox + z, (d ^ (2 * chips + 1)) * n_vox + (z ^ vox)) for d, z in places]
    return lax.ppermute(x, ("dp", "vox"), route)


def shares_of(x, size, fetch):
    lowest = 1
    while size > 4:
        parts = [x] + [fetch(x, lowest * d) for d in range(1, 4)]
        x = tree_sum([p.astype(F32) for p in parts]).astype(x.dtype)
        lowest, size = lowest * 4, size // 4
    return [x] + [fetch(x, lowest * d) for d in range(1, size)]


def over_chips(x):
    return shares_of(x, lax.axis_size("dp") // 2, lambda x, d: from_other_core(x, d, 0))


def over_vox(x):
    return shares_of(x, lax.axis_size("vox"), lambda x, d: from_other_core(x, 0, d))


def call(kernel, out_shape, *args, scratch=(), space=pltpu.VMEM):
    return pl.pallas_call(
        kernel,
        out_shape=out_shape,
        in_specs=[pl.BlockSpec(memory_space=space)] * len(args),
        out_specs=jax.tree.map(lambda _: pl.BlockSpec(memory_space=pltpu.VMEM), out_shape),
        scratch_shapes=list(scratch),
    )(*[pltpu.with_memory_space_constraint(arg, space) for arg in args])


def body(kernels, observed, initial, threshold):
    models, width = initial.shape
    rows = kernels.shape[0]
    layers = threshold.shape[1]
    n_vox = lax.axis_size("vox")
    assert width == 2 * layers * LANES and rows + KINDS * layers <= LANES and 2 * rows <= LANES
    packet_rows = rows + 2 * models
    g_shape = pltpu.VMEM((models, width + LANES), BF16)
    k_shape = pltpu.VMEM((rows, width), BF16)

    packet, wavelets, k_mine = call(
        functools.partial(first_kernel, layers),
        (pltpu.VMEM((packet_rows, LANES), BF16), pltpu.VMEM((models, width), F32), k_shape),
        initial,
        kernels,
        scratch=[pltpu.VMEM((models, LANES), F32), pltpu.SemaphoreType.DMA((2,))],
        space=pltpu.HBM,
    )
    packets = [packet] + [from_partner(packet, "vox", d) for d in range(1, n_vox)]
    k_other = from_partner(k_mine, "dp", 1)
    kw, kw_other, cut, cut_halo = call(
        functools.partial(preparing_kernel, layers, rows),
        (
            k_shape,
            k_shape,
            pltpu.VMEM((models, width), F32),
            pltpu.VMEM((models, LANES), F32),
        ),
        k_mine,
        k_other,
        jnp.swapaxes(threshold, 1, 2),
    )
    mine, halo = call(
        functools.partial(second_kernel, layers, n_vox),
        (pltpu.VMEM((packet_rows, LANES), F32), pltpu.VMEM((models, LANES), F32)),
        observed,
        *packets,
        scratch=[pltpu.VMEM((n_vox, packet_rows, LANES), BF16)],
    )
    other = from_partner(mine, "dp", 1)
    g = call(third_kernel, g_shape, mine, other, kw, kw_other)
    wavelets, predicted = call(
        functools.partial(fourth_kernel, layers, rows),
        (pltpu.VMEM((models, width), F32), pltpu.VMEM((models, LANES), F32)),
        wavelets,
        cut,
        halo,
        cut_halo,
        k_mine,
        k_other,
        *over_chips(g),
    )
    g, residual = call(
        fifth_kernel,
        (g_shape, pltpu.VMEM((models, rows), F32)),
        mine,
        other,
        kw,
        kw_other,
        *over_vox(predicted),
    )
    coefficients = call(
        functools.partial(sixth_kernel, layers, rows),
        jax.ShapeDtypeStruct((models, width), F32),
        wavelets,
        cut,
        *over_chips(g),
    )
    return coefficients, residual


def solution(mesh):
    return jax.shard_map(
        body,
        mesh=mesh,
        in_specs=(P("dp", "vox"), P(None, "dp"), P(None, "vox"), P()),
        out_specs=(P(None, "vox"), P(None, "dp")),
        check_vma=False,
    )
```

```python
import functools

import jax
import jax.numpy as jnp
from jax import lax
from jax.experimental import pallas as pl
from jax.experimental.pallas import tpu as pltpu
from jax.sharding import PartitionSpec as P

step_size = 0.5
LANES = 128
F32 = jnp.float32
BF16 = jnp.bfloat16

E_LAST, E_FIRST, E_SECOND, O_LAST, O_FIRST = range(5)
E_NEXT, D_BEFORE, S_NEXT, D_LAST, D_NEXT = range(5)
KINDS = 5


def lanes_of(shape):
    return lax.broadcasted_iota(jnp.int32, shape, len(shape) - 1)


def turned(x, by):
    return pltpu.roll(x, by % LANES, x.ndim - 1)


def shifted_in(x, by, edge):
    free = 0 if by == 1 else LANES - 1
    return jnp.where(lanes_of(x.shape) == free, edge, turned(x, by))


def edge_tile(pair_of, layers, base):
    tile = None
    for layer in range(layers):
        even, odd = pair_of(layer)
        start = base + KINDS * layer
        lane = lanes_of(even.shape)
        if tile is None:
            tile = jnp.zeros_like(even)
        tile = jnp.where((lane >= start) & (lane < start + 3), turned(even, start + 1), tile)
        tile = jnp.where((lane >= start + 3) & (lane < start + 5), turned(odd, start + 4), tile)
    return tile


def kind_lane(lane, base, kind):
    return lax.rem(lane - base + KINDS * LANES, KINDS) == kind


def shrink(values, cutoff):
    return values - jnp.clip(values, -cutoff, cutoff)


def layer_tiles(ref, layer):
    start = layer * 2 * LANES
    return ref[:, start : start + LANES], ref[:, start + LANES : start + 2 * LANES]


def stacked(ref, layers):
    tiles = [layer_tiles(ref, layer) for layer in range(layers)]
    return tuple(jnp.concatenate([t[p] for t in tiles], axis=0).astype(F32) for p in range(2))


def unstacked(even, odd, models):
    rows = [slice(start, start + models) for start in range(0, even.shape[0], models)]
    return jnp.concatenate([t[r] for r in rows for t in (even, odd)], axis=1)


def nt_dot(a, b):
    return lax.dot_general(a, b, (((1,), (1,)), ((), ())), preferred_element_type=F32)


def inverse_wave(smooth, detail, edge):
    even = smooth - 0.25 * (shifted_in(detail, 1, edge) + detail)
    odd = detail + 0.5 * (even + shifted_in(even, -1, edge))
    return even, odd


def forward_wave(even, odd):
    detail = odd - 0.5 * (even + shifted_in(even, -1, 0.0))
    smooth = even + 0.25 * (shifted_in(detail, 1, 0.0) + detail)
    return smooth, detail


def by_kind(lane, base, *values):
    kind = lax.rem(lane - base + KINDS * LANES, KINDS)
    result = values[0]
    for k, value in enumerate(values[1:], 1):
        result = jnp.where(kind == k, value, result)
    return result


def pieces(x, count):
    result = []
    for _ in range(count):
        result.append(x.astype(BF16).astype(F32))
        x = x - result[-1]
    return result


def first_kernel(layers, wave_hbm, k_hbm, observed_hbm, packet_ref, wave_ref, block_ref, observed_ref, tile, arrived):
    rows = k_hbm.shape[0]
    models = wave_ref.shape[0]
    loads = [
        pltpu.make_async_copy(source, target, arrived.at[i])
        for i, (source, target) in enumerate(
            ((wave_hbm, wave_ref), (k_hbm, block_ref.at[:rows]), (observed_hbm, observed_ref))
        )
    ]
    for load in loads:
        load.start()
    loads[0].wait()
    even, odd = inverse_wave(*stacked(wave_ref, layers), 0.0)
    model = unstacked(even, odd, models).astype(BF16)
    tile[...] = edge_tile(lambda l: layer_tiles(wave_ref, l), layers, rows)
    loads[1].wait()
    loads[2].wait()
    edges = edge_tile(lambda l: tuple(t[:rows].astype(F32) for t in layer_tiles(block_ref, l)), layers, rows)
    packet_ref[:rows, :] = edges.astype(BF16)
    tile[:, :rows] = nt_dot(model, block_ref[:rows, :])
    packet_ref[rows:, :] = jnp.concatenate(pieces(tile[...], 2), axis=0).astype(BF16)
    tile[...] = jnp.zeros_like(tile)
    tile[:, :rows] = observed_ref[...]
    below = pieces(tile[...], 3) + [jnp.zeros_like(tile)]
    below = [jnp.concatenate(below[i : i + 2], axis=0).astype(BF16) for i in (0, 2)]
    packed = [packet_ref[i : i + 2 * models, :] for i in range(0, packet_ref.shape[0], 2 * models)] + below
    for i, part in enumerate(packed):
        block_ref[rows:, i * LANES : (i + 1) * LANES] = part


def applied_kernel(layers, block_ref, kw_ref):
    rows = kw_ref.shape[0]
    kw_ref[...] = unstacked(*forward_wave(*stacked(block_ref.at[:rows], layers)), rows).astype(BF16)


def spread_kernel(layers, base, threshold_ref, cut_ref, cut_halo_ref):
    models = cut_ref.shape[0]
    lane = lanes_of((models, LANES))
    halo = jnp.zeros((models, LANES), F32)
    for layer in range(layers):
        smooth, detail = (
            jnp.broadcast_to(threshold_ref[:, p, layer : layer + 1], (models, LANES)) for p in range(2)
        )
        start = 2 * LANES * layer
        cut_ref[:, start : start + LANES] = smooth
        cut_ref[:, start + LANES : start + 2 * LANES] = detail
        start = base + KINDS * layer
        here = (lane >= start) & (lane < start + KINDS)
        halo = jnp.where(here, jnp.where(lane == start + S_NEXT, smooth, detail), halo)
    cut_halo_ref[...] = halo


def second_kernel(layers, n_vox, models, *refs):
    (block_ref, *packets, out_ref, halo_ref, held) = refs
    rows = held.shape[1] - 2 * models
    me = lax.axis_index("vox")
    for distance, packet in enumerate(packets, 1):
        held[me ^ distance] = packet[...]
    chunks = held.shape[1] // (2 * models)
    below = [block_ref[rows:, i * LANES : (i + 1) * LANES] for i in range(chunks + 2)]
    for i in range(chunks):
        held[me, i * 2 * models : (i + 1) * 2 * models] = below[i]
    high, low = below[chunks].astype(F32), below[chunks + 1].astype(F32)
    observed = ((high[:models] + high[models:]) + low[:models])[:, :rows]
    left, right = lax.rem(me + n_vox - 1, n_vox), lax.rem(me + 1, n_vox)
    lane = lanes_of((models, LANES))
    inside = (lane >= rows) & (lane < rows + KINDS * layers)

    def edge_values(which):
        both = held[which, rows:, :].astype(F32)
        return both[:models] + both[models:]

    edge = [edge_values(z) for z in range(n_vox)]
    terms, columns = [], []
    for z in range(n_vox):
        before, after = edge[z - 1], edge[(z + 1) % n_vox]
        next_smooth = turned(after, O_LAST - E_FIRST)
        next_detail = turned(after, O_LAST - O_FIRST)
        next_even = next_smooth - 0.25 * (edge[z] + next_detail)
        term = by_kind(
            lane,
            rows,
            0.0,
            -0.25 * turned(before, E_FIRST - O_LAST),
            0.0,
            0.5 * next_even,
            -0.125 * turned(before, O_FIRST - O_LAST),
        )
        terms.append(jnp.where(inside, term, 0.0).astype(BF16))
        columns.append(held[z, :rows, :])
    predicted = nt_dot(jnp.concatenate(terms, axis=1), jnp.concatenate(columns, axis=1))
    shares = edge[0]
    for z in range(1, n_vox):
        shares = shares + edge[z]
    predicted = predicted + shares[:, :rows]

    before, own, after = (held[z, :rows, :].astype(F32) for z in (left, me, right))
    details = by_kind(
        lanes_of(own.shape),
        rows,
        0.0,
        0.0,
        0.0,
        own - 0.5 * (turned(own, O_LAST - E_LAST) + turned(after, O_LAST - E_FIRST)),
        after - 0.5 * (turned(after, O_FIRST - E_FIRST) + turned(after, O_FIRST - E_SECOND)),
    )
    out_ref[:rows, :] = by_kind(
        lanes_of(own.shape),
        rows,
        turned(after, E_NEXT - E_FIRST),
        turned(before, D_BEFORE - O_LAST) - 0.5 * (turned(before, D_BEFORE - E_LAST) + own),
        turned(after, S_NEXT - E_FIRST) + 0.25 * (turned(details, S_NEXT - D_LAST) + turned(details, S_NEXT - D_NEXT)),
        details,
        details,
    )
    out_ref[rows:, :] = jnp.zeros((2 * models, LANES), F32)
    out_ref[rows : rows + models, :rows] = observed - predicted
    out_ref[rows + models :, :rows] = observed
    before, own, after = (edge_values(z) for z in (left, me, right))
    halo_ref[...] = by_kind(
        lane, rows, 0.0, turned(before, D_BEFORE - O_LAST), turned(after, S_NEXT - E_FIRST), own, after
    )


def in_core_order(mine, other, work):
    core = lax.rem(lax.axis_index("dp"), 2)

    @pl.when(core == 0)
    def _():
        work(mine, other)

    @pl.when(core == 1)
    def _():
        work(other, mine)


def back_projected(mine, other, g_ref):
    width = mine[1].shape[1]

    def work(*cores):
        sent = [residual.astype(BF16) for residual, _, _ in cores]
        g_ref[:, :width] = sum(
            jnp.dot(r, k[...], preferred_element_type=F32) for r, (_, k, _) in zip(sent, cores)
        ).astype(BF16)
        g_ref[:, width:] = sum(
            jnp.dot(r, h[...].astype(BF16), preferred_element_type=F32) for r, (_, _, h) in zip(sent, cores)
        ).astype(BF16)

    in_core_order(mine, other, work)


def third_kernel(mine_ref, other_ref, kw_ref, kw_other_ref, g_ref):
    rows = kw_ref.shape[0]
    models = g_ref.shape[0]

    def core(ref, k):
        return ref[rows : rows + models, :rows], k, ref.at[:rows]

    back_projected(core(mine_ref, kw_ref), core(other_ref, kw_other_ref), g_ref)


def tree_sum(values):
    while len(values) > 1:
        values = [a + b for a, b in zip(values[::2], values[1::2])]
    return values[0]


def at_ends(tile, layers, base):
    return jnp.concatenate([turned(tile, -(base + KINDS * layer + 1)) for layer in range(layers)], axis=0)


def stepped(layers, base, wave_ref, cut_ref, g_refs):
    width = wave_ref.shape[1]
    gradients = [stacked(g, layers) for g in g_refs]
    smooth_g, detail_g = (tree_sum([g[p] for g in gradients]) for p in range(2))
    edge = tree_sum([g[:, width:].astype(F32) for g in g_refs])
    ends = at_ends(edge, layers, base)
    lane = lanes_of(ends.shape)
    smooth_g += jnp.where(lane == 0, 0.25 * ends, jnp.where(lane == LANES - 1, -0.125 * ends, 0.0))
    detail_g += jnp.where(lane == LANES - 1, -0.5 * ends, 0.0)
    smooth, detail = (
        shrink(w + step_size * g, cut)
        for w, g, cut in zip(stacked(wave_ref, layers), (smooth_g, detail_g), stacked(cut_ref, layers))
    )
    return smooth, detail, edge


def fourth_kernel(layers, base, wave_ref, cut_ref, halo_ref, cut_halo_ref, block_ref, block_other_ref, *refs):
    *g_refs, new_ref, pred_ref = refs
    models = wave_ref.shape[0]
    rows = base
    smooth, detail, edge = stepped(layers, base, wave_ref, cut_ref, g_refs)
    new_ref[...] = unstacked(smooth, detail, models)
    halo = shrink(halo_ref[...] + step_size * edge, cut_halo_ref[...])
    next_even = turned(halo, E_NEXT - S_NEXT) - 0.25 * (turned(halo, E_NEXT - D_LAST) + turned(halo, E_NEXT - D_NEXT))
    ends = at_ends(by_kind(lanes_of(halo.shape), base, next_even, halo), layers, base)
    model = unstacked(*inverse_wave(smooth, detail, ends), models).astype(BF16)
    pred_ref[...] = jnp.zeros_like(pred_ref)

    def work(first, second):
        pred_ref[:, :rows] = nt_dot(model, first[:rows, :])
        pred_ref[:, rows : 2 * rows] = nt_dot(model, second[:rows, :])

    in_core_order(block_ref, block_other_ref, work)


def fifth_kernel(mine_ref, other_ref, kw_ref, kw_other_ref, *refs):
    *shares, g_ref, residual_ref = refs
    models, rows = residual_ref.shape
    predicted = tree_sum([s[...] for s in shares])
    first, second = predicted[:, :rows], predicted[:, rows : 2 * rows]
    is_first = lax.rem(lax.axis_index("dp"), 2) == 0

    def core(ref, k, predicted):
        return ref[rows + models :, :rows] - predicted, k, ref.at[:rows]

    mine = core(mine_ref, kw_ref, jnp.where(is_first, first, second))
    residual_ref[...] = mine[0]
    back_projected(mine, core(other_ref, kw_other_ref, jnp.where(is_first, second, first)), g_ref)


def sixth_kernel(layers, base, wave_ref, cut_ref, *refs):
    *g_refs, new_ref = refs
    smooth, detail, _ = stepped(layers, base, wave_ref, cut_ref, g_refs)
    new_ref[...] = unstacked(smooth, detail, wave_ref.shape[0])


def from_partner(x, axis, distance):
    return lax.ppermute(x, axis, [(i, i ^ distance) for i in range(lax.axis_size(axis))])


def from_other_core(x, chips, vox):
    n_vox = lax.axis_size("vox")
    places = [(d, z) for d in range(lax.axis_size("dp")) for z in range(n_vox)]
    route = [(d * n_vox + z, (d ^ (2 * chips + 1)) * n_vox + (z ^ vox)) for d, z in places]
    return lax.ppermute(x, ("dp", "vox"), route)


def shares_of(x, size, fetch):
    lowest = 1
    while size > 4:
        parts = [x] + [fetch(x, lowest * d) for d in range(1, 4)]
        x = tree_sum([p.astype(F32) for p in parts]).astype(x.dtype)
        lowest, size = lowest * 4, size // 4
    return [x] + [fetch(x, lowest * d) for d in range(1, size)]


def over_chips(x):
    return shares_of(x, lax.axis_size("dp") // 2, lambda x, d: from_other_core(x, d, 0))


def over_vox(x):
    return shares_of(x, lax.axis_size("vox"), lambda x, d: from_other_core(x, 0, d))


def call(kernel, out_shape, *args, scratch=(), space=pltpu.VMEM):
    return pl.pallas_call(
        kernel,
        out_shape=out_shape,
        in_specs=[pl.BlockSpec(memory_space=space)] * len(args),
        out_specs=jax.tree.map(lambda _: pl.BlockSpec(memory_space=pltpu.VMEM), out_shape),
        scratch_shapes=list(scratch),
    )(*[pltpu.with_memory_space_constraint(arg, space) for arg in args])


def body(kernels, observed, initial, threshold):
    models, width = initial.shape
    rows = kernels.shape[0]
    layers = threshold.shape[1]
    n_vox = lax.axis_size("vox")
    packet_rows = rows + 2 * models
    assert width == 2 * layers * LANES and rows + KINDS * layers <= LANES and 2 * rows <= LANES
    assert packet_rows % (2 * models) == 0 and packet_rows // (2 * models) + 2 <= 2 * layers
    g_shape = pltpu.VMEM((models, width + LANES), BF16)
    k_shape = pltpu.VMEM((rows, width), BF16)

    packet, wavelets, block = call(
        functools.partial(first_kernel, layers),
        (
            pltpu.VMEM((packet_rows, LANES), BF16),
            pltpu.VMEM((models, width), F32),
            pltpu.VMEM((rows + 2 * models, width), BF16),
        ),
        initial,
        kernels,
        observed,
        scratch=[
            pltpu.VMEM((models, rows), F32),
            pltpu.VMEM((models, LANES), F32),
            pltpu.SemaphoreType.DMA((3,)),
        ],
        space=pltpu.HBM,
    )
    block_other = from_partner(block, "dp", 1)
    packets = [from_other_core(packet, 0, d) for d in range(1, n_vox)]
    kw, kw_other = (call(functools.partial(applied_kernel, layers), k_shape, b) for b in (block, block_other))
    cut, cut_halo = call(
        functools.partial(spread_kernel, layers, rows),
        (pltpu.VMEM((models, width), F32), pltpu.VMEM((models, LANES), F32)),
        jnp.swapaxes(threshold, 1, 2),
    )
    other, halo = call(
        functools.partial(second_kernel, layers, n_vox, models),
        (pltpu.VMEM((packet_rows, LANES), F32), pltpu.VMEM((models, LANES), F32)),
        block_other,
        *packets,
        scratch=[pltpu.VMEM((n_vox, packet_rows, LANES), BF16)],
    )
    mine = from_partner(other, "dp", 1)
    g = call(third_kernel, g_shape, mine, other, kw, kw_other)
    wavelets, predicted = call(
        functools.partial(fourth_kernel, layers, rows),
        (pltpu.VMEM((models, width), F32), pltpu.VMEM((models, LANES), F32)),
        wavelets,
        cut,
        halo,
        cut_halo,
        block,
        block_other,
        *over_chips(g),
    )
    g, residual = call(
        fifth_kernel,
        (g_shape, pltpu.VMEM((models, rows), F32)),
        mine,
        other,
        kw,
        kw_other,
        *over_vox(predicted),
    )
    coefficients = call(
        functools.partial(sixth_kernel, layers, rows),
        jax.ShapeDtypeStruct((models, width), F32),
        wavelets,
        cut,
        *over_chips(g),
    )
    return coefficients, residual


def solution(mesh):
    return jax.shard_map(
        body,
        mesh=mesh,
        in_specs=(P("dp", "vox"), P(None, "dp"), P(None, "vox"), P()),
        out_specs=(P(None, "vox"), P(None, "dp")),
        check_vma=False,
    )
```

```python
import functools

import jax
import jax.numpy as jnp
from jax import lax
from jax.experimental import pallas as pl
from jax.experimental.pallas import tpu as pltpu
from jax.sharding import PartitionSpec as P

step_size = 0.5
LANES = 128
KERNEL_BYTES = 8 * 2**20
F32 = jnp.float32
BF16 = jnp.bfloat16

E_LAST, E_FIRST, E_SECOND, O_LAST, O_FIRST = range(5)
E_NEXT, D_BEFORE, S_NEXT, D_LAST, D_NEXT = range(5)
KINDS = 5


def lanes_of(shape):
    return lax.broadcasted_iota(jnp.int32, shape, len(shape) - 1)


def turned(x, by):
    return pltpu.roll(x, by % LANES, x.ndim - 1)


def shifted_in(x, by, edge):
    free = 0 if by == 1 else LANES - 1
    return jnp.where(lanes_of(x.shape) == free, edge, turned(x, by))


def edge_tile(pair_of, layers, base):
    tile = None
    for layer in range(layers):
        even, odd = pair_of(layer)
        start = base + KINDS * layer
        lane = lanes_of(even.shape)
        if tile is None:
            tile = jnp.zeros_like(even)
        tile = jnp.where((lane >= start) & (lane < start + 3), turned(even, start + 1), tile)
        tile = jnp.where((lane >= start + 3) & (lane < start + 5), turned(odd, start + 4), tile)
    return tile


def kind_lane(lane, base, kind):
    return lax.rem(lane - base + KINDS * LANES, KINDS) == kind


def shrink(values, cutoff):
    return values - jnp.clip(values, -cutoff, cutoff)


def layer_tiles(ref, layer):
    start = layer * 2 * LANES
    return ref[:, start : start + LANES], ref[:, start + LANES : start + 2 * LANES]


def stacked(ref, layers):
    tiles = [layer_tiles(ref, layer) for layer in range(layers)]
    return tuple(jnp.concatenate([t[p] for t in tiles], axis=0).astype(F32) for p in range(2))


def unstacked(even, odd, models):
    rows = [slice(start, start + models) for start in range(0, even.shape[0], models)]
    return jnp.concatenate([t[r] for r in rows for t in (even, odd)], axis=1)


def nt_dot(a, b):
    return lax.dot_general(a, b, (((1,), (1,)), ((), ())), preferred_element_type=F32)


def inverse_wave(smooth, detail, edge):
    even = smooth - 0.25 * (shifted_in(detail, 1, edge) + detail)
    odd = detail + 0.5 * (even + shifted_in(even, -1, edge))
    return even, odd


def forward_wave(even, odd):
    detail = odd - 0.5 * (even + shifted_in(even, -1, 0.0))
    smooth = even + 0.25 * (shifted_in(detail, 1, 0.0) + detail)
    return smooth, detail


def by_kind(lane, base, *values):
    kind = lax.rem(lane - base + KINDS * LANES, KINDS)
    result = values[0]
    for k, value in enumerate(values[1:], 1):
        result = jnp.where(kind == k, value, result)
    return result


def pieces(x, count):
    result = []
    for _ in range(count):
        result.append(x.astype(BF16).astype(F32))
        x = x - result[-1]
    return result


def first_kernel(layers, wave_hbm, k_hbm, observed_hbm, packet_ref, wave_ref, block_ref, observed_ref, tile, arrived):
    rows = k_hbm.shape[0]
    models = wave_ref.shape[0]
    loads = [
        pltpu.make_async_copy(source, target, arrived.at[i])
        for i, (source, target) in enumerate(
            ((wave_hbm, wave_ref), (k_hbm, block_ref.at[:rows]), (observed_hbm, observed_ref))
        )
    ]
    for load in loads:
        load.start()
    loads[0].wait()
    even, odd = inverse_wave(*stacked(wave_ref, layers), 0.0)
    model = unstacked(even, odd, models).astype(BF16)
    tile[...] = edge_tile(lambda l: layer_tiles(wave_ref, l), layers, rows)
    loads[1].wait()
    loads[2].wait()
    edges = edge_tile(lambda l: tuple(t[:rows].astype(F32) for t in layer_tiles(block_ref, l)), layers, rows)
    packet_ref[:rows, :] = edges.astype(BF16)
    tile[:, :rows] = nt_dot(model, block_ref[:rows, :])
    packet_ref[rows:, :] = jnp.concatenate(pieces(tile[...], 2), axis=0).astype(BF16)
    tile[...] = jnp.zeros_like(tile)
    tile[:, :rows] = observed_ref[...]
    below = pieces(tile[...], 3) + [jnp.zeros_like(tile)]
    below = [jnp.concatenate(below[i : i + 2], axis=0).astype(BF16) for i in (0, 2)]
    packed = [packet_ref[i : i + 2 * models, :] for i in range(0, packet_ref.shape[0], 2 * models)] + below
    for i, part in enumerate(packed):
        block_ref[rows:, i * LANES : (i + 1) * LANES] = part


def applied_kernel(layers, block_ref, kw_ref):
    rows = kw_ref.shape[0]
    kw_ref[...] = unstacked(*forward_wave(*stacked(block_ref.at[:rows], layers)), rows).astype(BF16)


def spread_kernel(layers, base, threshold_ref, cut_ref, cut_halo_ref):
    models = cut_ref.shape[0]
    lane = lanes_of((models, LANES))
    halo = jnp.zeros((models, LANES), F32)
    for layer in range(layers):
        smooth, detail = (
            jnp.broadcast_to(threshold_ref[:, p, layer : layer + 1], (models, LANES)) for p in range(2)
        )
        start = 2 * LANES * layer
        cut_ref[:, start : start + LANES] = smooth
        cut_ref[:, start + LANES : start + 2 * LANES] = detail
        start = base + KINDS * layer
        here = (lane >= start) & (lane < start + KINDS)
        halo = jnp.where(here, jnp.where(lane == start + S_NEXT, smooth, detail), halo)
    cut_halo_ref[...] = halo


def second_kernel(layers, n_vox, models, *refs):
    (block_ref, *packets, out_ref, halo_ref, held) = refs
    rows = held.shape[1] - 2 * models
    me = lax.axis_index("vox")
    for distance, packet in enumerate(packets, 1):
        held[me ^ distance] = packet[...]
    chunks = held.shape[1] // (2 * models)
    below = [block_ref[rows:, i * LANES : (i + 1) * LANES] for i in range(chunks + 2)]
    for i in range(chunks):
        held[me, i * 2 * models : (i + 1) * 2 * models] = below[i]
    high, low = below[chunks].astype(F32), below[chunks + 1].astype(F32)
    observed = ((high[:models] + high[models:]) + low[:models])[:, :rows]
    left, right = lax.rem(me + n_vox - 1, n_vox), lax.rem(me + 1, n_vox)
    lane = lanes_of((models, LANES))
    inside = (lane >= rows) & (lane < rows + KINDS * layers)

    def edge_values(which):
        both = held[which, rows:, :].astype(F32)
        return both[:models] + both[models:]

    edge = [edge_values(z) for z in range(n_vox)]
    terms, columns = [], []
    for z in range(n_vox):
        before, after = edge[z - 1], edge[(z + 1) % n_vox]
        next_smooth = turned(after, O_LAST - E_FIRST)
        next_detail = turned(after, O_LAST - O_FIRST)
        next_even = next_smooth - 0.25 * (edge[z] + next_detail)
        term = by_kind(
            lane,
            rows,
            0.0,
            -0.25 * turned(before, E_FIRST - O_LAST),
            0.0,
            0.5 * next_even,
            -0.125 * turned(before, O_FIRST - O_LAST),
        )
        terms.append(jnp.where(inside, term, 0.0).astype(BF16))
        columns.append(held[z, :rows, :])
    predicted = nt_dot(jnp.concatenate(terms, axis=1), jnp.concatenate(columns, axis=1))
    shares = edge[0]
    for z in range(1, n_vox):
        shares = shares + edge[z]
    predicted = predicted + shares[:, :rows]

    before, own, after = (held[z, :rows, :].astype(F32) for z in (left, me, right))
    details = by_kind(
        lanes_of(own.shape),
        rows,
        0.0,
        0.0,
        0.0,
        own - 0.5 * (turned(own, O_LAST - E_LAST) + turned(after, O_LAST - E_FIRST)),
        after - 0.5 * (turned(after, O_FIRST - E_FIRST) + turned(after, O_FIRST - E_SECOND)),
    )
    out_ref[:rows, :] = by_kind(
        lanes_of(own.shape),
        rows,
        turned(after, E_NEXT - E_FIRST),
        turned(before, D_BEFORE - O_LAST) - 0.5 * (turned(before, D_BEFORE - E_LAST) + own),
        turned(after, S_NEXT - E_FIRST) + 0.25 * (turned(details, S_NEXT - D_LAST) + turned(details, S_NEXT - D_NEXT)),
        details,
        details,
    )
    out_ref[rows:, :] = jnp.zeros((2 * models, LANES), F32)
    out_ref[rows : rows + models, :rows] = observed - predicted
    out_ref[rows + models :, :rows] = observed
    before, own, after = (edge_values(z) for z in (left, me, right))
    halo_ref[...] = by_kind(
        lane, rows, 0.0, turned(before, D_BEFORE - O_LAST), turned(after, S_NEXT - E_FIRST), own, after
    )


def in_core_order(mine, other, work):
    core = lax.rem(lax.axis_index("dp"), 2)

    @pl.when(core == 0)
    def _():
        work(mine, other)

    @pl.when(core == 1)
    def _():
        work(other, mine)


def back_projected(mine, other, g_ref):
    width = mine[1].shape[1]

    def work(*cores):
        sent = [residual.astype(BF16) for residual, _, _ in cores]
        g_ref[:, :width] = sum(
            jnp.dot(r, k[...], preferred_element_type=F32) for r, (_, k, _) in zip(sent, cores)
        ).astype(BF16)
        g_ref[:, width:] = sum(
            jnp.dot(r, h[...].astype(BF16), preferred_element_type=F32) for r, (_, _, h) in zip(sent, cores)
        ).astype(BF16)

    in_core_order(mine, other, work)


def third_kernel(mine_ref, other_ref, kw_ref, kw_other_ref, g_ref):
    rows = kw_ref.shape[0]
    models = g_ref.shape[0]

    def core(ref, k):
        return ref[rows : rows + models, :rows], k, ref.at[:rows]

    back_projected(core(mine_ref, kw_ref), core(other_ref, kw_other_ref), g_ref)


def tree_sum(values):
    while len(values) > 1:
        values = [a + b for a, b in zip(values[::2], values[1::2])]
    return values[0]


def at_ends(tile, layers, base):
    return jnp.concatenate([turned(tile, -(base + KINDS * layer + 1)) for layer in range(layers)], axis=0)


def stepped(layers, base, wave_ref, cut_ref, g_refs):
    width = wave_ref.shape[1]
    gradients = [stacked(g, layers) for g in g_refs]
    smooth_g, detail_g = (tree_sum([g[p] for g in gradients]) for p in range(2))
    edge = tree_sum([g[:, width:].astype(F32) for g in g_refs])
    ends = at_ends(edge, layers, base)
    lane = lanes_of(ends.shape)
    smooth_g += jnp.where(lane == 0, 0.25 * ends, jnp.where(lane == LANES - 1, -0.125 * ends, 0.0))
    detail_g += jnp.where(lane == LANES - 1, -0.5 * ends, 0.0)
    smooth, detail = (
        shrink(w + step_size * g, cut)
        for w, g, cut in zip(stacked(wave_ref, layers), (smooth_g, detail_g), stacked(cut_ref, layers))
    )
    return smooth, detail, edge


def fourth_kernel(layers, base, wave_ref, cut_ref, halo_ref, cut_halo_ref, block_ref, block_other_ref, *refs):
    *g_refs, new_ref, pred_ref = refs
    models = wave_ref.shape[0]
    rows = base
    smooth, detail, edge = stepped(layers, base, wave_ref, cut_ref, g_refs)
    new_ref[...] = unstacked(smooth, detail, models)
    halo = shrink(halo_ref[...] + step_size * edge, cut_halo_ref[...])
    next_even = turned(halo, E_NEXT - S_NEXT) - 0.25 * (turned(halo, E_NEXT - D_LAST) + turned(halo, E_NEXT - D_NEXT))
    ends = at_ends(by_kind(lanes_of(halo.shape), base, next_even, halo), layers, base)
    model = unstacked(*inverse_wave(smooth, detail, ends), models).astype(BF16)
    pred_ref[...] = jnp.zeros_like(pred_ref)

    def work(first, second):
        pred_ref[:, :rows] = nt_dot(model, first[:rows, :])
        pred_ref[:, rows : 2 * rows] = nt_dot(model, second[:rows, :])

    in_core_order(block_ref, block_other_ref, work)


def fifth_kernel(mine_ref, other_ref, kw_ref, kw_other_ref, *refs):
    *shares, g_ref, residual_ref = refs
    models, rows = residual_ref.shape
    predicted = tree_sum([s[...] for s in shares])
    first, second = predicted[:, :rows], predicted[:, rows : 2 * rows]
    is_first = lax.rem(lax.axis_index("dp"), 2) == 0

    def core(ref, k, predicted):
        return ref[rows + models :, :rows] - predicted, k, ref.at[:rows]

    mine = core(mine_ref, kw_ref, jnp.where(is_first, first, second))
    residual_ref[...] = mine[0]
    back_projected(mine, core(other_ref, kw_other_ref, jnp.where(is_first, second, first)), g_ref)


def sixth_kernel(layers, base, wave_ref, cut_ref, *refs):
    *g_refs, new_ref = refs
    smooth, detail, _ = stepped(layers, base, wave_ref, cut_ref, g_refs)
    new_ref[...] = unstacked(smooth, detail, wave_ref.shape[0])


def from_partner(x, axis, distance):
    return lax.ppermute(x, axis, [(i, i ^ distance) for i in range(lax.axis_size(axis))])


def from_other_core(x, chips, vox):
    n_vox = lax.axis_size("vox")
    places = [(d, z) for d in range(lax.axis_size("dp")) for z in range(n_vox)]
    route = [(d * n_vox + z, (d ^ (2 * chips + 1)) * n_vox + (z ^ vox)) for d, z in places]
    return lax.ppermute(x, ("dp", "vox"), route)


def shares_of(x, size, fetch):
    lowest = 1
    while size > 4:
        parts = [x] + [fetch(x, lowest * d) for d in range(1, 4)]
        x = tree_sum([p.astype(F32) for p in parts]).astype(x.dtype)
        lowest, size = lowest * 4, size // 4
    return [x] + [fetch(x, lowest * d) for d in range(1, size)]


def over_chips(x):
    return shares_of(x, lax.axis_size("dp") // 2, lambda x, d: from_other_core(x, d, 0))


def over_vox(x):
    return shares_of(x, lax.axis_size("vox"), lambda x, d: from_other_core(x, 0, d))


def call(kernel, out_shape, *args, scratch=(), space=pltpu.VMEM):
    return pl.pallas_call(
        kernel,
        out_shape=out_shape,
        in_specs=[pl.BlockSpec(memory_space=space)] * len(args),
        out_specs=jax.tree.map(lambda _: pl.BlockSpec(memory_space=pltpu.VMEM), out_shape),
        scratch_shapes=list(scratch),
        compiler_params=pltpu.CompilerParams(vmem_limit_bytes=KERNEL_BYTES),
    )(*[pltpu.with_memory_space_constraint(arg, space) for arg in args])


def body(kernels, observed, initial, threshold):
    models, width = initial.shape
    rows = kernels.shape[0]
    layers = threshold.shape[1]
    n_vox = lax.axis_size("vox")
    packet_rows = rows + 2 * models
    assert width == 2 * layers * LANES and rows + KINDS * layers <= LANES and 2 * rows <= LANES
    assert packet_rows % (2 * models) == 0 and packet_rows // (2 * models) + 2 <= 2 * layers
    g_shape = pltpu.VMEM((models, width + LANES), BF16)
    k_shape = pltpu.VMEM((rows, width), BF16)

    packet, wavelets, block = call(
        functools.partial(first_kernel, layers),
        (
            pltpu.VMEM((packet_rows, LANES), BF16),
            pltpu.VMEM((models, width), F32),
            pltpu.VMEM((rows + 2 * models, width), BF16),
        ),
        initial,
        kernels,
        observed,
        scratch=[
            pltpu.VMEM((models, rows), F32),
            pltpu.VMEM((models, LANES), F32),
            pltpu.SemaphoreType.DMA((3,)),
        ],
        space=pltpu.HBM,
    )
    block_other = from_partner(block, "dp", 1)
    packets = [from_other_core(packet, 0, d) for d in range(1, n_vox)]
    kw, kw_other = (call(functools.partial(applied_kernel, layers), k_shape, b) for b in (block, block_other))
    cut, cut_halo = call(
        functools.partial(spread_kernel, layers, rows),
        (pltpu.VMEM((models, width), F32), pltpu.VMEM((models, LANES), F32)),
        jnp.swapaxes(threshold, 1, 2),
    )
    other, halo = call(
        functools.partial(second_kernel, layers, n_vox, models),
        (pltpu.VMEM((packet_rows, LANES), F32), pltpu.VMEM((models, LANES), F32)),
        block_other,
        *packets,
        scratch=[pltpu.VMEM((n_vox, packet_rows, LANES), BF16)],
    )
    mine = from_partner(other, "dp", 1)
    g = call(third_kernel, g_shape, mine, other, kw, kw_other)
    wavelets, predicted = call(
        functools.partial(fourth_kernel, layers, rows),
        (pltpu.VMEM((models, width), F32), pltpu.VMEM((models, LANES), F32)),
        wavelets,
        cut,
        halo,
        cut_halo,
        block,
        block_other,
        *over_chips(g),
    )
    g, residual = call(
        fifth_kernel,
        (g_shape, pltpu.VMEM((models, rows), F32)),
        mine,
        other,
        kw,
        kw_other,
        *over_vox(predicted),
    )
    coefficients = call(
        functools.partial(sixth_kernel, layers, rows),
        jax.ShapeDtypeStruct((models, width), F32),
        wavelets,
        cut,
        *over_chips(g),
    )
    return coefficients, residual


def solution(mesh):
    return jax.shard_map(
        body,
        mesh=mesh,
        in_specs=(P("dp", "vox"), P(None, "dp"), P(None, "vox"), P()),
        out_specs=(P(None, "vox"), P(None, "dp")),
        check_vma=False,
    )
```

```python
import functools

import jax
import jax.numpy as jnp
from jax import lax
from jax.experimental import pallas as pl
from jax.experimental.pallas import tpu as pltpu
from jax.sharding import PartitionSpec as P

step_size = 0.5
LANES = 128
KERNEL_BYTES = 8 * 2**20
F32 = jnp.float32
BF16 = jnp.bfloat16

E_LAST, E_FIRST, E_SECOND, O_LAST, O_FIRST = range(5)
E_NEXT, D_BEFORE, S_NEXT, D_LAST, D_NEXT = range(5)
KINDS = 5


def lanes_of(shape):
    return lax.broadcasted_iota(jnp.int32, shape, len(shape) - 1)


def turned(x, by):
    return pltpu.roll(x, by % LANES, x.ndim - 1)


def shifted_in(x, by, edge):
    free = 0 if by == 1 else LANES - 1
    return jnp.where(lanes_of(x.shape) == free, edge, turned(x, by))


def edge_tile(pair_of, layers, base):
    tile = None
    for layer in range(layers):
        even, odd = pair_of(layer)
        start = base + KINDS * layer
        lane = lanes_of(even.shape)
        if tile is None:
            tile = jnp.zeros_like(even)
        tile = jnp.where((lane >= start) & (lane < start + 3), turned(even, start + 1), tile)
        tile = jnp.where((lane >= start + 3) & (lane < start + 5), turned(odd, start + 4), tile)
    return tile


def kind_lane(lane, base, kind):
    return lax.rem(lane - base + KINDS * LANES, KINDS) == kind


def shrink(values, cutoff):
    return values - jnp.clip(values, -cutoff, cutoff)


def layer_tiles(ref, layer):
    start = layer * 2 * LANES
    return ref[:, start : start + LANES], ref[:, start + LANES : start + 2 * LANES]


def stacked(ref, layers):
    tiles = [layer_tiles(ref, layer) for layer in range(layers)]
    return tuple(jnp.concatenate([t[p] for t in tiles], axis=0).astype(F32) for p in range(2))


def unstacked(even, odd, models):
    rows = [slice(start, start + models) for start in range(0, even.shape[0], models)]
    return jnp.concatenate([t[r] for r in rows for t in (even, odd)], axis=1)


def nt_dot(a, b):
    return lax.dot_general(a, b, (((1,), (1,)), ((), ())), preferred_element_type=F32)


def inverse_wave(smooth, detail, edge):
    even = smooth - 0.25 * (shifted_in(detail, 1, edge) + detail)
    odd = detail + 0.5 * (even + shifted_in(even, -1, edge))
    return even, odd


def forward_wave(even, odd):
    detail = odd - 0.5 * (even + shifted_in(even, -1, 0.0))
    smooth = even + 0.25 * (shifted_in(detail, 1, 0.0) + detail)
    return smooth, detail


def by_kind(lane, base, *values):
    kind = lax.rem(lane - base + KINDS * LANES, KINDS)
    result = values[0]
    for k, value in enumerate(values[1:], 1):
        result = jnp.where(kind == k, value, result)
    return result


def pieces(x, count):
    result = []
    for _ in range(count):
        result.append(x.astype(BF16).astype(F32))
        x = x - result[-1]
    return result


def first_kernel(layers, wave_hbm, k_hbm, observed_hbm, packet_ref, wave_ref, block_ref, observed_ref, tile, arrived):
    rows = k_hbm.shape[0]
    models = wave_ref.shape[0]
    loads = [
        pltpu.make_async_copy(source, target, arrived.at[i])
        for i, (source, target) in enumerate(
            ((wave_hbm, wave_ref), (k_hbm, block_ref.at[:rows]), (observed_hbm, observed_ref))
        )
    ]
    for load in loads:
        load.start()
    loads[0].wait()
    even, odd = inverse_wave(*stacked(wave_ref, layers), 0.0)
    model = unstacked(even, odd, models).astype(BF16)
    tile[...] = edge_tile(lambda l: layer_tiles(wave_ref, l), layers, rows)
    loads[1].wait()
    loads[2].wait()
    edges = edge_tile(lambda l: tuple(t[:rows].astype(F32) for t in layer_tiles(block_ref, l)), layers, rows)
    packet_ref[:rows, :] = edges.astype(BF16)
    tile[:, :rows] = nt_dot(model, block_ref[:rows, :])
    packet_ref[rows:, :] = jnp.concatenate(pieces(tile[...], 2), axis=0).astype(BF16)
    tile[...] = jnp.zeros_like(tile)
    tile[:, :rows] = observed_ref[...]
    below = pieces(tile[...], 3) + [jnp.zeros_like(tile)]
    below = [jnp.concatenate(below[i : i + 2], axis=0).astype(BF16) for i in (0, 2)]
    packed = [packet_ref[i : i + 2 * models, :] for i in range(0, packet_ref.shape[0], 2 * models)] + below
    for i, part in enumerate(packed):
        block_ref[rows:, i * LANES : (i + 1) * LANES] = part


def applied_kernel(layers, block_ref, kw_ref):
    rows = kw_ref.shape[0]
    kw_ref[...] = unstacked(*forward_wave(*stacked(block_ref.at[:rows], layers)), rows).astype(BF16)


def spread_kernel(layers, base, threshold_ref, cut_ref, cut_halo_ref):
    models = cut_ref.shape[0]
    lane = lanes_of((models, LANES))
    halo = jnp.zeros((models, LANES), F32)
    for layer in range(layers):
        smooth, detail = (
            jnp.broadcast_to(threshold_ref[:, p, layer : layer + 1], (models, LANES)) for p in range(2)
        )
        start = 2 * LANES * layer
        cut_ref[:, start : start + LANES] = smooth
        cut_ref[:, start + LANES : start + 2 * LANES] = detail
        start = base + KINDS * layer
        here = (lane >= start) & (lane < start + KINDS)
        halo = jnp.where(here, jnp.where(lane == start + S_NEXT, smooth, detail), halo)
    cut_halo_ref[...] = halo


def second_kernel(layers, n_vox, models, *refs):
    (block_ref, *packets, out_ref, halo_ref, held) = refs
    rows = held.shape[1] - 2 * models
    me = lax.axis_index("vox")
    for distance, packet in enumerate(packets, 1):
        held[me ^ distance] = packet[...]
    chunks = held.shape[1] // (2 * models)
    below = [block_ref[rows:, i * LANES : (i + 1) * LANES] for i in range(chunks + 2)]
    for i in range(chunks):
        held[me, i * 2 * models : (i + 1) * 2 * models] = below[i]
    high, low = below[chunks].astype(F32), below[chunks + 1].astype(F32)
    observed = ((high[:models] + high[models:]) + low[:models])[:, :rows]
    left, right = lax.rem(me + n_vox - 1, n_vox), lax.rem(me + 1, n_vox)
    lane = lanes_of((models, LANES))
    inside = (lane >= rows) & (lane < rows + KINDS * layers)

    def edge_values(which):
        both = held[which, rows:, :].astype(F32)
        return both[:models] + both[models:]

    edge = [edge_values(z) for z in range(n_vox)]
    terms, columns = [], []
    for z in range(n_vox):
        before, after = edge[z - 1], edge[(z + 1) % n_vox]
        next_smooth = turned(after, O_LAST - E_FIRST)
        next_detail = turned(after, O_LAST - O_FIRST)
        next_even = next_smooth - 0.25 * (edge[z] + next_detail)
        term = by_kind(
            lane,
            rows,
            0.0,
            -0.25 * turned(before, E_FIRST - O_LAST),
            0.0,
            0.5 * next_even,
            -0.125 * turned(before, O_FIRST - O_LAST),
        )
        terms.append(jnp.where(inside, term, 0.0).astype(BF16))
        columns.append(held[z, :rows, :])
    predicted = nt_dot(jnp.concatenate(terms, axis=1), jnp.concatenate(columns, axis=1))
    shares = edge[0]
    for z in range(1, n_vox):
        shares = shares + edge[z]
    predicted = predicted + shares[:, :rows]

    before, own, after = (held[z, :rows, :].astype(F32) for z in (left, me, right))
    details = by_kind(
        lanes_of(own.shape),
        rows,
        0.0,
        0.0,
        0.0,
        own - 0.5 * (turned(own, O_LAST - E_LAST) + turned(after, O_LAST - E_FIRST)),
        after - 0.5 * (turned(after, O_FIRST - E_FIRST) + turned(after, O_FIRST - E_SECOND)),
    )
    out_ref[:rows, :] = by_kind(
        lanes_of(own.shape),
        rows,
        turned(after, E_NEXT - E_FIRST),
        turned(before, D_BEFORE - O_LAST) - 0.5 * (turned(before, D_BEFORE - E_LAST) + own),
        turned(after, S_NEXT - E_FIRST) + 0.25 * (turned(details, S_NEXT - D_LAST) + turned(details, S_NEXT - D_NEXT)),
        details,
        details,
    )
    out_ref[rows:, :] = jnp.zeros((2 * models, LANES), F32)
    out_ref[rows : rows + models, :rows] = observed - predicted
    out_ref[rows + models :, :rows] = observed
    before, own, after = (edge_values(z) for z in (left, me, right))
    halo_ref[...] = by_kind(
        lane, rows, 0.0, turned(before, D_BEFORE - O_LAST), turned(after, S_NEXT - E_FIRST), own, after
    )


def in_core_order(mine, other, work):
    core = lax.rem(lax.axis_index("dp"), 2)

    @pl.when(core == 0)
    def _():
        work(mine, other)

    @pl.when(core == 1)
    def _():
        work(other, mine)


def back_projected(mine, other, g_ref):
    width = mine[1].shape[1]

    def work(*cores):
        sent = [residual.astype(BF16) for residual, _, _ in cores]
        g_ref[:, :width] = sum(
            jnp.dot(r, k[...], preferred_element_type=F32) for r, (_, k, _) in zip(sent, cores)
        ).astype(BF16)
        g_ref[:, width:] = sum(
            jnp.dot(r, h[...].astype(BF16), preferred_element_type=F32) for r, (_, _, h) in zip(sent, cores)
        ).astype(BF16)

    in_core_order(mine, other, work)


def third_kernel(mine_ref, other_ref, kw_ref, kw_other_ref, g_ref):
    rows = kw_ref.shape[0]
    models = g_ref.shape[0]

    def core(ref, k):
        return ref[rows : rows + models, :rows], k, ref.at[:rows]

    back_projected(core(mine_ref, kw_ref), core(other_ref, kw_other_ref), g_ref)


def added(shares):
    if len(shares) < 4:
        return sum(shares[1:], shares[0])
    own, near, swapped, far = shares
    is_first = lax.rem(lax.axis_index("dp"), 2) == 0
    return (own + jnp.where(is_first, near, swapped)) + (jnp.where(is_first, swapped, near) + far)


def at_ends(tile, layers, base):
    return jnp.concatenate([turned(tile, -(base + KINDS * layer + 1)) for layer in range(layers)], axis=0)


def stepped(layers, base, wave_ref, cut_ref, g_refs):
    width = wave_ref.shape[1]
    gradients = [stacked(g, layers) for g in g_refs]
    smooth_g, detail_g = (added([g[p] for g in gradients]) for p in range(2))
    edge = added([g[:, width:].astype(F32) for g in g_refs])
    ends = at_ends(edge, layers, base)
    lane = lanes_of(ends.shape)
    smooth_g += jnp.where(lane == 0, 0.25 * ends, jnp.where(lane == LANES - 1, -0.125 * ends, 0.0))
    detail_g += jnp.where(lane == LANES - 1, -0.5 * ends, 0.0)
    smooth, detail = (
        shrink(w + step_size * g, cut)
        for w, g, cut in zip(stacked(wave_ref, layers), (smooth_g, detail_g), stacked(cut_ref, layers))
    )
    return smooth, detail, edge


def fourth_kernel(layers, base, wave_ref, cut_ref, halo_ref, cut_halo_ref, block_ref, block_other_ref, *refs):
    *g_refs, new_ref, pred_ref = refs
    models = wave_ref.shape[0]
    rows = base
    smooth, detail, edge = stepped(layers, base, wave_ref, cut_ref, g_refs)
    new_ref[...] = unstacked(smooth, detail, models)
    halo = shrink(halo_ref[...] + step_size * edge, cut_halo_ref[...])
    next_even = turned(halo, E_NEXT - S_NEXT) - 0.25 * (turned(halo, E_NEXT - D_LAST) + turned(halo, E_NEXT - D_NEXT))
    ends = at_ends(by_kind(lanes_of(halo.shape), base, next_even, halo), layers, base)
    model = unstacked(*inverse_wave(smooth, detail, ends), models).astype(BF16)
    pred_ref[...] = jnp.zeros_like(pred_ref)

    def work(first, second):
        pred_ref[:, :rows] = nt_dot(model, first[:rows, :])
        pred_ref[:, rows : 2 * rows] = nt_dot(model, second[:rows, :])

    in_core_order(block_ref, block_other_ref, work)


def fifth_kernel(mine_ref, other_ref, kw_ref, kw_other_ref, *refs):
    *shares, g_ref, residual_ref = refs
    models, rows = residual_ref.shape
    predicted = added([s[...] for s in shares])
    first, second = predicted[:, :rows], predicted[:, rows : 2 * rows]
    is_first = lax.rem(lax.axis_index("dp"), 2) == 0

    def core(ref, k, predicted):
        return ref[rows + models :, :rows] - predicted, k, ref.at[:rows]

    mine = core(mine_ref, kw_ref, jnp.where(is_first, first, second))
    residual_ref[...] = mine[0]
    back_projected(mine, core(other_ref, kw_other_ref, jnp.where(is_first, second, first)), g_ref)


def sixth_kernel(layers, base, wave_ref, cut_ref, *refs):
    *g_refs, new_ref = refs
    smooth, detail, _ = stepped(layers, base, wave_ref, cut_ref, g_refs)
    new_ref[...] = unstacked(smooth, detail, wave_ref.shape[0])


def from_partner(x, axis, distance):
    return lax.ppermute(x, axis, [(i, i ^ distance) for i in range(lax.axis_size(axis))])


def from_other_core(x, *steps):
    n_vox = lax.axis_size("vox")
    route = []
    for d in range(lax.axis_size("dp")):
        chips, vox = steps[(d + 1) % 2 % len(steps)]
        route += [(d * n_vox + z, (d ^ (2 * chips + 1)) * n_vox + (z ^ vox)) for z in range(n_vox)]
    return lax.ppermute(x, ("dp", "vox"), route)


def shares_of(x, size, step):
    lowest = 1
    while True:
        near, middle, far = (step(lowest * n) for n in (1, 2, 3))
        if size < 4:
            return [x] + [from_other_core(x, near)] * (size - 1)
        fetched = from_other_core(x, near, middle)
        shares = [x, fetched, from_partner(fetched, "dp", 1), from_other_core(x, far)]
        if size == 4:
            return shares
        x = added([s.astype(F32) for s in shares]).astype(x.dtype)
        lowest, size = lowest * 4, size // 4


def over_chips(x):
    return shares_of(x, lax.axis_size("dp") // 2, lambda n: (n, 0))


def over_vox(x):
    return shares_of(x, lax.axis_size("vox"), lambda n: (0, n))


def call(kernel, out_shape, *args, scratch=(), space=pltpu.VMEM):
    return pl.pallas_call(
        kernel,
        out_shape=out_shape,
        in_specs=[pl.BlockSpec(memory_space=space)] * len(args),
        out_specs=jax.tree.map(lambda _: pl.BlockSpec(memory_space=pltpu.VMEM), out_shape),
        scratch_shapes=list(scratch),
        compiler_params=pltpu.CompilerParams(vmem_limit_bytes=KERNEL_BYTES),
    )(*[pltpu.with_memory_space_constraint(arg, space) for arg in args])


def body(kernels, observed, initial, threshold):
    models, width = initial.shape
    rows = kernels.shape[0]
    layers = threshold.shape[1]
    n_vox = lax.axis_size("vox")
    packet_rows = rows + 2 * models
    assert width == 2 * layers * LANES and rows + KINDS * layers <= LANES and 2 * rows <= LANES
    assert packet_rows % (2 * models) == 0 and packet_rows // (2 * models) + 2 <= 2 * layers
    g_shape = pltpu.VMEM((models, width + LANES), BF16)
    k_shape = pltpu.VMEM((rows, width), BF16)

    packet, wavelets, block = call(
        functools.partial(first_kernel, layers),
        (
            pltpu.VMEM((packet_rows, LANES), BF16),
            pltpu.VMEM((models, width), F32),
            pltpu.VMEM((rows + 2 * models, width), BF16),
        ),
        initial,
        kernels,
        observed,
        scratch=[
            pltpu.VMEM((models, rows), F32),
            pltpu.VMEM((models, LANES), F32),
            pltpu.SemaphoreType.DMA((3,)),
        ],
        space=pltpu.HBM,
    )
    block_other = from_partner(block, "dp", 1)
    packets = [from_other_core(packet, (0, d)) for d in range(1, n_vox)]
    kw, kw_other = (call(functools.partial(applied_kernel, layers), k_shape, b) for b in (block, block_other))
    cut, cut_halo = call(
        functools.partial(spread_kernel, layers, rows),
        (pltpu.VMEM((models, width), F32), pltpu.VMEM((models, LANES), F32)),
        jnp.swapaxes(threshold, 1, 2),
    )
    other, halo = call(
        functools.partial(second_kernel, layers, n_vox, models),
        (pltpu.VMEM((packet_rows, LANES), F32), pltpu.VMEM((models, LANES), F32)),
        block_other,
        *packets,
        scratch=[pltpu.VMEM((n_vox, packet_rows, LANES), BF16)],
    )
    mine = from_partner(other, "dp", 1)
    g = call(third_kernel, g_shape, mine, other, kw, kw_other)
    wavelets, predicted = call(
        functools.partial(fourth_kernel, layers, rows),
        (pltpu.VMEM((models, width), F32), pltpu.VMEM((models, LANES), F32)),
        wavelets,
        cut,
        halo,
        cut_halo,
        block,
        block_other,
        *over_chips(g),
    )
    g, residual = call(
        fifth_kernel,
        (g_shape, pltpu.VMEM((models, rows), F32)),
        mine,
        other,
        kw,
        kw_other,
        *over_vox(predicted),
    )
    coefficients = call(
        functools.partial(sixth_kernel, layers, rows),
        jax.ShapeDtypeStruct((models, width), F32),
        wavelets,
        cut,
        *over_chips(g),
    )
    return coefficients, residual


def solution(mesh):
    return jax.shard_map(
        body,
        mesh=mesh,
        in_specs=(P("dp", "vox"), P(None, "dp"), P(None, "vox"), P()),
        out_specs=(P(None, "vox"), P(None, "dp")),
        check_vma=False,
    )
```

```python
import functools

import jax
import jax.numpy as jnp
from jax import lax
from jax.experimental import pallas as pl
from jax.experimental.pallas import tpu as pltpu
from jax.sharding import PartitionSpec as P

step_size = 0.5
LANES = 128
KERNEL_BYTES = 8 * 2**20
F32 = jnp.float32
BF16 = jnp.bfloat16

E_LAST, E_FIRST, E_SECOND, O_LAST, O_FIRST = range(5)
E_NEXT, D_BEFORE, S_NEXT, D_LAST, D_NEXT = range(5)
KINDS = 5


def lanes_of(shape):
    return lax.broadcasted_iota(jnp.int32, shape, len(shape) - 1)


def turned(x, by):
    return pltpu.roll(x, by % LANES, x.ndim - 1)


def shifted_in(x, by, edge):
    free = 0 if by == 1 else LANES - 1
    return jnp.where(lanes_of(x.shape) == free, edge, turned(x, by))


def edge_tile(pair_of, layers, base):
    tile = None
    for layer in range(layers):
        even, odd = pair_of(layer)
        start = base + KINDS * layer
        lane = lanes_of(even.shape)
        if tile is None:
            tile = jnp.zeros_like(even)
        tile = jnp.where((lane >= start) & (lane < start + 3), turned(even, start + 1), tile)
        tile = jnp.where((lane >= start + 3) & (lane < start + 5), turned(odd, start + 4), tile)
    return tile


def kind_lane(lane, base, kind):
    return lax.rem(lane - base + KINDS * LANES, KINDS) == kind


def shrink(values, cutoff):
    return values - jnp.clip(values, -cutoff, cutoff)


def layer_tiles(ref, layer):
    start = layer * 2 * LANES
    return ref[:, start : start + LANES], ref[:, start + LANES : start + 2 * LANES]


def stacked(ref, layers):
    tiles = [layer_tiles(ref, layer) for layer in range(layers)]
    return tuple(jnp.concatenate([t[p] for t in tiles], axis=0).astype(F32) for p in range(2))


def unstacked(even, odd, models):
    rows = [slice(start, start + models) for start in range(0, even.shape[0], models)]
    return jnp.concatenate([t[r] for r in rows for t in (even, odd)], axis=1)


def nt_dot(a, b):
    return lax.dot_general(a, b, (((1,), (1,)), ((), ())), preferred_element_type=F32)


def inverse_wave(smooth, detail, edge):
    even = smooth - 0.25 * (shifted_in(detail, 1, edge) + detail)
    odd = detail + 0.5 * (even + shifted_in(even, -1, edge))
    return even, odd


def forward_wave(even, odd):
    detail = odd - 0.5 * (even + shifted_in(even, -1, 0.0))
    smooth = even + 0.25 * (shifted_in(detail, 1, 0.0) + detail)
    return smooth, detail


def by_kind(lane, base, *values):
    kind = lax.rem(lane - base + KINDS * LANES, KINDS)
    result = values[0]
    for k, value in enumerate(values[1:], 1):
        result = jnp.where(kind == k, value, result)
    return result


def pieces(x, count):
    result = []
    for _ in range(count):
        result.append(x.astype(BF16).astype(F32))
        x = x - result[-1]
    return result


def first_kernel(layers, wave_hbm, k_hbm, observed_hbm, packet_ref, wave_ref, block_ref, observed_ref, tile, arrived):
    rows = k_hbm.shape[0]
    models = wave_ref.shape[0]
    loads = [
        pltpu.make_async_copy(source, target, arrived.at[i])
        for i, (source, target) in enumerate(
            ((wave_hbm, wave_ref), (k_hbm, block_ref.at[:rows]), (observed_hbm, observed_ref))
        )
    ]
    for load in loads:
        load.start()
    loads[0].wait()
    even, odd = inverse_wave(*stacked(wave_ref, layers), 0.0)
    model = unstacked(even, odd, models).astype(BF16)
    tile[...] = edge_tile(lambda l: layer_tiles(wave_ref, l), layers, rows)
    loads[1].wait()
    loads[2].wait()
    edges = edge_tile(lambda l: tuple(t[:rows].astype(F32) for t in layer_tiles(block_ref, l)), layers, rows)
    packet_ref[:rows, :] = edges.astype(BF16)
    tile[:, :rows] = nt_dot(model, block_ref[:rows, :])
    packet_ref[rows:, :] = jnp.concatenate(pieces(tile[...], 2), axis=0).astype(BF16)
    tile[...] = jnp.zeros_like(tile)
    tile[:, :rows] = observed_ref[...]
    below = pieces(tile[...], 3) + [jnp.zeros_like(tile)]
    below = [jnp.concatenate(below[i : i + 2], axis=0).astype(BF16) for i in (0, 2)]
    packed = [packet_ref[i : i + 2 * models, :] for i in range(0, packet_ref.shape[0], 2 * models)] + below
    for i, part in enumerate(packed):
        block_ref[rows:, i * LANES : (i + 1) * LANES] = part


def applied_kernel(layers, block_ref, kw_ref):
    rows = kw_ref.shape[0]
    kw_ref[...] = unstacked(*forward_wave(*stacked(block_ref.at[:rows], layers)), rows).astype(BF16)


def spread_kernel(layers, base, threshold_ref, cut_ref, cut_halo_ref):
    models = cut_ref.shape[0]
    lane = lanes_of((models, LANES))
    halo = jnp.zeros((models, LANES), F32)
    for layer in range(layers):
        smooth, detail = (
            jnp.broadcast_to(threshold_ref[:, p, layer : layer + 1], (models, LANES)) for p in range(2)
        )
        start = 2 * LANES * layer
        cut_ref[:, start : start + LANES] = smooth
        cut_ref[:, start + LANES : start + 2 * LANES] = detail
        start = base + KINDS * layer
        here = (lane >= start) & (lane < start + KINDS)
        halo = jnp.where(here, jnp.where(lane == start + S_NEXT, smooth, detail), halo)
    cut_halo_ref[...] = halo


def second_kernel(layers, n_vox, models, *refs):
    (block_ref, *packets, out_ref, halo_ref, held) = refs
    rows = held.shape[1] - 2 * models
    me = lax.axis_index("vox")
    for distance, packet in enumerate(packets, 1):
        held[me ^ distance] = packet[...]
    chunks = held.shape[1] // (2 * models)
    below = [block_ref[rows:, i * LANES : (i + 1) * LANES] for i in range(chunks + 2)]
    for i in range(chunks):
        held[me, i * 2 * models : (i + 1) * 2 * models] = below[i]
    high, low = below[chunks].astype(F32), below[chunks + 1].astype(F32)
    observed = ((high[:models] + high[models:]) + low[:models])[:, :rows]
    left, right = lax.rem(me + n_vox - 1, n_vox), lax.rem(me + 1, n_vox)
    lane = lanes_of((models, LANES))
    inside = (lane >= rows) & (lane < rows + KINDS * layers)

    def edge_values(which):
        both = held[which, rows:, :].astype(F32)
        return both[:models] + both[models:]

    edge = [edge_values(z) for z in range(n_vox)]
    terms, columns = [], []
    for z in range(n_vox):
        before, after = edge[z - 1], edge[(z + 1) % n_vox]
        next_smooth = turned(after, O_LAST - E_FIRST)
        next_detail = turned(after, O_LAST - O_FIRST)
        next_even = next_smooth - 0.25 * (edge[z] + next_detail)
        term = by_kind(
            lane,
            rows,
            0.0,
            -0.25 * turned(before, E_FIRST - O_LAST),
            0.0,
            0.5 * next_even,
            -0.125 * turned(before, O_FIRST - O_LAST),
        )
        terms.append(jnp.where(inside, term, 0.0).astype(BF16))
        columns.append(held[z, :rows, :])
    predicted = nt_dot(jnp.concatenate(terms, axis=1), jnp.concatenate(columns, axis=1))
    shares = edge[0]
    for z in range(1, n_vox):
        shares = shares + edge[z]
    predicted = predicted + shares[:, :rows]

    before, own, after = (held[z, :rows, :].astype(F32) for z in (left, me, right))
    details = by_kind(
        lanes_of(own.shape),
        rows,
        0.0,
        0.0,
        0.0,
        own - 0.5 * (turned(own, O_LAST - E_LAST) + turned(after, O_LAST - E_FIRST)),
        after - 0.5 * (turned(after, O_FIRST - E_FIRST) + turned(after, O_FIRST - E_SECOND)),
    )
    out_ref[:rows, :] = by_kind(
        lanes_of(own.shape),
        rows,
        turned(after, E_NEXT - E_FIRST),
        turned(before, D_BEFORE - O_LAST) - 0.5 * (turned(before, D_BEFORE - E_LAST) + own),
        turned(after, S_NEXT - E_FIRST) + 0.25 * (turned(details, S_NEXT - D_LAST) + turned(details, S_NEXT - D_NEXT)),
        details,
        details,
    )
    out_ref[rows:, :] = jnp.zeros((2 * models, LANES), F32)
    out_ref[rows : rows + models, :rows] = observed - predicted
    out_ref[rows + models :, :rows] = observed
    before, own, after = (edge_values(z) for z in (left, me, right))
    halo_ref[...] = by_kind(
        lane, rows, 0.0, turned(before, D_BEFORE - O_LAST), turned(after, S_NEXT - E_FIRST), own, after
    )


def in_core_order(mine, other, work):
    core = lax.rem(lax.axis_index("dp"), 2)

    @pl.when(core == 0)
    def _():
        work(mine, other)

    @pl.when(core == 1)
    def _():
        work(other, mine)


def back_projected(mine, other, g_ref):
    width = mine[1].shape[1]

    def work(*cores):
        sent = [residual.astype(BF16) for residual, _, _ in cores]
        g_ref[:, :width] = sum(
            jnp.dot(r, k[...], preferred_element_type=F32) for r, (_, k, _) in zip(sent, cores)
        ).astype(BF16)
        g_ref[:, width:] = sum(
            jnp.dot(r, h[...].astype(BF16), preferred_element_type=F32) for r, (_, _, h) in zip(sent, cores)
        ).astype(BF16)

    in_core_order(mine, other, work)


def third_kernel(mine_ref, other_ref, kw_ref, kw_other_ref, g_ref):
    rows = kw_ref.shape[0]
    models = g_ref.shape[0]

    def core(ref, k):
        return ref[rows : rows + models, :rows], k, ref.at[:rows]

    back_projected(core(mine_ref, kw_ref), core(other_ref, kw_other_ref), g_ref)


def added(shares, swapped=False):
    if len(shares) < 4:
        return sum(shares[1:], shares[0])
    own, near, middle, far = shares
    if swapped:
        is_first = lax.rem(lax.axis_index("dp"), 2) == 0
        near, middle = jnp.where(is_first, near, middle), jnp.where(is_first, middle, near)
    return (own + near) + (middle + far)


def at_ends(tile, layers, base):
    return jnp.concatenate([turned(tile, -(base + KINDS * layer + 1)) for layer in range(layers)], axis=0)


def stepped(layers, base, wave_ref, cut_ref, g_refs):
    width = wave_ref.shape[1]
    gradients = [stacked(g, layers) for g in g_refs]
    smooth_g, detail_g = (added([g[p] for g in gradients], True) for p in range(2))
    edge = added([g[:, width:].astype(F32) for g in g_refs], True)
    ends = at_ends(edge, layers, base)
    lane = lanes_of(ends.shape)
    smooth_g += jnp.where(lane == 0, 0.25 * ends, jnp.where(lane == LANES - 1, -0.125 * ends, 0.0))
    detail_g += jnp.where(lane == LANES - 1, -0.5 * ends, 0.0)
    smooth, detail = (
        shrink(w + step_size * g, cut)
        for w, g, cut in zip(stacked(wave_ref, layers), (smooth_g, detail_g), stacked(cut_ref, layers))
    )
    return smooth, detail, edge


def fourth_kernel(layers, base, wave_ref, cut_ref, halo_ref, cut_halo_ref, block_ref, block_other_ref, *refs):
    *g_refs, new_ref, pred_ref = refs
    models = wave_ref.shape[0]
    rows = base
    smooth, detail, edge = stepped(layers, base, wave_ref, cut_ref, g_refs)
    new_ref[...] = unstacked(smooth, detail, models)
    halo = shrink(halo_ref[...] + step_size * edge, cut_halo_ref[...])
    next_even = turned(halo, E_NEXT - S_NEXT) - 0.25 * (turned(halo, E_NEXT - D_LAST) + turned(halo, E_NEXT - D_NEXT))
    ends = at_ends(by_kind(lanes_of(halo.shape), base, next_even, halo), layers, base)
    model = unstacked(*inverse_wave(smooth, detail, ends), models).astype(BF16)
    pred_ref[...] = jnp.zeros_like(pred_ref)

    def work(first, second):
        pred_ref[:, :rows] = nt_dot(model, first[:rows, :])
        pred_ref[:, rows : 2 * rows] = nt_dot(model, second[:rows, :])

    in_core_order(block_ref, block_other_ref, work)


def fifth_kernel(mine_ref, other_ref, kw_ref, kw_other_ref, *refs):
    *shares, g_ref, residual_ref = refs
    models, rows = residual_ref.shape
    predicted = added([s[...] for s in shares])
    first, second = predicted[:, :rows], predicted[:, rows : 2 * rows]
    is_first = lax.rem(lax.axis_index("dp"), 2) == 0

    def core(ref, k, predicted):
        return ref[rows + models :, :rows] - predicted, k, ref.at[:rows]

    mine = core(mine_ref, kw_ref, jnp.where(is_first, first, second))
    residual_ref[...] = mine[0]
    back_projected(mine, core(other_ref, kw_other_ref, jnp.where(is_first, second, first)), g_ref)


def sixth_kernel(layers, base, wave_ref, cut_ref, *refs):
    *g_refs, new_ref = refs
    smooth, detail, _ = stepped(layers, base, wave_ref, cut_ref, g_refs)
    new_ref[...] = unstacked(smooth, detail, wave_ref.shape[0])


def from_partner(x, axis, distance):
    return lax.ppermute(x, axis, [(i, i ^ distance) for i in range(lax.axis_size(axis))])


def from_other_core(x, *steps):
    n_vox = lax.axis_size("vox")
    route = []
    for d in range(lax.axis_size("dp")):
        chips, vox = steps[(d + 1) % 2 % len(steps)]
        route += [(d * n_vox + z, (d ^ (2 * chips + 1)) * n_vox + (z ^ vox)) for z in range(n_vox)]
    return lax.ppermute(x, ("dp", "vox"), route)


def all_shares(x, step):
    return [x] + [from_other_core(x, step(n)) for n in (1, 2, 3)]


def swapped_shares(x, step):
    fetched = from_other_core(x, step(1), step(2))
    return [x, fetched, from_partner(fetched, "dp", 1), from_other_core(x, step(3))]


def shares_over(x, size, step, four, **how):
    lowest = 1
    while size > 4:
        x = added([s.astype(F32) for s in four(x, lambda n: step(lowest * n))], **how).astype(x.dtype)
        lowest, size = lowest * 4, size // 4
    if size == 4:
        return four(x, lambda n: step(lowest * n))
    return [x] + [from_other_core(x, step(lowest))] * (size - 1)


def over_chips(x):
    return shares_over(x, lax.axis_size("dp") // 2, lambda n: (n, 0), swapped_shares, swapped=True)


def over_vox(x):
    return shares_over(x, lax.axis_size("vox"), lambda n: (0, n), all_shares)


def call(kernel, out_shape, *args, scratch=(), space=pltpu.VMEM):
    return pl.pallas_call(
        kernel,
        out_shape=out_shape,
        in_specs=[pl.BlockSpec(memory_space=space)] * len(args),
        out_specs=jax.tree.map(lambda _: pl.BlockSpec(memory_space=pltpu.VMEM), out_shape),
        scratch_shapes=list(scratch),
        compiler_params=pltpu.CompilerParams(vmem_limit_bytes=KERNEL_BYTES),
    )(*[pltpu.with_memory_space_constraint(arg, space) for arg in args])


def body(kernels, observed, initial, threshold):
    models, width = initial.shape
    rows = kernels.shape[0]
    layers = threshold.shape[1]
    n_vox = lax.axis_size("vox")
    packet_rows = rows + 2 * models
    assert width == 2 * layers * LANES and rows + KINDS * layers <= LANES and 2 * rows <= LANES
    assert packet_rows % (2 * models) == 0 and packet_rows // (2 * models) + 2 <= 2 * layers
    g_shape = pltpu.VMEM((models, width + LANES), BF16)
    k_shape = pltpu.VMEM((rows, width), BF16)

    packet, wavelets, block = call(
        functools.partial(first_kernel, layers),
        (
            pltpu.VMEM((packet_rows, LANES), BF16),
            pltpu.VMEM((models, width), F32),
            pltpu.VMEM((rows + 2 * models, width), BF16),
        ),
        initial,
        kernels,
        observed,
        scratch=[
            pltpu.VMEM((models, rows), F32),
            pltpu.VMEM((models, LANES), F32),
            pltpu.SemaphoreType.DMA((3,)),
        ],
        space=pltpu.HBM,
    )
    block_other = from_partner(block, "dp", 1)
    packets = [from_other_core(packet, (0, d)) for d in range(1, n_vox)]
    kw, kw_other = (call(functools.partial(applied_kernel, layers), k_shape, b) for b in (block, block_other))
    cut, cut_halo = call(
        functools.partial(spread_kernel, layers, rows),
        (pltpu.VMEM((models, width), F32), pltpu.VMEM((models, LANES), F32)),
        jnp.swapaxes(threshold, 1, 2),
    )
    other, halo = call(
        functools.partial(second_kernel, layers, n_vox, models),
        (pltpu.VMEM((packet_rows, LANES), F32), pltpu.VMEM((models, LANES), F32)),
        block_other,
        *packets,
        scratch=[pltpu.VMEM((n_vox, packet_rows, LANES), BF16)],
    )
    mine = from_partner(other, "dp", 1)
    g = call(third_kernel, g_shape, mine, other, kw, kw_other)
    wavelets, predicted = call(
        functools.partial(fourth_kernel, layers, rows),
        (pltpu.VMEM((models, width), F32), pltpu.VMEM((models, LANES), F32)),
        wavelets,
        cut,
        halo,
        cut_halo,
        block,
        block_other,
        *over_chips(g),
    )
    g, residual = call(
        fifth_kernel,
        (g_shape, pltpu.VMEM((models, rows), F32)),
        mine,
        other,
        kw,
        kw_other,
        *over_vox(predicted),
    )
    coefficients = call(
        functools.partial(sixth_kernel, layers, rows),
        jax.ShapeDtypeStruct((models, width), F32),
        wavelets,
        cut,
        *over_chips(g),
    )
    return coefficients, residual


def solution(mesh):
    return jax.shard_map(
        body,
        mesh=mesh,
        in_specs=(P("dp", "vox"), P(None, "dp"), P(None, "vox"), P()),
        out_specs=(P(None, "vox"), P(None, "dp")),
        check_vma=False,
    )
```

```python
import functools

import jax
import jax.numpy as jnp
from jax import lax
from jax.experimental import pallas as pl
from jax.experimental.pallas import tpu as pltpu
from jax.sharding import PartitionSpec as P

step_size = 0.5
LANES = 128
KERNEL_BYTES = 8 * 2**20
F32 = jnp.float32
BF16 = jnp.bfloat16

E_LAST, E_FIRST, E_SECOND, O_LAST, O_FIRST = range(5)
E_NEXT, D_BEFORE, S_NEXT, D_LAST, D_NEXT = range(5)
KINDS = 5


def lanes_of(shape):
    return lax.broadcasted_iota(jnp.int32, shape, len(shape) - 1)


def turned(x, by):
    return pltpu.roll(x, by % LANES, x.ndim - 1)


def shifted_in(x, by, edge):
    free = 0 if by == 1 else LANES - 1
    return jnp.where(lanes_of(x.shape) == free, edge, turned(x, by))


def edge_tile(pair_of, layers, base):
    tile = None
    for layer in range(layers):
        even, odd = pair_of(layer)
        start = base + KINDS * layer
        lane = lanes_of(even.shape)
        if tile is None:
            tile = jnp.zeros_like(even)
        tile = jnp.where((lane >= start) & (lane < start + 3), turned(even, start + 1), tile)
        tile = jnp.where((lane >= start + 3) & (lane < start + 5), turned(odd, start + 4), tile)
    return tile


def kind_lane(lane, base, kind):
    return lax.rem(lane - base + KINDS * LANES, KINDS) == kind


def shrink(values, cutoff):
    return values - jnp.clip(values, -cutoff, cutoff)


def layer_tiles(ref, layer):
    start = layer * 2 * LANES
    return ref[:, start : start + LANES], ref[:, start + LANES : start + 2 * LANES]


def stacked(ref, layers):
    tiles = [layer_tiles(ref, layer) for layer in range(layers)]
    return tuple(jnp.concatenate([t[p] for t in tiles], axis=0).astype(F32) for p in range(2))


def unstacked(even, odd, models):
    rows = [slice(start, start + models) for start in range(0, even.shape[0], models)]
    return jnp.concatenate([t[r] for r in rows for t in (even, odd)], axis=1)


def nt_dot(a, b):
    return lax.dot_general(a, b, (((1,), (1,)), ((), ())), preferred_element_type=F32)


def inverse_wave(smooth, detail, edge):
    even = smooth - 0.25 * (shifted_in(detail, 1, edge) + detail)
    odd = detail + 0.5 * (even + shifted_in(even, -1, edge))
    return even, odd


def forward_wave(even, odd):
    detail = odd - 0.5 * (even + shifted_in(even, -1, 0.0))
    smooth = even + 0.25 * (shifted_in(detail, 1, 0.0) + detail)
    return smooth, detail


def by_kind(lane, base, *values):
    kind = lax.rem(lane - base + KINDS * LANES, KINDS)
    result = values[0]
    for k, value in enumerate(values[1:], 1):
        result = jnp.where(kind == k, value, result)
    return result


def pieces(x, count):
    result = []
    for _ in range(count):
        result.append(x.astype(BF16).astype(F32))
        x = x - result[-1]
    return result


def first_kernel(layers, wave_hbm, k_hbm, observed_hbm, packet_ref, wave_ref, block_ref, observed_ref, tile, arrived):
    rows = k_hbm.shape[0]
    models = wave_ref.shape[0]
    loads = [
        pltpu.make_async_copy(source, target, arrived.at[i])
        for i, (source, target) in enumerate(
            ((wave_hbm, wave_ref), (k_hbm, block_ref.at[:rows]), (observed_hbm, observed_ref))
        )
    ]
    for load in loads:
        load.start()
    loads[0].wait()
    even, odd = inverse_wave(*stacked(wave_ref, layers), 0.0)
    model = unstacked(even, odd, models).astype(BF16)
    tile[...] = edge_tile(lambda l: layer_tiles(wave_ref, l), layers, rows)
    loads[1].wait()
    loads[2].wait()
    edges = edge_tile(lambda l: tuple(t[:rows].astype(F32) for t in layer_tiles(block_ref, l)), layers, rows)
    packet_ref[:rows, :] = edges.astype(BF16)
    tile[:, :rows] = nt_dot(model, block_ref[:rows, :])
    packet_ref[rows:, :] = jnp.concatenate(pieces(tile[...], 2), axis=0).astype(BF16)
    tile[...] = jnp.zeros_like(tile)
    tile[:, :rows] = observed_ref[...]
    below = pieces(tile[...], 3) + [jnp.zeros_like(tile)]
    below = [jnp.concatenate(below[i : i + 2], axis=0).astype(BF16) for i in (0, 2)]
    packed = [packet_ref[i : i + 2 * models, :] for i in range(0, packet_ref.shape[0], 2 * models)] + below
    for i, part in enumerate(packed):
        block_ref[rows:, i * LANES : (i + 1) * LANES] = part


def on_first_core():
    return lax.rem(lax.axis_index("dp"), 2) == 0


def applied_kernel(layers, rows, block_ref, other_ref, kw_ref):
    core = lax.rem(lax.axis_index("dp"), 2)
    kw_ref[2 * rows :, :] = jnp.zeros((kw_ref.shape[0] - 2 * rows, kw_ref.shape[1]), BF16)
    for which, source in ((core, block_ref), (1 - core, other_ref)):
        waves = forward_wave(*stacked(source.at[:rows], layers))
        kw_ref[pl.ds(pl.multiple_of(which * rows, 16), rows), :] = unstacked(*waves, rows).astype(BF16)


def transposing_kernel(rows, block_ref, other_ref, kt_ref):
    is_first = on_first_core()
    rest = jnp.zeros((LANES - 2 * rows, LANES), F32)
    for start in range(0, kt_ref.shape[0], LANES):
        mine, other = (ref[:rows, start : start + LANES].astype(F32) for ref in (block_ref, other_ref))
        both = [jnp.where(is_first, mine, other), jnp.where(is_first, other, mine), rest]
        kt_ref[start : start + LANES, :] = jnp.concatenate(both, axis=0).T.astype(BF16)


def spread_kernel(layers, base, threshold_ref, cut_ref, cut_halo_ref):
    models = cut_ref.shape[0]
    lane = lanes_of((models, LANES))
    halo = jnp.zeros((models, LANES), F32)
    for layer in range(layers):
        smooth, detail = (
            jnp.broadcast_to(threshold_ref[:, p, layer : layer + 1], (models, LANES)) for p in range(2)
        )
        start = 2 * LANES * layer
        cut_ref[:, start : start + LANES] = smooth
        cut_ref[:, start + LANES : start + 2 * LANES] = detail
        start = base + KINDS * layer
        here = (lane >= start) & (lane < start + KINDS)
        halo = jnp.where(here, jnp.where(lane == start + S_NEXT, smooth, detail), halo)
    cut_halo_ref[...] = halo


def second_kernel(layers, n_vox, models, *refs):
    (block_ref, *packets, out_ref, halo_ref, held) = refs
    rows = held.shape[1] - 2 * models
    me = lax.axis_index("vox")
    for distance, packet in enumerate(packets, 1):
        held[me ^ distance] = packet[...]
    chunks = held.shape[1] // (2 * models)
    below = [block_ref[rows:, i * LANES : (i + 1) * LANES] for i in range(chunks + 2)]
    for i in range(chunks):
        held[me, i * 2 * models : (i + 1) * 2 * models] = below[i]
    high, low = below[chunks].astype(F32), below[chunks + 1].astype(F32)
    observed = ((high[:models] + high[models:]) + low[:models])[:, :rows]
    left, right = lax.rem(me + n_vox - 1, n_vox), lax.rem(me + 1, n_vox)
    lane = lanes_of((models, LANES))
    inside = (lane >= rows) & (lane < rows + KINDS * layers)

    def edge_values(which):
        both = held[which, rows:, :].astype(F32)
        return both[:models] + both[models:]

    edge = [edge_values(z) for z in range(n_vox)]
    terms, columns = [], []
    for z in range(n_vox):
        before, after = edge[z - 1], edge[(z + 1) % n_vox]
        next_smooth = turned(after, O_LAST - E_FIRST)
        next_detail = turned(after, O_LAST - O_FIRST)
        next_even = next_smooth - 0.25 * (edge[z] + next_detail)
        term = by_kind(
            lane,
            rows,
            0.0,
            -0.25 * turned(before, E_FIRST - O_LAST),
            0.0,
            0.5 * next_even,
            -0.125 * turned(before, O_FIRST - O_LAST),
        )
        terms.append(jnp.where(inside, term, 0.0).astype(BF16))
        columns.append(held[z, :rows, :])
    predicted = nt_dot(jnp.concatenate(terms, axis=1), jnp.concatenate(columns, axis=1))
    shares = edge[0]
    for z in range(1, n_vox):
        shares = shares + edge[z]
    predicted = predicted + shares[:, :rows]

    before, own, after = (held[z, :rows, :].astype(F32) for z in (left, me, right))
    details = by_kind(
        lanes_of(own.shape),
        rows,
        0.0,
        0.0,
        0.0,
        own - 0.5 * (turned(own, O_LAST - E_LAST) + turned(after, O_LAST - E_FIRST)),
        after - 0.5 * (turned(after, O_FIRST - E_FIRST) + turned(after, O_FIRST - E_SECOND)),
    )
    out_ref[:rows, :] = by_kind(
        lanes_of(own.shape),
        rows,
        turned(after, E_NEXT - E_FIRST),
        turned(before, D_BEFORE - O_LAST) - 0.5 * (turned(before, D_BEFORE - E_LAST) + own),
        turned(after, S_NEXT - E_FIRST) + 0.25 * (turned(details, S_NEXT - D_LAST) + turned(details, S_NEXT - D_NEXT)),
        details,
        details,
    )
    out_ref[rows:, :] = jnp.zeros((2 * models, LANES), F32)
    out_ref[rows : rows + models, :rows] = observed - predicted
    out_ref[rows + models :, :rows] = observed
    before, own, after = (edge_values(z) for z in (left, me, right))
    halo_ref[...] = by_kind(
        lane, rows, 0.0, turned(before, D_BEFORE - O_LAST), turned(after, S_NEXT - E_FIRST), own, after
    )


def back_projected(residual, kw_ref, columns, g_ref):
    width = kw_ref.shape[1]
    sent = residual.astype(BF16)
    g_ref[:, :width] = jnp.dot(sent, kw_ref[...], preferred_element_type=F32).astype(BF16)
    g_ref[:, width:] = jnp.dot(sent, columns, preferred_element_type=F32).astype(BF16)


def third_kernel(mine_ref, other_ref, kw_ref, g_ref, columns_ref, observed_ref):
    models = g_ref.shape[0]
    rows = mine_ref.shape[0] - 2 * models
    is_first = on_first_core()
    mine, other = mine_ref[...], other_ref[...]
    first, second = jnp.where(is_first, mine, other), jnp.where(is_first, other, mine)
    rest = jnp.zeros((LANES - 2 * rows, LANES), F32)
    columns = jnp.concatenate([first[:rows], second[:rows], rest], axis=0).astype(BF16)
    columns_ref[...] = columns
    below = first[rows:] + turned(second[rows:], rows)
    observed_ref[...] = below[models:]
    back_projected(below[:models], kw_ref, columns, g_ref)


def added(shares, swapped=False):
    if len(shares) < 4:
        return sum(shares[1:], shares[0])
    own, near, middle, far = shares
    if swapped:
        is_first = on_first_core()
        near, middle = jnp.where(is_first, near, middle), jnp.where(is_first, middle, near)
    return (own + near) + (middle + far)


def at_ends(tile, layers, base):
    return jnp.concatenate([turned(tile, -(base + KINDS * layer + 1)) for layer in range(layers)], axis=0)


def halo_gradient(g_refs):
    return added([g[:, g.shape[1] - LANES :].astype(F32) for g in g_refs], True)


def stepped(layers, base, wave_ref, cut_ref, g_refs, edge):
    gradients = [stacked(g, layers) for g in g_refs]
    smooth_g, detail_g = (added([g[p] for g in gradients], True) for p in range(2))
    ends = at_ends(edge, layers, base)
    lane = lanes_of(ends.shape)
    smooth_g += jnp.where(lane == 0, 0.25 * ends, jnp.where(lane == LANES - 1, -0.125 * ends, 0.0))
    detail_g += jnp.where(lane == LANES - 1, -0.5 * ends, 0.0)
    return tuple(
        shrink(w + step_size * g, cut)
        for w, g, cut in zip(stacked(wave_ref, layers), (smooth_g, detail_g), stacked(cut_ref, layers))
    )


def fourth_kernel(layers, base, wave_ref, cut_ref, halo_ref, cut_halo_ref, kt_ref, *refs):
    *g_refs, new_ref, pred_ref = refs
    models = wave_ref.shape[0]
    edge = halo_gradient(g_refs)
    smooth, detail = stepped(layers, base, wave_ref, cut_ref, g_refs, edge)
    new_ref[...] = unstacked(smooth, detail, models)
    halo = shrink(halo_ref[...] + step_size * edge, cut_halo_ref[...])
    next_even = turned(halo, E_NEXT - S_NEXT) - 0.25 * (turned(halo, E_NEXT - D_LAST) + turned(halo, E_NEXT - D_NEXT))
    ends = at_ends(by_kind(lanes_of(halo.shape), base, next_even, halo), layers, base)
    model = unstacked(*inverse_wave(smooth, detail, ends), models).astype(BF16)
    pred_ref[...] = jnp.dot(model, kt_ref[...], preferred_element_type=F32)


def fifth_kernel(kw_ref, columns_ref, observed_ref, *refs):
    *shares, g_ref, residual_ref = refs
    rows = residual_ref.shape[1]
    residual = observed_ref[...] - added([s[...] for s in shares])
    back_projected(residual, kw_ref, columns_ref[...], g_ref)
    residual_ref[...] = jnp.where(on_first_core(), residual, turned(residual, -rows))[:, :rows]


def sixth_kernel(layers, base, wave_ref, cut_ref, *refs):
    *g_refs, new_ref = refs
    waves = stepped(layers, base, wave_ref, cut_ref, g_refs, halo_gradient(g_refs))
    new_ref[...] = unstacked(*waves, wave_ref.shape[0])


def from_partner(x, axis, distance):
    return lax.ppermute(x, axis, [(i, i ^ distance) for i in range(lax.axis_size(axis))])


def from_other_core(x, *steps):
    n_vox = lax.axis_size("vox")
    route = []
    for d in range(lax.axis_size("dp")):
        chips, vox = steps[(d + 1) % 2 % len(steps)]
        route += [(d * n_vox + z, (d ^ (2 * chips + 1)) * n_vox + (z ^ vox)) for z in range(n_vox)]
    return lax.ppermute(x, ("dp", "vox"), route)


def all_shares(x, step):
    return [x] + [from_other_core(x, step(n)) for n in (1, 2, 3)]


def swapped_shares(x, step):
    fetched = from_other_core(x, step(1), step(2))
    return [x, fetched, from_partner(fetched, "dp", 1), from_other_core(x, step(3))]


def shares_over(x, size, step, four, **how):
    lowest = 1
    while size > 4:
        x = added([s.astype(F32) for s in four(x, lambda n: step(lowest * n))], **how).astype(x.dtype)
        lowest, size = lowest * 4, size // 4
    if size == 4:
        return four(x, lambda n: step(lowest * n))
    return [x] + [from_other_core(x, step(lowest))] * (size - 1)


def over_chips(x):
    return shares_over(x, lax.axis_size("dp") // 2, lambda n: (n, 0), swapped_shares, swapped=True)


def over_vox(x):
    return shares_over(x, lax.axis_size("vox"), lambda n: (0, n), all_shares)


def call(kernel, out_shape, *args, scratch=(), space=pltpu.VMEM):
    return pl.pallas_call(
        kernel,
        out_shape=out_shape,
        in_specs=[pl.BlockSpec(memory_space=space)] * len(args),
        out_specs=jax.tree.map(lambda _: pl.BlockSpec(memory_space=pltpu.VMEM), out_shape),
        scratch_shapes=list(scratch),
        compiler_params=pltpu.CompilerParams(vmem_limit_bytes=KERNEL_BYTES),
    )(*[pltpu.with_memory_space_constraint(arg, space) for arg in args])


def body(kernels, observed, initial, threshold):
    models, width = initial.shape
    rows = kernels.shape[0]
    layers = threshold.shape[1]
    n_vox = lax.axis_size("vox")
    packet_rows = rows + 2 * models
    assert width == 2 * layers * LANES and rows + KINDS * layers <= LANES and 2 * rows <= LANES
    assert packet_rows % (2 * models) == 0 and packet_rows // (2 * models) + 2 <= 2 * layers
    g_shape = pltpu.VMEM((models, width + LANES), BF16)
    tile_shape = pltpu.VMEM((models, LANES), F32)

    packet, wavelets, block = call(
        functools.partial(first_kernel, layers),
        (
            pltpu.VMEM((packet_rows, LANES), BF16),
            pltpu.VMEM((models, width), F32),
            pltpu.VMEM((rows + 2 * models, width), BF16),
        ),
        initial,
        kernels,
        observed,
        scratch=[
            pltpu.VMEM((models, rows), F32),
            pltpu.VMEM((models, LANES), F32),
            pltpu.SemaphoreType.DMA((3,)),
        ],
        space=pltpu.HBM,
    )
    block_other = from_partner(block, "dp", 1)
    packets = [from_other_core(packet, (0, d)) for d in range(1, n_vox)]
    kw = call(functools.partial(applied_kernel, layers, rows), pltpu.VMEM((LANES, width), BF16), block, block_other)
    kt = call(functools.partial(transposing_kernel, rows), pltpu.VMEM((width, LANES), BF16), block, block_other)
    cut, cut_halo = call(
        functools.partial(spread_kernel, layers, rows),
        (pltpu.VMEM((models, width), F32), tile_shape),
        jnp.swapaxes(threshold, 1, 2),
    )
    other, halo = call(
        functools.partial(second_kernel, layers, n_vox, models),
        (pltpu.VMEM((packet_rows, LANES), F32), tile_shape),
        block_other,
        *packets,
        scratch=[pltpu.VMEM((n_vox, packet_rows, LANES), BF16)],
    )
    mine = from_partner(other, "dp", 1)
    g, columns, observed = call(
        third_kernel, (g_shape, pltpu.VMEM((LANES, LANES), BF16), tile_shape), mine, other, kw
    )
    wavelets, predicted = call(
        functools.partial(fourth_kernel, layers, rows),
        (pltpu.VMEM((models, width), F32), tile_shape),
        wavelets,
        cut,
        halo,
        cut_halo,
        kt,
        *over_chips(g),
    )
    g, residual = call(
        fifth_kernel,
        (g_shape, pltpu.VMEM((models, rows), F32)),
        kw,
        columns,
        observed,
        *over_vox(predicted),
    )
    coefficients = call(
        functools.partial(sixth_kernel, layers, rows),
        jax.ShapeDtypeStruct((models, width), F32),
        wavelets,
        cut,
        *over_chips(g),
    )
    return coefficients, residual


def solution(mesh):
    return jax.shard_map(
        body,
        mesh=mesh,
        in_specs=(P("dp", "vox"), P(None, "dp"), P(None, "vox"), P()),
        out_specs=(P(None, "vox"), P(None, "dp")),
        check_vma=False,
    )
```

```python
import functools

import jax
import jax.numpy as jnp
from jax import lax
from jax.experimental import pallas as pl
from jax.experimental.pallas import tpu as pltpu
from jax.sharding import PartitionSpec as P

step_size = 0.5
LANES = 128
KERNEL_BYTES = 8 * 2**20
F32 = jnp.float32
BF16 = jnp.bfloat16

E_LAST, E_FIRST, E_SECOND, O_LAST, O_FIRST = range(5)
E_NEXT, D_BEFORE, S_NEXT, D_LAST, D_NEXT = range(5)
KINDS = 5


def lanes_of(shape):
    return lax.broadcasted_iota(jnp.int32, shape, len(shape) - 1)


def turned(x, by):
    return pltpu.roll(x, by % LANES, x.ndim - 1)


def shifted_in(x, by, edge):
    free = 0 if by == 1 else LANES - 1
    return jnp.where(lanes_of(x.shape) == free, edge, turned(x, by))


def edge_tile(pair_of, layers, base):
    tile = None
    for layer in range(layers):
        even, odd = pair_of(layer)
        start = base + KINDS * layer
        lane = lanes_of(even.shape)
        if tile is None:
            tile = jnp.zeros_like(even)
        tile = jnp.where((lane >= start) & (lane < start + 3), turned(even, start + 1), tile)
        tile = jnp.where((lane >= start + 3) & (lane < start + 5), turned(odd, start + 4), tile)
    return tile


def kind_lane(lane, base, kind):
    return lax.rem(lane - base + KINDS * LANES, KINDS) == kind


def shrink(values, cutoff):
    return values - jnp.clip(values, -cutoff, cutoff)


def layer_tiles(ref, layer):
    start = layer * 2 * LANES
    return ref[:, start : start + LANES], ref[:, start + LANES : start + 2 * LANES]


def stacked(ref, layers):
    tiles = [layer_tiles(ref, layer) for layer in range(layers)]
    return tuple(jnp.concatenate([t[p] for t in tiles], axis=0).astype(F32) for p in range(2))


def unstacked(even, odd, models):
    rows = [slice(start, start + models) for start in range(0, even.shape[0], models)]
    return jnp.concatenate([t[r] for r in rows for t in (even, odd)], axis=1)


def nt_dot(a, b):
    return lax.dot_general(a, b, (((1,), (1,)), ((), ())), preferred_element_type=F32)


def inverse_wave(smooth, detail, edge):
    even = smooth - 0.25 * (shifted_in(detail, 1, edge) + detail)
    odd = detail + 0.5 * (even + shifted_in(even, -1, edge))
    return even, odd


def forward_wave(even, odd):
    detail = odd - 0.5 * (even + shifted_in(even, -1, 0.0))
    smooth = even + 0.25 * (shifted_in(detail, 1, 0.0) + detail)
    return smooth, detail


def by_kind(lane, base, *values):
    kind = lax.rem(lane - base + KINDS * LANES, KINDS)
    result = values[0]
    for k, value in enumerate(values[1:], 1):
        result = jnp.where(kind == k, value, result)
    return result


def pieces(x, count):
    result = []
    for _ in range(count):
        result.append(x.astype(BF16).astype(F32))
        x = x - result[-1]
    return result


def first_kernel(layers, wave_hbm, k_hbm, observed_hbm, packet_ref, wave_ref, block_ref, observed_ref, tile, arrived):
    rows = k_hbm.shape[0]
    models = wave_ref.shape[0]
    loads = [
        pltpu.make_async_copy(source, target, arrived.at[i])
        for i, (source, target) in enumerate(
            ((wave_hbm, wave_ref), (k_hbm, block_ref.at[:rows]), (observed_hbm, observed_ref))
        )
    ]
    for load in loads:
        load.start()
    loads[0].wait()
    even, odd = inverse_wave(*stacked(wave_ref, layers), 0.0)
    model = unstacked(even, odd, models).astype(BF16)
    tile[...] = edge_tile(lambda l: layer_tiles(wave_ref, l), layers, rows)
    loads[1].wait()
    loads[2].wait()
    edges = edge_tile(lambda l: tuple(t[:rows].astype(F32) for t in layer_tiles(block_ref, l)), layers, rows)
    packet_ref[:rows, :] = edges.astype(BF16)
    tile[:, :rows] = nt_dot(model, block_ref[:rows, :])
    packet_ref[rows:, :] = jnp.concatenate(pieces(tile[...], 2), axis=0).astype(BF16)
    tile[...] = jnp.zeros_like(tile)
    tile[:, :rows] = observed_ref[...]
    below = pieces(tile[...], 3) + [jnp.zeros_like(tile)]
    below = [jnp.concatenate(below[i : i + 2], axis=0).astype(BF16) for i in (0, 2)]
    packed = [packet_ref[i : i + 2 * models, :] for i in range(0, packet_ref.shape[0], 2 * models)] + below
    for i, part in enumerate(packed):
        block_ref[rows:, i * LANES : (i + 1) * LANES] = part


def on_first_core():
    return lax.rem(lax.axis_index("dp"), 2) == 0


def applied_kernel(layers, rows, block_ref, other_ref, kw_ref):
    core = lax.rem(lax.axis_index("dp"), 2)
    kw_ref[2 * rows :, :] = jnp.zeros((kw_ref.shape[0] - 2 * rows, kw_ref.shape[1]), BF16)
    for which, source in ((core, block_ref), (1 - core, other_ref)):
        waves = forward_wave(*stacked(source.at[:rows], layers))
        kw_ref[pl.ds(pl.multiple_of(which * rows, 16), rows), :] = unstacked(*waves, rows).astype(BF16)


def transposing_kernel(rows, block_ref, other_ref, kt_ref):
    is_first = on_first_core()
    rest = jnp.zeros((LANES - 2 * rows, LANES), F32)
    for start in range(0, kt_ref.shape[0], LANES):
        mine, other = (ref[:rows, start : start + LANES].astype(F32) for ref in (block_ref, other_ref))
        both = [jnp.where(is_first, mine, other), jnp.where(is_first, other, mine), rest]
        kt_ref[start : start + LANES, :] = jnp.concatenate(both, axis=0).T.astype(BF16)


def spread_kernel(layers, base, threshold_ref, cut_ref, cut_halo_ref):
    models = cut_ref.shape[0]
    lane = lanes_of((models, LANES))
    halo = jnp.zeros((models, LANES), F32)
    for layer in range(layers):
        smooth, detail = (
            jnp.broadcast_to(threshold_ref[:, p, layer : layer + 1], (models, LANES)) for p in range(2)
        )
        start = 2 * LANES * layer
        cut_ref[:, start : start + LANES] = smooth
        cut_ref[:, start + LANES : start + 2 * LANES] = detail
        start = base + KINDS * layer
        here = (lane >= start) & (lane < start + KINDS)
        halo = jnp.where(here, jnp.where(lane == start + S_NEXT, smooth, detail), halo)
    cut_halo_ref[...] = halo


def second_kernel(layers, n_vox, models, *refs):
    (block_ref, *packets, out_ref, halo_ref, held) = refs
    rows = held.shape[1] - 2 * models
    me = lax.axis_index("vox")
    for distance, packet in enumerate(packets, 1):
        held[me ^ distance] = packet[...]
    chunks = held.shape[1] // (2 * models)
    below = [block_ref[rows:, i * LANES : (i + 1) * LANES] for i in range(chunks + 2)]
    for i in range(chunks):
        held[me, i * 2 * models : (i + 1) * 2 * models] = below[i]
    high, low = below[chunks].astype(F32), below[chunks + 1].astype(F32)
    observed = ((high[:models] + high[models:]) + low[:models])[:, :rows]
    left, right = lax.rem(me + n_vox - 1, n_vox), lax.rem(me + 1, n_vox)
    lane = lanes_of((models, LANES))
    inside = (lane >= rows) & (lane < rows + KINDS * layers)

    def edge_values(which):
        both = held[which, rows:, :].astype(F32)
        return both[:models] + both[models:]

    edge = [edge_values(z) for z in range(n_vox)]
    terms, columns = [], []
    for z in range(n_vox):
        before, after = edge[z - 1], edge[(z + 1) % n_vox]
        next_smooth = turned(after, O_LAST - E_FIRST)
        next_detail = turned(after, O_LAST - O_FIRST)
        next_even = next_smooth - 0.25 * (edge[z] + next_detail)
        term = by_kind(
            lane,
            rows,
            0.0,
            -0.25 * turned(before, E_FIRST - O_LAST),
            0.0,
            0.5 * next_even,
            -0.125 * turned(before, O_FIRST - O_LAST),
        )
        terms.append(jnp.where(inside, term, 0.0).astype(BF16))
        columns.append(held[z, :rows, :])
    predicted = nt_dot(jnp.concatenate(terms, axis=1), jnp.concatenate(columns, axis=1))
    shares = edge[0]
    for z in range(1, n_vox):
        shares = shares + edge[z]
    predicted = predicted + shares[:, :rows]

    before, own, after = (held[z, :rows, :].astype(F32) for z in (left, me, right))
    details = by_kind(
        lanes_of(own.shape),
        rows,
        0.0,
        0.0,
        0.0,
        own - 0.5 * (turned(own, O_LAST - E_LAST) + turned(after, O_LAST - E_FIRST)),
        after - 0.5 * (turned(after, O_FIRST - E_FIRST) + turned(after, O_FIRST - E_SECOND)),
    )
    out_ref[:rows, :] = by_kind(
        lanes_of(own.shape),
        rows,
        turned(after, E_NEXT - E_FIRST),
        turned(before, D_BEFORE - O_LAST) - 0.5 * (turned(before, D_BEFORE - E_LAST) + own),
        turned(after, S_NEXT - E_FIRST) + 0.25 * (turned(details, S_NEXT - D_LAST) + turned(details, S_NEXT - D_NEXT)),
        details,
        details,
    )
    out_ref[rows:, :] = jnp.zeros((2 * models, LANES), F32)
    out_ref[rows : rows + models, :rows] = observed - predicted
    out_ref[rows + models :, :rows] = observed
    before, own, after = (edge_values(z) for z in (left, me, right))
    halo_ref[...] = by_kind(
        lane, rows, 0.0, turned(before, D_BEFORE - O_LAST), turned(after, S_NEXT - E_FIRST), own, after
    )


def back_projected(residual, kw_ref, columns, g_ref):
    width = kw_ref.shape[1]
    sent = residual.astype(BF16)
    g_ref[:, :width] = jnp.dot(sent, kw_ref[...], preferred_element_type=F32).astype(BF16)
    g_ref[:, width:] = jnp.dot(sent, columns, preferred_element_type=F32).astype(BF16)


def third_kernel(mine_ref, other_ref, kw_ref, g_ref, columns_ref, observed_ref):
    models = g_ref.shape[0]
    rows = mine_ref.shape[0] - 2 * models
    is_first = on_first_core()
    mine, other = mine_ref[...], other_ref[...]
    first, second = jnp.where(is_first, mine, other), jnp.where(is_first, other, mine)
    rest = jnp.zeros((LANES - 2 * rows, LANES), F32)
    columns = jnp.concatenate([first[:rows], second[:rows], rest], axis=0).astype(BF16)
    columns_ref[...] = columns
    below = first[rows:] + turned(second[rows:], rows)
    observed_ref[...] = below[models:]
    back_projected(below[:models], kw_ref, columns, g_ref)


def added(shares):
    while len(shares) > 1:
        shares = [a + b for a, b in zip(shares[::2], shares[1::2])]
    return shares[0]


def at_ends(tile, layers, base):
    return jnp.concatenate([turned(tile, -(base + KINDS * layer + 1)) for layer in range(layers)], axis=0)


def halo_gradient(g_refs):
    return added([g[:, g.shape[1] - LANES :].astype(F32) for g in g_refs])


def stepped(layers, base, wave_ref, cut_ref, g_refs, edge):
    gradients = [stacked(g, layers) for g in g_refs]
    smooth_g, detail_g = (added([g[p] for g in gradients]) for p in range(2))
    ends = at_ends(edge, layers, base)
    lane = lanes_of(ends.shape)
    smooth_g += jnp.where(lane == 0, 0.25 * ends, jnp.where(lane == LANES - 1, -0.125 * ends, 0.0))
    detail_g += jnp.where(lane == LANES - 1, -0.5 * ends, 0.0)
    return tuple(
        shrink(w + step_size * g, cut)
        for w, g, cut in zip(stacked(wave_ref, layers), (smooth_g, detail_g), stacked(cut_ref, layers))
    )


def fourth_kernel(layers, base, wave_ref, cut_ref, halo_ref, cut_halo_ref, kt_ref, *refs):
    *g_refs, new_ref, pred_ref = refs
    models = wave_ref.shape[0]
    edge = halo_gradient(g_refs)
    smooth, detail = stepped(layers, base, wave_ref, cut_ref, g_refs, edge)
    new_ref[...] = unstacked(smooth, detail, models)
    halo = shrink(halo_ref[...] + step_size * edge, cut_halo_ref[...])
    next_even = turned(halo, E_NEXT - S_NEXT) - 0.25 * (turned(halo, E_NEXT - D_LAST) + turned(halo, E_NEXT - D_NEXT))
    ends = at_ends(by_kind(lanes_of(halo.shape), base, next_even, halo), layers, base)
    model = unstacked(*inverse_wave(smooth, detail, ends), models).astype(BF16)
    pred_ref[...] = jnp.dot(model, kt_ref[...], preferred_element_type=F32)


def fifth_kernel(kw_ref, columns_ref, observed_ref, *refs):
    *shares, g_ref, residual_ref = refs
    residual = observed_ref[...] - added([s[...] for s in shares])
    back_projected(residual, kw_ref, columns_ref[...], g_ref)
    residual_ref[...] = residual


def sixth_kernel(layers, base, wave_ref, cut_ref, *refs):
    *g_refs, new_ref = refs
    waves = stepped(layers, base, wave_ref, cut_ref, g_refs, halo_gradient(g_refs))
    new_ref[...] = unstacked(*waves, wave_ref.shape[0])


def seventh_kernel(wave_ref, other_wave_ref, residual_ref, other_residual_ref, out_ref, own_ref):
    rows = own_ref.shape[1]
    is_first = on_first_core()
    out_ref[...] = jnp.where(is_first, other_wave_ref[...], wave_ref[...])
    own_ref[...] = jnp.where(is_first, residual_ref[...], turned(other_residual_ref[...], -rows))[:, :rows]


def from_partner(x, axis, distance):
    return lax.ppermute(x, axis, [(i, i ^ distance) for i in range(lax.axis_size(axis))])


def from_other_core(x, vox):
    n_vox = lax.axis_size("vox")
    places = [(d, z) for d in range(lax.axis_size("dp")) for z in range(n_vox)]
    return lax.ppermute(x, ("dp", "vox"), [(d * n_vox + z, (d ^ 1) * n_vox + (z ^ vox)) for d, z in places])


def from_same_core(x, chips, vox):
    n_vox = lax.axis_size("vox")
    places = [(d, z) for d in range(lax.axis_size("dp")) for z in range(n_vox)]
    return lax.ppermute(x, ("dp", "vox"), [(d * n_vox + z, (d ^ (2 * chips)) * n_vox + (z ^ vox)) for d, z in places])


def handed_over(x, sender, chips, vox):
    n_vox = lax.axis_size("vox")
    route = []
    for d in range(lax.axis_size("dp")):
        away = (chips, vox) if d % 2 == sender else (0, 0)
        route += [(d * n_vox + z, (d ^ 1 ^ (2 * away[0])) * n_vox + (z ^ away[1])) for z in range(n_vox)]
    return lax.ppermute(x, ("dp", "vox"), route)


def shares_over(x, size, step, sender):
    lowest = 1
    while size > 4:
        fours = [x] + [from_same_core(x, *step(lowest * n)) for n in (1, 2, 3)]
        x = added([f.astype(F32) for f in fours]).astype(x.dtype)
        lowest, size = lowest * 4, size // 4
    return [handed_over(x, sender, *step(lowest * n)) for n in range(size)]


def over_chips(x):
    return shares_over(x, lax.axis_size("dp") // 2, lambda n: (n, 0), 0)


def over_vox(x):
    return shares_over(x, lax.axis_size("vox"), lambda n: (0, n), 1)


def call(kernel, out_shape, *args, scratch=(), space=pltpu.VMEM):
    return pl.pallas_call(
        kernel,
        out_shape=out_shape,
        in_specs=[pl.BlockSpec(memory_space=space)] * len(args),
        out_specs=jax.tree.map(lambda _: pl.BlockSpec(memory_space=pltpu.VMEM), out_shape),
        scratch_shapes=list(scratch),
        compiler_params=pltpu.CompilerParams(vmem_limit_bytes=KERNEL_BYTES),
    )(*[pltpu.with_memory_space_constraint(arg, space) for arg in args])


def body(kernels, observed, initial, threshold):
    models, width = initial.shape
    rows = kernels.shape[0]
    layers = threshold.shape[1]
    n_vox = lax.axis_size("vox")
    packet_rows = rows + 2 * models
    assert width == 2 * layers * LANES and rows + KINDS * layers <= LANES and 2 * rows <= LANES
    assert packet_rows % (2 * models) == 0 and packet_rows // (2 * models) + 2 <= 2 * layers
    g_shape = pltpu.VMEM((models, width + LANES), BF16)
    tile_shape = pltpu.VMEM((models, LANES), F32)

    packet, wavelets, block = call(
        functools.partial(first_kernel, layers),
        (
            pltpu.VMEM((packet_rows, LANES), BF16),
            pltpu.VMEM((models, width), F32),
            pltpu.VMEM((rows + 2 * models, width), BF16),
        ),
        initial,
        kernels,
        observed,
        scratch=[
            pltpu.VMEM((models, rows), F32),
            pltpu.VMEM((models, LANES), F32),
            pltpu.SemaphoreType.DMA((3,)),
        ],
        space=pltpu.HBM,
    )
    block_other = from_partner(block, "dp", 1)
    packets = [from_other_core(packet, d) for d in range(1, n_vox)]
    kw = call(functools.partial(applied_kernel, layers, rows), pltpu.VMEM((LANES, width), BF16), block, block_other)
    kt = call(functools.partial(transposing_kernel, rows), pltpu.VMEM((width, LANES), BF16), block, block_other)
    cut, cut_halo = call(
        functools.partial(spread_kernel, layers, rows),
        (pltpu.VMEM((models, width), F32), tile_shape),
        jnp.swapaxes(threshold, 1, 2),
    )
    other, halo = call(
        functools.partial(second_kernel, layers, n_vox, models),
        (pltpu.VMEM((packet_rows, LANES), F32), tile_shape),
        block_other,
        *packets,
        scratch=[pltpu.VMEM((n_vox, packet_rows, LANES), BF16)],
    )
    mine = from_partner(other, "dp", 1)
    g, columns, observed = call(
        third_kernel, (g_shape, pltpu.VMEM((LANES, LANES), BF16), tile_shape), mine, other, kw
    )
    wavelets, predicted = call(
        functools.partial(fourth_kernel, layers, rows),
        (pltpu.VMEM((models, width), F32), tile_shape),
        wavelets,
        cut,
        halo,
        cut_halo,
        kt,
        *over_chips(g),
    )
    g, residual = call(fifth_kernel, (g_shape, tile_shape), kw, columns, observed, *over_vox(predicted))
    coefficients = call(
        functools.partial(sixth_kernel, layers, rows),
        pltpu.VMEM((models, width), F32),
        wavelets,
        cut,
        *over_chips(g),
    )
    return call(
        seventh_kernel,
        (jax.ShapeDtypeStruct((models, width), F32), jax.ShapeDtypeStruct((models, rows), F32)),
        coefficients,
        from_partner(coefficients, "dp", 1),
        residual,
        from_partner(residual, "dp", 1),
    )


def solution(mesh):
    return jax.shard_map(
        body,
        mesh=mesh,
        in_specs=(P("dp", "vox"), P(None, "dp"), P(None, "vox"), P()),
        out_specs=(P(None, "vox"), P(None, "dp")),
        check_vma=False,
    )
```

```python
import functools

import jax
import jax.numpy as jnp
from jax import lax
from jax.experimental import pallas as pl
from jax.experimental.pallas import tpu as pltpu
from jax.sharding import PartitionSpec as P

step_size = 0.5
LANES = 128
KERNEL_BYTES = 8 * 2**20
F32 = jnp.float32
BF16 = jnp.bfloat16

E_LAST, E_FIRST, E_SECOND, O_LAST, O_FIRST = range(5)
E_NEXT, D_BEFORE, S_NEXT, D_LAST, D_NEXT = range(5)
KINDS = 5


def lanes_of(shape):
    return lax.broadcasted_iota(jnp.int32, shape, len(shape) - 1)


def turned(x, by):
    return pltpu.roll(x, by % LANES, x.ndim - 1)


def shifted_in(x, by, edge):
    free = 0 if by == 1 else LANES - 1
    return jnp.where(lanes_of(x.shape) == free, edge, turned(x, by))


def edge_tile(pair_of, layers, base):
    tile = None
    for layer in range(layers):
        even, odd = pair_of(layer)
        start = base + KINDS * layer
        lane = lanes_of(even.shape)
        if tile is None:
            tile = jnp.zeros_like(even)
        tile = jnp.where((lane >= start) & (lane < start + 3), turned(even, start + 1), tile)
        tile = jnp.where((lane >= start + 3) & (lane < start + 5), turned(odd, start + 4), tile)
    return tile


def kind_lane(lane, base, kind):
    return lax.rem(lane - base + KINDS * LANES, KINDS) == kind


def shrink(values, cutoff):
    return values - jnp.clip(values, -cutoff, cutoff)


def layer_tiles(ref, layer):
    start = layer * 2 * LANES
    return ref[:, start : start + LANES], ref[:, start + LANES : start + 2 * LANES]


def stacked(ref, layers):
    tiles = [layer_tiles(ref, layer) for layer in range(layers)]
    return tuple(jnp.concatenate([t[p] for t in tiles], axis=0).astype(F32) for p in range(2))


def unstacked(even, odd, models):
    rows = [slice(start, start + models) for start in range(0, even.shape[0], models)]
    return jnp.concatenate([t[r] for r in rows for t in (even, odd)], axis=1)


def nt_dot(a, b):
    return lax.dot_general(a, b, (((1,), (1,)), ((), ())), preferred_element_type=F32)


def inverse_wave(smooth, detail, edge):
    even = smooth - 0.25 * (shifted_in(detail, 1, edge) + detail)
    odd = detail + 0.5 * (even + shifted_in(even, -1, edge))
    return even, odd


def forward_wave(even, odd):
    detail = odd - 0.5 * (even + shifted_in(even, -1, 0.0))
    smooth = even + 0.25 * (shifted_in(detail, 1, 0.0) + detail)
    return smooth, detail


def by_kind(lane, base, *values):
    kind = lax.rem(lane - base + KINDS * LANES, KINDS)
    result = values[0]
    for k, value in enumerate(values[1:], 1):
        result = jnp.where(kind == k, value, result)
    return result


def pieces(x, count):
    result = []
    for _ in range(count):
        result.append(x.astype(BF16).astype(F32))
        x = x - result[-1]
    return result


def first_kernel(layers, wave_hbm, k_hbm, observed_hbm, packet_ref, wave_ref, k_ref, observed_ref, tile, arrived):
    rows = k_ref.shape[0]
    models = wave_ref.shape[0]
    loads = [
        pltpu.make_async_copy(source, target, arrived.at[i])
        for i, (source, target) in enumerate(
            ((wave_hbm, wave_ref), (k_hbm, k_ref), (observed_hbm, observed_ref))
        )
    ]
    for load in loads:
        load.start()
    loads[0].wait()
    even, odd = inverse_wave(*stacked(wave_ref, layers), 0.0)
    model = unstacked(even, odd, models).astype(BF16)
    tile[...] = edge_tile(lambda l: layer_tiles(wave_ref, l), layers, rows)
    loads[1].wait()
    loads[2].wait()
    edges = edge_tile(lambda l: tuple(t.astype(F32) for t in layer_tiles(k_ref, l)), layers, rows)
    packet_ref[:rows, :] = edges.astype(BF16)
    tile[:, :rows] = nt_dot(model, k_ref[...])
    parts = pieces(tile[...], 2)
    tile[...] = jnp.zeros_like(tile)
    tile[:, :rows] = observed_ref[...]
    parts += pieces(tile[...], 3) + [jnp.zeros_like(tile)]
    packet_ref[rows:, :] = jnp.concatenate(parts, axis=0).astype(BF16)


def joining_kernel(models, mine_ref, other_ref, k_in_ref, both_ref, observed_ref, k_ref):
    del k_in_ref, k_ref
    is_first = on_first_core()
    mine, other = mine_ref[...].astype(F32), other_ref[...].astype(F32)
    first, second = jnp.where(is_first, mine, other), jnp.where(is_first, other, mine)
    end = mine.shape[0] - 4 * models
    rows = end - 2 * models
    both_ref[...] = jnp.concatenate([first[:end], second[:end]], axis=0).astype(BF16)

    def observations(packet):
        high, middle, low = (packet[i : i + models] for i in range(end, end + 3 * models, models))
        return (high + middle) + low

    observed_ref[...] = observations(first) + turned(observations(second), rows)


def on_first_core():
    return lax.rem(lax.axis_index("dp"), 2) == 0


def applied_kernel(layers, k_ref, k_other_ref, kw_ref):
    core = lax.rem(lax.axis_index("dp"), 2)
    rows = k_ref.shape[0]
    kw_ref[2 * rows :, :] = jnp.zeros((kw_ref.shape[0] - 2 * rows, kw_ref.shape[1]), BF16)
    for which, source in ((core, k_ref), (1 - core, k_other_ref)):
        waves = forward_wave(*stacked(source, layers))
        kw_ref[pl.ds(pl.multiple_of(which * rows, 16), rows), :] = unstacked(*waves, rows).astype(BF16)


def transposing_kernel(k_ref, k_other_ref, kt_ref):
    is_first = on_first_core()
    rows = k_ref.shape[0]
    rest = jnp.zeros((LANES - 2 * rows, LANES), F32)
    for start in range(0, kt_ref.shape[0], LANES):
        mine, other = (ref[:, start : start + LANES].astype(F32) for ref in (k_ref, k_other_ref))
        both = [jnp.where(is_first, mine, other), jnp.where(is_first, other, mine), rest]
        kt_ref[start : start + LANES, :] = jnp.concatenate(both, axis=0).T.astype(BF16)


def spread_kernel(layers, base, threshold_ref, cut_ref, cut_halo_ref):
    models = cut_ref.shape[0]
    lane = lanes_of((models, LANES))
    halo = jnp.zeros((models, LANES), F32)
    for layer in range(layers):
        smooth, detail = (
            jnp.broadcast_to(threshold_ref[:, p, layer : layer + 1], (models, LANES)) for p in range(2)
        )
        start = 2 * LANES * layer
        cut_ref[:, start : start + LANES] = smooth
        cut_ref[:, start + LANES : start + 2 * LANES] = detail
        start = base + KINDS * layer
        here = (lane >= start) & (lane < start + KINDS)
        halo = jnp.where(here, jnp.where(lane == start + S_NEXT, smooth, detail), halo)
    cut_halo_ref[...] = halo


def back_projected(residual, kw_ref, columns, g_ref):
    width = kw_ref.shape[1]
    sent = residual.astype(BF16)
    g_ref[:, :width] = jnp.dot(sent, kw_ref[...], preferred_element_type=F32).astype(BF16)
    g_ref[:, width:] = jnp.dot(sent, columns, preferred_element_type=F32).astype(BF16)


def edge_terms(edge, base, layers):
    lane = lanes_of(edge[0].shape)
    inside = (lane >= base) & (lane < base + KINDS * layers)
    terms = []
    for z, own in enumerate(edge):
        before, after = edge[z - 1], edge[(z + 1) % len(edge)]
        next_smooth = turned(after, O_LAST - E_FIRST)
        next_detail = turned(after, O_LAST - O_FIRST)
        next_even = next_smooth - 0.25 * (own + next_detail)
        term = by_kind(
            lane,
            base,
            0.0,
            -0.25 * turned(before, E_FIRST - O_LAST),
            0.0,
            0.5 * next_even,
            -0.125 * turned(before, O_FIRST - O_LAST),
        )
        terms.append(jnp.where(inside, term, 0.0).astype(BF16))
    return jnp.concatenate(terms, axis=1)


def halo_columns(before, own, after, base):
    lane = lanes_of(own.shape)
    details = by_kind(
        lane,
        base,
        0.0,
        0.0,
        0.0,
        own - 0.5 * (turned(own, O_LAST - E_LAST) + turned(after, O_LAST - E_FIRST)),
        after - 0.5 * (turned(after, O_FIRST - E_FIRST) + turned(after, O_FIRST - E_SECOND)),
    )
    return by_kind(
        lane,
        base,
        turned(after, E_NEXT - E_FIRST),
        turned(before, D_BEFORE - O_LAST) - 0.5 * (turned(before, D_BEFORE - E_LAST) + own),
        turned(after, S_NEXT - E_FIRST) + 0.25 * (turned(details, S_NEXT - D_LAST) + turned(details, S_NEXT - D_NEXT)),
        details,
        details,
    )


def second_kernel(layers, n_vox, observed_ref, kw_ref, *refs):
    (*packets, g_ref, columns_ref, halo_ref, held, tile) = refs
    models = observed_ref.shape[0]
    size = held.shape[1] // 2
    rows = size - 2 * models
    me = lax.axis_index("vox")
    for distance, packet in enumerate(reversed(packets)):
        held[me ^ distance] = packet[...]
    left, right = lax.rem(me + n_vox - 1, n_vox), lax.rem(me + 1, n_vox)
    lane = lanes_of((models, LANES))

    def values(which, core):
        both = held[which, core * size + rows : (core + 1) * size, :].astype(F32)
        return both[:models] + both[models:]

    terms = edge_terms([values(z, 0) for z in range(n_vox)], rows, layers)
    columns = []
    tile[...] = jnp.zeros_like(tile)
    for core in range(2):
        edges = jnp.concatenate([held[z, core * size : core * size + rows, :] for z in range(n_vox)], axis=1)
        shares = values(0, core)
        for z in range(1, n_vox):
            shares = shares + values(z, core)
        tile[:, core * rows : (core + 1) * rows] = nt_dot(terms, edges) + shares[:, :rows]
        around = [held[z, core * size : core * size + rows, :].astype(F32) for z in (left, me, right)]
        columns.append(halo_columns(*around, rows))
    columns.append(jnp.zeros((LANES - 2 * rows, LANES), F32))
    columns = jnp.concatenate(columns, axis=0).astype(BF16)
    columns_ref[...] = columns
    back_projected(observed_ref[...] - tile[...], kw_ref, columns, g_ref)
    before, own, after = (values(z, 0) for z in (left, me, right))
    halo_ref[...] = by_kind(
        lane, rows, 0.0, turned(before, D_BEFORE - O_LAST), turned(after, S_NEXT - E_FIRST), own, after
    )


def added(shares):
    while len(shares) > 1:
        shares = [a + b for a, b in zip(shares[::2], shares[1::2])]
    return shares[0]


def at_ends(tile, layers, base):
    return jnp.concatenate([turned(tile, -(base + KINDS * layer + 1)) for layer in range(layers)], axis=0)


def halo_gradient(g_refs):
    return added([g[:, g.shape[1] - LANES :].astype(F32) for g in g_refs])


def stepped(layers, base, wave_ref, cut_ref, g_refs, edge):
    gradients = [stacked(g, layers) for g in g_refs]
    smooth_g, detail_g = (added([g[p] for g in gradients]) for p in range(2))
    ends = at_ends(edge, layers, base)
    lane = lanes_of(ends.shape)
    smooth_g += jnp.where(lane == 0, 0.25 * ends, jnp.where(lane == LANES - 1, -0.125 * ends, 0.0))
    detail_g += jnp.where(lane == LANES - 1, -0.5 * ends, 0.0)
    return tuple(
        shrink(w + step_size * g, cut)
        for w, g, cut in zip(stacked(wave_ref, layers), (smooth_g, detail_g), stacked(cut_ref, layers))
    )


def fourth_kernel(layers, base, wave_ref, cut_ref, halo_ref, cut_halo_ref, kt_ref, *refs):
    *g_refs, new_ref, pred_ref = refs
    models = wave_ref.shape[0]
    edge = halo_gradient(g_refs)
    smooth, detail = stepped(layers, base, wave_ref, cut_ref, g_refs, edge)
    new_ref[...] = unstacked(smooth, detail, models)
    halo = shrink(halo_ref[...] + step_size * edge, cut_halo_ref[...])
    next_even = turned(halo, E_NEXT - S_NEXT) - 0.25 * (turned(halo, E_NEXT - D_LAST) + turned(halo, E_NEXT - D_NEXT))
    ends = at_ends(by_kind(lanes_of(halo.shape), base, next_even, halo), layers, base)
    model = unstacked(*inverse_wave(smooth, detail, ends), models).astype(BF16)
    pred_ref[...] = jnp.dot(model, kt_ref[...], preferred_element_type=F32)


def fifth_kernel(kw_ref, columns_ref, observed_ref, *refs):
    *shares, g_ref, residual_ref = refs
    residual = observed_ref[...] - added([s[...] for s in shares])
    back_projected(residual, kw_ref, columns_ref[...], g_ref)
    residual_ref[...] = residual


def sixth_kernel(layers, base, wave_ref, cut_ref, *refs):
    *g_refs, new_ref = refs
    waves = stepped(layers, base, wave_ref, cut_ref, g_refs, halo_gradient(g_refs))
    new_ref[...] = unstacked(*waves, wave_ref.shape[0])


def seventh_kernel(wave_ref, other_wave_ref, residual_ref, other_residual_ref, out_ref, own_ref):
    rows = own_ref.shape[1]
    is_first = on_first_core()
    out_ref[...] = jnp.where(is_first, other_wave_ref[...], wave_ref[...])
    own_ref[...] = jnp.where(is_first, residual_ref[...], turned(other_residual_ref[...], -rows))[:, :rows]


def from_partner(x, axis, distance):
    return lax.ppermute(x, axis, [(i, i ^ distance) for i in range(lax.axis_size(axis))])


def from_same_core(x, chips, vox):
    n_vox = lax.axis_size("vox")
    places = [(d, z) for d in range(lax.axis_size("dp")) for z in range(n_vox)]
    return lax.ppermute(x, ("dp", "vox"), [(d * n_vox + z, (d ^ (2 * chips)) * n_vox + (z ^ vox)) for d, z in places])


def handed_over(x, sender, chips, vox):
    n_vox = lax.axis_size("vox")
    route = []
    for d in range(lax.axis_size("dp")):
        away = (chips, vox) if d % 2 == sender else (0, 0)
        route += [(d * n_vox + z, (d ^ 1 ^ (2 * away[0])) * n_vox + (z ^ away[1])) for z in range(n_vox)]
    return lax.ppermute(x, ("dp", "vox"), route)


def shares_over(x, size, step, sender):
    lowest = 1
    while size > 4:
        fours = [x] + [from_same_core(x, *step(lowest * n)) for n in (1, 2, 3)]
        x = added([f.astype(F32) for f in fours]).astype(x.dtype)
        lowest, size = lowest * 4, size // 4
    return [handed_over(x, sender, *step(lowest * n)) for n in reversed(range(size))]


def over_chips(x):
    return shares_over(x, lax.axis_size("dp") // 2, lambda n: (n, 0), 0)


def over_vox(x):
    return shares_over(x, lax.axis_size("vox"), lambda n: (0, n), 1)


def call(kernel, out_shape, *args, scratch=(), space=pltpu.VMEM, aliases=None):
    return pl.pallas_call(
        kernel,
        out_shape=out_shape,
        in_specs=[pl.BlockSpec(memory_space=space)] * len(args),
        out_specs=jax.tree.map(lambda _: pl.BlockSpec(memory_space=pltpu.VMEM), out_shape),
        scratch_shapes=list(scratch),
        input_output_aliases=aliases or {},
        compiler_params=pltpu.CompilerParams(vmem_limit_bytes=KERNEL_BYTES),
    )(*[pltpu.with_memory_space_constraint(arg, space) for arg in args])


def body(kernels, observed, initial, threshold):
    models, width = initial.shape
    rows = kernels.shape[0]
    layers = threshold.shape[1]
    n_vox = lax.axis_size("vox")
    assert width == 2 * layers * LANES and rows + KINDS * layers <= LANES and 2 * rows <= LANES
    g_shape = pltpu.VMEM((models, width + LANES), BF16)
    k_shape = pltpu.VMEM((rows, width), BF16)
    tile_shape = pltpu.VMEM((models, LANES), F32)
    both_shape = pltpu.VMEM((2 * (rows + 2 * models), LANES), BF16)

    packet, wavelets, k_mine = call(
        functools.partial(first_kernel, layers),
        (pltpu.VMEM((rows + 6 * models, LANES), BF16), pltpu.VMEM((models, width), F32), k_shape),
        initial,
        kernels,
        observed,
        scratch=[pltpu.VMEM((models, rows), F32), tile_shape, pltpu.SemaphoreType.DMA((3,))],
        space=pltpu.HBM,
    )
    both, observed_both, k_mine = call(
        functools.partial(joining_kernel, models),
        (both_shape, tile_shape, k_shape),
        packet,
        from_partner(packet, "dp", 1),
        k_mine,
        aliases={2: 2},
    )
    k_other = from_partner(k_mine, "dp", 1)
    packets = [handed_over(both, 1, 0, d) for d in reversed(range(1, n_vox))] + [both]
    kw = call(functools.partial(applied_kernel, layers), pltpu.VMEM((LANES, width), BF16), k_mine, k_other)
    kt = call(transposing_kernel, pltpu.VMEM((width, LANES), BF16), k_mine, k_other)
    cut, cut_halo = call(
        functools.partial(spread_kernel, layers, rows),
        (pltpu.VMEM((models, width), F32), tile_shape),
        jnp.swapaxes(threshold, 1, 2),
    )
    g, columns, halo = call(
        functools.partial(second_kernel, layers, n_vox),
        (g_shape, pltpu.VMEM((LANES, LANES), BF16), tile_shape),
        observed_both,
        kw,
        *packets,
        scratch=[pltpu.VMEM((n_vox, *both_shape.shape), BF16), tile_shape],
    )
    wavelets, predicted = call(
        functools.partial(fourth_kernel, layers, rows),
        (pltpu.VMEM((models, width), F32), tile_shape),
        wavelets,
        cut,
        from_partner(halo, "dp", 1),
        cut_halo,
        kt,
        *over_chips(g),
    )
    g, residual = call(fifth_kernel, (g_shape, tile_shape), kw, columns, observed_both, *over_vox(predicted))
    coefficients = call(
        functools.partial(sixth_kernel, layers, rows),
        pltpu.VMEM((models, width), F32),
        wavelets,
        cut,
        *over_chips(g),
    )
    return call(
        seventh_kernel,
        (jax.ShapeDtypeStruct((models, width), F32), jax.ShapeDtypeStruct((models, rows), F32)),
        coefficients,
        from_partner(coefficients, "dp", 1),
        residual,
        from_partner(residual, "dp", 1),
    )


def solution(mesh):
    return jax.shard_map(
        body,
        mesh=mesh,
        in_specs=(P("dp", "vox"), P(None, "dp"), P(None, "vox"), P()),
        out_specs=(P(None, "vox"), P(None, "dp")),
        check_vma=False,
    )
```

```python
import functools

import jax
import jax.numpy as jnp
from jax import lax
from jax.experimental import pallas as pl
from jax.experimental.pallas import tpu as pltpu
from jax.sharding import PartitionSpec as P

step_size = 0.5
LANES = 128
KERNEL_BYTES = 8 * 2**20
F32 = jnp.float32
BF16 = jnp.bfloat16

E_LAST, E_FIRST, E_SECOND, O_LAST, O_FIRST = range(5)
E_NEXT, D_BEFORE, S_NEXT, D_LAST, D_NEXT = range(5)
KINDS = 5


def lanes_of(shape):
    return lax.broadcasted_iota(jnp.int32, shape, len(shape) - 1)


def turned(x, by):
    return pltpu.roll(x, by % LANES, x.ndim - 1)


def shifted_in(x, by, edge):
    free = 0 if by == 1 else LANES - 1
    return jnp.where(lanes_of(x.shape) == free, edge, turned(x, by))


def edge_tile(pair_of, layers, base):
    tile = None
    for layer in range(layers):
        even, odd = pair_of(layer)
        start = base + KINDS * layer
        lane = lanes_of(even.shape)
        if tile is None:
            tile = jnp.zeros_like(even)
        tile = jnp.where((lane >= start) & (lane < start + 3), turned(even, start + 1), tile)
        tile = jnp.where((lane >= start + 3) & (lane < start + 5), turned(odd, start + 4), tile)
    return tile


def kind_lane(lane, base, kind):
    return lax.rem(lane - base + KINDS * LANES, KINDS) == kind


def shrink(values, cutoff):
    return values - jnp.clip(values, -cutoff, cutoff)


def layer_tiles(ref, layer):
    start = layer * 2 * LANES
    return ref[:, start : start + LANES], ref[:, start + LANES : start + 2 * LANES]


def stacked(ref, layers):
    tiles = [layer_tiles(ref, layer) for layer in range(layers)]
    return tuple(jnp.concatenate([t[p] for t in tiles], axis=0).astype(F32) for p in range(2))


def unstacked(even, odd, models):
    rows = [slice(start, start + models) for start in range(0, even.shape[0], models)]
    return jnp.concatenate([t[r] for r in rows for t in (even, odd)], axis=1)


def nt_dot(a, b):
    return lax.dot_general(a, b, (((1,), (1,)), ((), ())), preferred_element_type=F32)


def inverse_wave(smooth, detail, edge):
    even = smooth - 0.25 * (shifted_in(detail, 1, edge) + detail)
    odd = detail + 0.5 * (even + shifted_in(even, -1, edge))
    return even, odd


def forward_wave(even, odd):
    detail = odd - 0.5 * (even + shifted_in(even, -1, 0.0))
    smooth = even + 0.25 * (shifted_in(detail, 1, 0.0) + detail)
    return smooth, detail


def by_kind(lane, base, *values):
    kind = lax.rem(lane - base + KINDS * LANES, KINDS)
    result = values[0]
    for k, value in enumerate(values[1:], 1):
        result = jnp.where(kind == k, value, result)
    return result


def pieces(x, count):
    result = []
    for _ in range(count):
        result.append(x.astype(BF16).astype(F32))
        x = x - result[-1]
    return result


def first_kernel(layers, wave_hbm, k_hbm, observed_hbm, packet_ref, wave_ref, k_ref, observed_ref, tile, arrived):
    rows = k_ref.shape[0]
    models = wave_ref.shape[0]
    loads = [
        pltpu.make_async_copy(source, target, arrived.at[i])
        for i, (source, target) in enumerate(
            ((wave_hbm, wave_ref), (k_hbm, k_ref), (observed_hbm, observed_ref))
        )
    ]
    for load in loads:
        load.start()
    loads[0].wait()
    even, odd = inverse_wave(*stacked(wave_ref, layers), 0.0)
    model = unstacked(even, odd, models).astype(BF16)
    tile[...] = edge_tile(lambda l: layer_tiles(wave_ref, l), layers, rows)
    loads[1].wait()
    loads[2].wait()
    edges = edge_tile(lambda l: tuple(t.astype(F32) for t in layer_tiles(k_ref, l)), layers, rows)
    packet_ref[:rows, :] = edges.astype(BF16)
    tile[:, :rows] = nt_dot(model, k_ref[...])
    parts = pieces(tile[...], 2)
    tile[...] = jnp.zeros_like(tile)
    tile[:, :rows] = observed_ref[...]
    parts += pieces(tile[...], 3) + [jnp.zeros_like(tile)]
    packet_ref[rows:, :] = jnp.concatenate(parts, axis=0).astype(BF16)


def joining_kernel(models, mine_ref, other_ref, k_in_ref, both_ref, observed_ref, k_ref):
    del k_in_ref, k_ref
    is_first = on_first_core()
    mine, other = mine_ref[...].astype(F32), other_ref[...].astype(F32)
    first, second = jnp.where(is_first, mine, other), jnp.where(is_first, other, mine)
    end = mine.shape[0] - 4 * models
    rows = end - 2 * models
    both_ref[...] = jnp.concatenate([first[:end], second[:end]], axis=0).astype(BF16)

    def observations(packet):
        high, middle, low = (packet[i : i + models] for i in range(end, end + 3 * models, models))
        return (high + middle) + low

    observed_ref[...] = observations(first) + turned(observations(second), rows)


def on_first_core():
    return lax.rem(lax.axis_index("dp"), 2) == 0


def applied_kernel(layers, k_ref, k_other_ref, kw_ref):
    core = lax.rem(lax.axis_index("dp"), 2)
    rows = k_ref.shape[0]
    kw_ref[2 * rows :, :] = jnp.zeros((kw_ref.shape[0] - 2 * rows, kw_ref.shape[1]), BF16)
    for which, source in ((core, k_ref), (1 - core, k_other_ref)):
        waves = forward_wave(*stacked(source, layers))
        kw_ref[pl.ds(pl.multiple_of(which * rows, 16), rows), :] = unstacked(*waves, rows).astype(BF16)


def transposing_kernel(k_ref, k_other_ref, kt_ref):
    is_first = on_first_core()
    rows = k_ref.shape[0]
    rest = jnp.zeros((LANES - 2 * rows, LANES), F32)
    for start in range(0, kt_ref.shape[0], LANES):
        mine, other = (ref[:, start : start + LANES].astype(F32) for ref in (k_ref, k_other_ref))
        both = [jnp.where(is_first, mine, other), jnp.where(is_first, other, mine), rest]
        kt_ref[start : start + LANES, :] = jnp.concatenate(both, axis=0).T.astype(BF16)


def spread_kernel(layers, base, threshold_ref, cut_ref, cut_halo_ref):
    models = cut_ref.shape[0]
    lane = lanes_of((models, LANES))
    halo = jnp.zeros((models, LANES), F32)
    for layer in range(layers):
        smooth, detail = (
            jnp.broadcast_to(threshold_ref[:, p, layer : layer + 1], (models, LANES)) for p in range(2)
        )
        start = 2 * LANES * layer
        cut_ref[:, start : start + LANES] = smooth
        cut_ref[:, start + LANES : start + 2 * LANES] = detail
        start = base + KINDS * layer
        here = (lane >= start) & (lane < start + KINDS)
        halo = jnp.where(here, jnp.where(lane == start + S_NEXT, smooth, detail), halo)
    cut_halo_ref[...] = halo


def back_projected(residual, kw_ref, columns, g_ref):
    width = kw_ref.shape[1]
    sent = residual.astype(BF16)
    g_ref[:, :width] = jnp.dot(sent, kw_ref[...], preferred_element_type=F32).astype(BF16)
    g_ref[:, width:] = jnp.dot(sent, columns, preferred_element_type=F32).astype(BF16)


def edge_terms(edge, base, layers):
    lane = lanes_of(edge[0].shape)
    inside = (lane >= base) & (lane < base + KINDS * layers)
    terms = []
    for z, own in enumerate(edge):
        before, after = edge[z - 1], edge[(z + 1) % len(edge)]
        next_smooth = turned(after, O_LAST - E_FIRST)
        next_detail = turned(after, O_LAST - O_FIRST)
        next_even = next_smooth - 0.25 * (own + next_detail)
        term = by_kind(
            lane,
            base,
            0.0,
            -0.25 * turned(before, E_FIRST - O_LAST),
            0.0,
            0.5 * next_even,
            -0.125 * turned(before, O_FIRST - O_LAST),
        )
        terms.append(jnp.where(inside, term, 0.0).astype(BF16))
    return jnp.concatenate(terms, axis=1)


def halo_columns(before, own, after, base):
    lane = lanes_of(own.shape)
    details = by_kind(
        lane,
        base,
        0.0,
        0.0,
        0.0,
        own - 0.5 * (turned(own, O_LAST - E_LAST) + turned(after, O_LAST - E_FIRST)),
        after - 0.5 * (turned(after, O_FIRST - E_FIRST) + turned(after, O_FIRST - E_SECOND)),
    )
    return by_kind(
        lane,
        base,
        turned(after, E_NEXT - E_FIRST),
        turned(before, D_BEFORE - O_LAST) - 0.5 * (turned(before, D_BEFORE - E_LAST) + own),
        turned(after, S_NEXT - E_FIRST) + 0.25 * (turned(details, S_NEXT - D_LAST) + turned(details, S_NEXT - D_NEXT)),
        details,
        details,
    )


def second_kernel(layers, n_vox, distances, observed_ref, kw_ref, *refs):
    (*packets, g_ref, columns_ref, halo_ref, held, tile) = refs
    models = observed_ref.shape[0]
    size = held.shape[1] // 2
    rows = size - 2 * models
    me = lax.axis_index("vox")
    for distance, packet in zip(distances, packets):
        held[me ^ distance] = packet[...]
    left, right = lax.rem(me + n_vox - 1, n_vox), lax.rem(me + 1, n_vox)
    lane = lanes_of((models, LANES))

    def values(which, core):
        both = held[which, core * size + rows : (core + 1) * size, :].astype(F32)
        return both[:models] + both[models:]

    terms = edge_terms([values(z, 0) for z in range(n_vox)], rows, layers)
    columns = []
    tile[...] = jnp.zeros_like(tile)
    for core in range(2):
        edges = jnp.concatenate([held[z, core * size : core * size + rows, :] for z in range(n_vox)], axis=1)
        shares = values(0, core)
        for z in range(1, n_vox):
            shares = shares + values(z, core)
        tile[:, core * rows : (core + 1) * rows] = nt_dot(terms, edges) + shares[:, :rows]
        around = [held[z, core * size : core * size + rows, :].astype(F32) for z in (left, me, right)]
        columns.append(halo_columns(*around, rows))
    columns.append(jnp.zeros((LANES - 2 * rows, LANES), F32))
    columns = jnp.concatenate(columns, axis=0).astype(BF16)
    columns_ref[...] = columns
    back_projected(observed_ref[...] - tile[...], kw_ref, columns, g_ref)
    before, own, after = (values(z, 0) for z in (left, me, right))
    halo_ref[...] = by_kind(
        lane, rows, 0.0, turned(before, D_BEFORE - O_LAST), turned(after, S_NEXT - E_FIRST), own, after
    )


def added(shares):
    while len(shares) > 1:
        shares = [a + b for a, b in zip(shares[::2], shares[1::2])]
    return shares[0]


def at_ends(tile, layers, base):
    return jnp.concatenate([turned(tile, -(base + KINDS * layer + 1)) for layer in range(layers)], axis=0)


def halo_gradient(g_refs):
    return added([g[:, g.shape[1] - LANES :].astype(F32) for g in g_refs])


def stepped(layers, base, wave_ref, cut_ref, g_refs, edge):
    gradients = [stacked(g, layers) for g in g_refs]
    smooth_g, detail_g = (added([g[p] for g in gradients]) for p in range(2))
    ends = at_ends(edge, layers, base)
    lane = lanes_of(ends.shape)
    smooth_g += jnp.where(lane == 0, 0.25 * ends, jnp.where(lane == LANES - 1, -0.125 * ends, 0.0))
    detail_g += jnp.where(lane == LANES - 1, -0.5 * ends, 0.0)
    return tuple(
        shrink(w + step_size * g, cut)
        for w, g, cut in zip(stacked(wave_ref, layers), (smooth_g, detail_g), stacked(cut_ref, layers))
    )


def fourth_kernel(layers, base, wave_ref, cut_ref, halo_ref, cut_halo_ref, kt_ref, *refs):
    *g_refs, new_ref, pred_ref = refs
    models = wave_ref.shape[0]
    edge = halo_gradient(g_refs)
    smooth, detail = stepped(layers, base, wave_ref, cut_ref, g_refs, edge)
    new_ref[...] = unstacked(smooth, detail, models)
    halo = shrink(halo_ref[...] + step_size * edge, cut_halo_ref[...])
    next_even = turned(halo, E_NEXT - S_NEXT) - 0.25 * (turned(halo, E_NEXT - D_LAST) + turned(halo, E_NEXT - D_NEXT))
    ends = at_ends(by_kind(lanes_of(halo.shape), base, next_even, halo), layers, base)
    model = unstacked(*inverse_wave(smooth, detail, ends), models).astype(BF16)
    pred_ref[...] = jnp.dot(model, kt_ref[...], preferred_element_type=F32)


def fifth_kernel(kw_ref, columns_ref, observed_ref, *refs):
    *shares, g_ref, residual_ref = refs
    residual = observed_ref[...] - added([s[...] for s in shares])
    back_projected(residual, kw_ref, columns_ref[...], g_ref)
    residual_ref[...] = residual


def sixth_kernel(layers, base, wave_ref, cut_ref, *refs):
    *g_refs, new_ref = refs
    waves = stepped(layers, base, wave_ref, cut_ref, g_refs, halo_gradient(g_refs))
    new_ref[...] = unstacked(*waves, wave_ref.shape[0])


def seventh_kernel(wave_ref, other_wave_ref, residual_ref, other_residual_ref, out_ref, own_ref):
    rows = own_ref.shape[1]
    is_first = on_first_core()
    out_ref[...] = jnp.where(is_first, other_wave_ref[...], wave_ref[...])
    own_ref[...] = jnp.where(is_first, residual_ref[...], turned(other_residual_ref[...], -rows))[:, :rows]


def from_partner(x, axis, distance):
    return lax.ppermute(x, axis, [(i, i ^ distance) for i in range(lax.axis_size(axis))])


def from_same_core(x, chips, vox):
    n_vox = lax.axis_size("vox")
    places = [(d, z) for d in range(lax.axis_size("dp")) for z in range(n_vox)]
    return lax.ppermute(x, ("dp", "vox"), [(d * n_vox + z, (d ^ (2 * chips)) * n_vox + (z ^ vox)) for d, z in places])


def handed_over(x, sender, chips, vox):
    n_vox = lax.axis_size("vox")
    route = []
    for d in range(lax.axis_size("dp")):
        away = (chips, vox) if d % 2 == sender else (0, 0)
        route += [(d * n_vox + z, (d ^ 1 ^ (2 * away[0])) * n_vox + (z ^ away[1])) for z in range(n_vox)]
    return lax.ppermute(x, ("dp", "vox"), route)


def shares_over(x, size, step, sender):
    lowest = 1
    while size > 4:
        fours = [x] + [from_same_core(x, *step(lowest * n)) for n in (1, 2, 3)]
        x = added([f.astype(F32) for f in fours]).astype(x.dtype)
        lowest, size = lowest * 4, size // 4
    return [handed_over(x, sender, *step(lowest * n)) for n in reversed(range(size))]


def over_chips(x):
    return shares_over(x, lax.axis_size("dp") // 2, lambda n: (n, 0), 0)


def over_vox(x):
    return shares_over(x, lax.axis_size("vox"), lambda n: (0, n), 1)


def call(kernel, out_shape, *args, scratch=(), space=pltpu.VMEM, aliases=None):
    return pl.pallas_call(
        kernel,
        out_shape=out_shape,
        in_specs=[pl.BlockSpec(memory_space=space)] * len(args),
        out_specs=jax.tree.map(lambda _: pl.BlockSpec(memory_space=pltpu.VMEM), out_shape),
        scratch_shapes=list(scratch),
        input_output_aliases=aliases or {},
        compiler_params=pltpu.CompilerParams(vmem_limit_bytes=KERNEL_BYTES),
    )(*[pltpu.with_memory_space_constraint(arg, space) for arg in args])


def body(kernels, observed, initial, threshold):
    models, width = initial.shape
    rows = kernels.shape[0]
    layers = threshold.shape[1]
    n_vox = lax.axis_size("vox")
    assert width == 2 * layers * LANES and rows + KINDS * layers <= LANES and 2 * rows <= LANES
    g_shape = pltpu.VMEM((models, width + LANES), BF16)
    k_shape = pltpu.VMEM((rows, width), BF16)
    tile_shape = pltpu.VMEM((models, LANES), F32)
    both_shape = pltpu.VMEM((2 * (rows + 2 * models), LANES), BF16)

    packet, wavelets, k_mine = call(
        functools.partial(first_kernel, layers),
        (pltpu.VMEM((rows + 6 * models, LANES), BF16), pltpu.VMEM((models, width), F32), k_shape),
        initial,
        kernels,
        observed,
        scratch=[pltpu.VMEM((models, rows), F32), tile_shape, pltpu.SemaphoreType.DMA((3,))],
        space=pltpu.HBM,
    )
    both, observed_both, k_mine = call(
        functools.partial(joining_kernel, models),
        (both_shape, tile_shape, k_shape),
        packet,
        from_partner(packet, "dp", 1),
        k_mine,
        aliases={2: 2},
    )
    k_other = from_partner(k_mine, "dp", 1)
    distances = sorted(range(1, n_vox), key=lambda d: (d != n_vox // 2, -d))
    packets = [handed_over(both, 1, 0, d) for d in distances] + [both]
    kw = call(functools.partial(applied_kernel, layers), pltpu.VMEM((LANES, width), BF16), k_mine, k_other)
    kt = call(transposing_kernel, pltpu.VMEM((width, LANES), BF16), k_mine, k_other)
    cut, cut_halo = call(
        functools.partial(spread_kernel, layers, rows),
        (pltpu.VMEM((models, width), F32), tile_shape),
        jnp.swapaxes(threshold, 1, 2),
    )
    g, columns, halo = call(
        functools.partial(second_kernel, layers, n_vox, distances + [0]),
        (g_shape, pltpu.VMEM((LANES, LANES), BF16), tile_shape),
        observed_both,
        kw,
        *packets,
        scratch=[pltpu.VMEM((n_vox, *both_shape.shape), BF16), tile_shape],
    )
    wavelets, predicted = call(
        functools.partial(fourth_kernel, layers, rows),
        (pltpu.VMEM((models, width), F32), tile_shape),
        wavelets,
        cut,
        from_partner(halo, "dp", 1),
        cut_halo,
        kt,
        *over_chips(g),
    )
    g, residual = call(fifth_kernel, (g_shape, tile_shape), kw, columns, observed_both, *over_vox(predicted))
    coefficients = call(
        functools.partial(sixth_kernel, layers, rows),
        pltpu.VMEM((models, width), F32),
        wavelets,
        cut,
        *over_chips(g),
    )
    return call(
        seventh_kernel,
        (jax.ShapeDtypeStruct((models, width), F32), jax.ShapeDtypeStruct((models, rows), F32)),
        coefficients,
        from_partner(coefficients, "dp", 1),
        residual,
        from_partner(residual, "dp", 1),
    )


def solution(mesh):
    return jax.shard_map(
        body,
        mesh=mesh,
        in_specs=(P("dp", "vox"), P(None, "dp"), P(None, "vox"), P()),
        out_specs=(P(None, "vox"), P(None, "dp")),
        check_vma=False,
    )
```

```python
import functools

import jax
import jax.numpy as jnp
from jax import lax
from jax.experimental import pallas as pl
from jax.experimental.pallas import tpu as pltpu
from jax.sharding import PartitionSpec as P

step_size = 0.5
LANES = 128
KERNEL_BYTES = 8 * 2**20
F32 = jnp.float32
BF16 = jnp.bfloat16

E_LAST, E_FIRST, E_SECOND, O_LAST, O_FIRST = range(5)
E_NEXT, D_BEFORE, S_NEXT, D_LAST, D_NEXT = range(5)
KINDS = 5


def lanes_of(shape):
    return lax.broadcasted_iota(jnp.int32, shape, len(shape) - 1)


def turned(x, by):
    return pltpu.roll(x, by % LANES, x.ndim - 1)


def shifted_in(x, by, edge):
    free = 0 if by == 1 else LANES - 1
    return jnp.where(lanes_of(x.shape) == free, edge, turned(x, by))


def edge_tile(pair_of, layers, base):
    tile = None
    for layer in range(layers):
        even, odd = pair_of(layer)
        start = base + KINDS * layer
        lane = lanes_of(even.shape)
        if tile is None:
            tile = jnp.zeros_like(even)
        tile = jnp.where((lane >= start) & (lane < start + 3), turned(even, start + 1), tile)
        tile = jnp.where((lane >= start + 3) & (lane < start + 5), turned(odd, start + 4), tile)
    return tile


def kind_lane(lane, base, kind):
    return lax.rem(lane - base + KINDS * LANES, KINDS) == kind


def shrink(values, cutoff):
    return values - jnp.clip(values, -cutoff, cutoff)


def layer_tiles(ref, layer):
    start = layer * 2 * LANES
    return ref[:, start : start + LANES], ref[:, start + LANES : start + 2 * LANES]


def stacked(ref, layers):
    tiles = [layer_tiles(ref, layer) for layer in range(layers)]
    return tuple(jnp.concatenate([t[p] for t in tiles], axis=0).astype(F32) for p in range(2))


def unstacked(even, odd, models):
    rows = [slice(start, start + models) for start in range(0, even.shape[0], models)]
    return jnp.concatenate([t[r] for r in rows for t in (even, odd)], axis=1)


def nt_dot(a, b):
    return lax.dot_general(a, b, (((1,), (1,)), ((), ())), preferred_element_type=F32)


def inverse_wave(smooth, detail, edge):
    even = smooth - 0.25 * (shifted_in(detail, 1, edge) + detail)
    odd = detail + 0.5 * (even + shifted_in(even, -1, edge))
    return even, odd


def forward_wave(even, odd):
    detail = odd - 0.5 * (even + shifted_in(even, -1, 0.0))
    smooth = even + 0.25 * (shifted_in(detail, 1, 0.0) + detail)
    return smooth, detail


def by_kind(lane, base, *values):
    kind = lax.rem(lane - base + KINDS * LANES, KINDS)
    result = values[0]
    for k, value in enumerate(values[1:], 1):
        result = jnp.where(kind == k, value, result)
    return result


def pieces(x, count):
    result = []
    for _ in range(count):
        result.append(x.astype(BF16).astype(F32))
        x = x - result[-1]
    return result


def first_kernel(layers, wave_hbm, k_hbm, observed_hbm, packet_ref, wave_ref, k_ref, observed_ref, tile, arrived):
    rows = k_ref.shape[0]
    models = wave_ref.shape[0]
    loads = [
        pltpu.make_async_copy(source, target, arrived.at[i])
        for i, (source, target) in enumerate(
            ((wave_hbm, wave_ref), (k_hbm, k_ref), (observed_hbm, observed_ref))
        )
    ]
    for load in loads:
        load.start()
    loads[0].wait()
    even, odd = inverse_wave(*stacked(wave_ref, layers), 0.0)
    model = unstacked(even, odd, models).astype(BF16)
    tile[...] = edge_tile(lambda l: layer_tiles(wave_ref, l), layers, rows)
    loads[1].wait()
    loads[2].wait()
    edges = edge_tile(lambda l: tuple(t.astype(F32) for t in layer_tiles(k_ref, l)), layers, rows)
    packet_ref[:rows, :] = edges.astype(BF16)
    tile[:, :rows] = nt_dot(model, k_ref[...])
    parts = pieces(tile[...], 2)
    tile[...] = jnp.zeros_like(tile)
    tile[:, :rows] = observed_ref[...]
    parts += pieces(tile[...], 3) + [jnp.zeros_like(tile)]
    packet_ref[rows:, :] = jnp.concatenate(parts, axis=0).astype(BF16)


def joining_kernel(models, mine_ref, other_ref, k_in_ref, both_ref, observed_ref, k_ref):
    del k_in_ref, k_ref
    is_first = on_first_core()
    mine, other = mine_ref[...].astype(F32), other_ref[...].astype(F32)
    first, second = jnp.where(is_first, mine, other), jnp.where(is_first, other, mine)
    end = mine.shape[0] - 4 * models
    rows = end - 2 * models
    both_ref[...] = jnp.concatenate([first[:end], second[:end]], axis=0).astype(BF16)

    def observations(packet):
        high, middle, low = (packet[i : i + models] for i in range(end, end + 3 * models, models))
        return (high + middle) + low

    observed_ref[...] = observations(first) + turned(observations(second), rows)


def on_first_core():
    return lax.rem(lax.axis_index("dp"), 2) == 0


def applied_kernel(layers, k_ref, k_other_ref, kw_ref):
    core = lax.rem(lax.axis_index("dp"), 2)
    rows = k_ref.shape[0]
    kw_ref[2 * rows :, :] = jnp.zeros((kw_ref.shape[0] - 2 * rows, kw_ref.shape[1]), BF16)
    for which, source in ((core, k_ref), (1 - core, k_other_ref)):
        waves = forward_wave(*stacked(source, layers))
        kw_ref[pl.ds(pl.multiple_of(which * rows, 16), rows), :] = unstacked(*waves, rows).astype(BF16)


def transposing_kernel(k_ref, k_other_ref, kt_ref):
    is_first = on_first_core()
    rows = k_ref.shape[0]
    rest = jnp.zeros((LANES - 2 * rows, LANES), F32)
    for start in range(0, kt_ref.shape[0], LANES):
        mine, other = (ref[:, start : start + LANES].astype(F32) for ref in (k_ref, k_other_ref))
        both = [jnp.where(is_first, mine, other), jnp.where(is_first, other, mine), rest]
        kt_ref[start : start + LANES, :] = jnp.concatenate(both, axis=0).T.astype(BF16)


def spread_kernel(layers, base, threshold_ref, cut_ref, cut_halo_ref):
    models = cut_ref.shape[0]
    lane = lanes_of((models, LANES))
    halo = jnp.zeros((models, LANES), F32)
    for layer in range(layers):
        smooth, detail = (
            jnp.broadcast_to(threshold_ref[:, p, layer : layer + 1], (models, LANES)) for p in range(2)
        )
        start = 2 * LANES * layer
        cut_ref[:, start : start + LANES] = smooth
        cut_ref[:, start + LANES : start + 2 * LANES] = detail
        start = base + KINDS * layer
        here = (lane >= start) & (lane < start + KINDS)
        halo = jnp.where(here, jnp.where(lane == start + S_NEXT, smooth, detail), halo)
    cut_halo_ref[...] = halo


def back_projected(residual, kw_ref, columns, g_ref):
    width = kw_ref.shape[1]
    sent = residual.astype(BF16)
    g_ref[:, :width] = jnp.dot(sent, kw_ref[...], preferred_element_type=F32).astype(BF16)
    g_ref[:, width:] = jnp.dot(sent, columns, preferred_element_type=F32).astype(BF16)


def edge_terms(edge, base, layers):
    lane = lanes_of(edge[0].shape)
    inside = (lane >= base) & (lane < base + KINDS * layers)
    terms = []
    for z, own in enumerate(edge):
        before, after = edge[z - 1], edge[(z + 1) % len(edge)]
        next_smooth = turned(after, O_LAST - E_FIRST)
        next_detail = turned(after, O_LAST - O_FIRST)
        next_even = next_smooth - 0.25 * (own + next_detail)
        term = by_kind(
            lane,
            base,
            0.0,
            -0.25 * turned(before, E_FIRST - O_LAST),
            0.0,
            0.5 * next_even,
            -0.125 * turned(before, O_FIRST - O_LAST),
        )
        terms.append(jnp.where(inside, term, 0.0).astype(BF16))
    return jnp.concatenate(terms, axis=1)


def halo_columns(before, own, after, base):
    lane = lanes_of(own.shape)
    details = by_kind(
        lane,
        base,
        0.0,
        0.0,
        0.0,
        own - 0.5 * (turned(own, O_LAST - E_LAST) + turned(after, O_LAST - E_FIRST)),
        after - 0.5 * (turned(after, O_FIRST - E_FIRST) + turned(after, O_FIRST - E_SECOND)),
    )
    return by_kind(
        lane,
        base,
        turned(after, E_NEXT - E_FIRST),
        turned(before, D_BEFORE - O_LAST) - 0.5 * (turned(before, D_BEFORE - E_LAST) + own),
        turned(after, S_NEXT - E_FIRST) + 0.25 * (turned(details, S_NEXT - D_LAST) + turned(details, S_NEXT - D_NEXT)),
        details,
        details,
    )


def second_kernel(layers, n_vox, distances, observed_ref, kw_ref, *refs):
    (*packets, g_ref, columns_ref, halo_ref, held) = refs
    models = observed_ref.shape[0]
    size = held.shape[1] // 2
    rows = size - 2 * models
    me = lax.axis_index("vox")
    for distance, packet in zip(distances, packets):
        held[me ^ distance] = packet[...]
    left, right = lax.rem(me + n_vox - 1, n_vox), lax.rem(me + 1, n_vox)
    lane = lanes_of((models, LANES))

    def values(which, core):
        both = held[which, core * size + rows : (core + 1) * size, :].astype(F32)
        return both[:models] + both[models:]

    terms = edge_terms([values(z, 0) for z in range(n_vox)], rows, layers)
    edges, columns, shares = [], [], []
    for core in range(2):
        edges.append(
            jnp.concatenate([held[z, core * size : core * size + rows, :] for z in range(n_vox)], axis=1)
        )
        share = values(0, core)
        for z in range(1, n_vox):
            share = share + values(z, core)
        shares.append(jnp.where(lane < rows, share, 0.0))
        around = [held[z, core * size : core * size + rows, :].astype(F32) for z in (left, me, right)]
        columns.append(halo_columns(*around, rows))
    known = observed_ref[...] - (shares[0] + turned(shares[1], rows))
    residual = known[:, : 2 * rows] - nt_dot(terms, jnp.concatenate(edges, axis=0))
    columns = jnp.concatenate(columns, axis=0).astype(BF16)
    columns_ref[...] = jnp.zeros_like(columns_ref)
    columns_ref[: 2 * rows, :] = columns
    back_projected(residual, kw_ref.at[: 2 * rows], columns, g_ref)
    before, own, after = (values(z, 0) for z in (left, me, right))
    halo_ref[...] = by_kind(
        lane, rows, 0.0, turned(before, D_BEFORE - O_LAST), turned(after, S_NEXT - E_FIRST), own, after
    )


def added(shares):
    while len(shares) > 1:
        shares = [a + b for a, b in zip(shares[::2], shares[1::2])]
    return shares[0]


def at_ends(tile, layers, base):
    return jnp.concatenate([turned(tile, -(base + KINDS * layer + 1)) for layer in range(layers)], axis=0)


def halo_gradient(g_refs):
    return added([g[:, g.shape[1] - LANES :].astype(F32) for g in g_refs])


def stepped(layers, base, wave_ref, cut_ref, g_refs, edge):
    gradients = [stacked(g, layers) for g in g_refs]
    smooth_g, detail_g = (added([g[p] for g in gradients]) for p in range(2))
    ends = at_ends(edge, layers, base)
    lane = lanes_of(ends.shape)
    smooth_g += jnp.where(lane == 0, 0.25 * ends, jnp.where(lane == LANES - 1, -0.125 * ends, 0.0))
    detail_g += jnp.where(lane == LANES - 1, -0.5 * ends, 0.0)
    return tuple(
        shrink(w + step_size * g, cut)
        for w, g, cut in zip(stacked(wave_ref, layers), (smooth_g, detail_g), stacked(cut_ref, layers))
    )


def fourth_kernel(layers, base, wave_ref, cut_ref, halo_ref, cut_halo_ref, kt_ref, *refs):
    *g_refs, new_ref, pred_ref = refs
    models = wave_ref.shape[0]
    edge = halo_gradient(g_refs)
    smooth, detail = stepped(layers, base, wave_ref, cut_ref, g_refs, edge)
    new_ref[...] = unstacked(smooth, detail, models)
    halo = shrink(halo_ref[...] + step_size * edge, cut_halo_ref[...])
    next_even = turned(halo, E_NEXT - S_NEXT) - 0.25 * (turned(halo, E_NEXT - D_LAST) + turned(halo, E_NEXT - D_NEXT))
    ends = at_ends(by_kind(lanes_of(halo.shape), base, next_even, halo), layers, base)
    model = unstacked(*inverse_wave(smooth, detail, ends), models).astype(BF16)
    pred_ref[...] = jnp.dot(model, kt_ref[...], preferred_element_type=F32)


def fifth_kernel(kw_ref, columns_ref, observed_ref, *refs):
    *shares, g_ref, residual_ref = refs
    residual = observed_ref[...] - added([s[...] for s in shares])
    back_projected(residual, kw_ref, columns_ref[...], g_ref)
    residual_ref[...] = residual


def sixth_kernel(layers, base, residual_in_ref, wave_ref, cut_ref, *refs):
    *g_refs, new_ref, residual_ref = refs
    del residual_in_ref, residual_ref
    waves = stepped(layers, base, wave_ref, cut_ref, g_refs, halo_gradient(g_refs))
    new_ref[...] = unstacked(*waves, wave_ref.shape[0])


def seventh_kernel(wave_ref, other_wave_ref, residual_ref, other_residual_ref, out_ref, own_ref):
    rows = own_ref.shape[1]
    is_first = on_first_core()
    out_ref[...] = jnp.where(is_first, other_wave_ref[...], wave_ref[...])
    own_ref[...] = jnp.where(is_first, residual_ref[...], turned(other_residual_ref[...], -rows))[:, :rows]


def from_partner(x, axis, distance):
    return lax.ppermute(x, axis, [(i, i ^ distance) for i in range(lax.axis_size(axis))])


def from_same_core(x, chips, vox):
    n_vox = lax.axis_size("vox")
    places = [(d, z) for d in range(lax.axis_size("dp")) for z in range(n_vox)]
    return lax.ppermute(x, ("dp", "vox"), [(d * n_vox + z, (d ^ (2 * chips)) * n_vox + (z ^ vox)) for d, z in places])


def handed_over(x, sender, chips, vox):
    n_vox = lax.axis_size("vox")
    route = []
    for d in range(lax.axis_size("dp")):
        away = (chips, vox) if d % 2 == sender else (0, 0)
        route += [(d * n_vox + z, (d ^ 1 ^ (2 * away[0])) * n_vox + (z ^ away[1])) for z in range(n_vox)]
    return lax.ppermute(x, ("dp", "vox"), route)


def shares_over(x, size, step, sender):
    lowest = 1
    while size > 4:
        fours = [x] + [from_same_core(x, *step(lowest * n)) for n in (1, 2, 3)]
        x = added([f.astype(F32) for f in fours]).astype(x.dtype)
        lowest, size = lowest * 4, size // 4
    return [handed_over(x, sender, *step(lowest * n)) for n in reversed(range(size))]


def over_chips(x):
    return shares_over(x, lax.axis_size("dp") // 2, lambda n: (n, 0), 0)


def over_vox(x):
    return shares_over(x, lax.axis_size("vox"), lambda n: (0, n), 1)


def call(kernel, out_shape, *args, scratch=(), space=pltpu.VMEM, aliases=None):
    return pl.pallas_call(
        kernel,
        out_shape=out_shape,
        in_specs=[pl.BlockSpec(memory_space=space)] * len(args),
        out_specs=jax.tree.map(lambda _: pl.BlockSpec(memory_space=pltpu.VMEM), out_shape),
        scratch_shapes=list(scratch),
        input_output_aliases=aliases or {},
        compiler_params=pltpu.CompilerParams(vmem_limit_bytes=KERNEL_BYTES),
    )(*[pltpu.with_memory_space_constraint(arg, space) for arg in args])


def body(kernels, observed, initial, threshold):
    models, width = initial.shape
    rows = kernels.shape[0]
    layers = threshold.shape[1]
    n_vox = lax.axis_size("vox")
    assert width == 2 * layers * LANES and rows + KINDS * layers <= LANES and 2 * rows <= LANES
    g_shape = pltpu.VMEM((models, width + LANES), BF16)
    k_shape = pltpu.VMEM((rows, width), BF16)
    tile_shape = pltpu.VMEM((models, LANES), F32)
    both_shape = pltpu.VMEM((2 * (rows + 2 * models), LANES), BF16)

    packet, wavelets, k_mine = call(
        functools.partial(first_kernel, layers),
        (pltpu.VMEM((rows + 6 * models, LANES), BF16), pltpu.VMEM((models, width), F32), k_shape),
        initial,
        kernels,
        observed,
        scratch=[pltpu.VMEM((models, rows), F32), tile_shape, pltpu.SemaphoreType.DMA((3,))],
        space=pltpu.HBM,
    )
    both, observed_both, k_mine = call(
        functools.partial(joining_kernel, models),
        (both_shape, tile_shape, k_shape),
        packet,
        from_partner(packet, "dp", 1),
        k_mine,
        aliases={2: 2},
    )
    k_other = from_partner(k_mine, "dp", 1)
    distances = sorted(range(1, n_vox), key=lambda d: (d != n_vox // 2, -d))
    packets = [handed_over(both, 1, 0, d) for d in distances] + [both]
    kw = call(functools.partial(applied_kernel, layers), pltpu.VMEM((LANES, width), BF16), k_mine, k_other)
    kt = call(transposing_kernel, pltpu.VMEM((width, LANES), BF16), k_mine, k_other)
    cut, cut_halo = call(
        functools.partial(spread_kernel, layers, rows),
        (pltpu.VMEM((models, width), F32), tile_shape),
        jnp.swapaxes(threshold, 1, 2),
    )
    g, columns, halo = call(
        functools.partial(second_kernel, layers, n_vox, distances + [0]),
        (g_shape, pltpu.VMEM((LANES, LANES), BF16), tile_shape),
        observed_both,
        kw,
        *packets,
        scratch=[pltpu.VMEM((n_vox, *both_shape.shape), BF16)],
    )
    wavelets, predicted = call(
        functools.partial(fourth_kernel, layers, rows),
        (pltpu.VMEM((models, width), F32), tile_shape),
        wavelets,
        cut,
        from_partner(halo, "dp", 1),
        cut_halo,
        kt,
        *over_chips(g),
    )
    g, residual = call(fifth_kernel, (g_shape, tile_shape), kw, columns, observed_both, *over_vox(predicted))
    coefficients, residual_other = call(
        functools.partial(sixth_kernel, layers, rows),
        (pltpu.VMEM((models, width), F32), tile_shape),
        from_partner(residual, "dp", 1),
        wavelets,
        cut,
        *over_chips(g),
        aliases={0: 1},
    )
    return call(
        seventh_kernel,
        (jax.ShapeDtypeStruct((models, width), F32), jax.ShapeDtypeStruct((models, rows), F32)),
        coefficients,
        from_partner(coefficients, "dp", 1),
        residual,
        residual_other,
    )


def solution(mesh):
    return jax.shard_map(
        body,
        mesh=mesh,
        in_specs=(P("dp", "vox"), P(None, "dp"), P(None, "vox"), P()),
        out_specs=(P(None, "vox"), P(None, "dp")),
        check_vma=False,
    )
```

```python
import functools

import jax
import jax.numpy as jnp
from jax import lax
from jax.experimental import pallas as pl
from jax.experimental.pallas import tpu as pltpu
from jax.sharding import PartitionSpec as P

step_size = 0.5
LANES = 128
KERNEL_BYTES = 8 * 2**20
F32 = jnp.float32
BF16 = jnp.bfloat16

E_LAST, E_FIRST, E_SECOND, O_LAST, O_FIRST = range(5)
E_NEXT, D_BEFORE, S_NEXT, D_LAST, D_NEXT = range(5)
KINDS = 5


def lanes_of(shape):
    return lax.broadcasted_iota(jnp.int32, shape, len(shape) - 1)


def turned(x, by):
    return pltpu.roll(x, by % LANES, x.ndim - 1)


def shifted_in(x, by, edge):
    free = 0 if by == 1 else LANES - 1
    return jnp.where(lanes_of(x.shape) == free, edge, turned(x, by))


def edge_tile(pair_of, layers, base):
    tile = None
    for layer in range(layers):
        even, odd = pair_of(layer)
        start = base + KINDS * layer
        lane = lanes_of(even.shape)
        if tile is None:
            tile = jnp.zeros_like(even)
        tile = jnp.where((lane >= start) & (lane < start + 3), turned(even, start + 1), tile)
        tile = jnp.where((lane >= start + 3) & (lane < start + 5), turned(odd, start + 4), tile)
    return tile


def kind_lane(lane, base, kind):
    return lax.rem(lane - base + KINDS * LANES, KINDS) == kind


def shrink(values, cutoff):
    return values - jnp.clip(values, -cutoff, cutoff)


def layer_tiles(ref, layer):
    start = layer * 2 * LANES
    return ref[:, start : start + LANES], ref[:, start + LANES : start + 2 * LANES]


def stacked(ref, layers):
    tiles = [layer_tiles(ref, layer) for layer in range(layers)]
    return tuple(jnp.concatenate([t[p] for t in tiles], axis=0).astype(F32) for p in range(2))


def unstacked(even, odd, models):
    rows = [slice(start, start + models) for start in range(0, even.shape[0], models)]
    return jnp.concatenate([t[r] for r in rows for t in (even, odd)], axis=1)


def nt_dot(a, b):
    return lax.dot_general(a, b, (((1,), (1,)), ((), ())), preferred_element_type=F32)


def inverse_wave(smooth, detail, edge):
    even = smooth - 0.25 * (shifted_in(detail, 1, edge) + detail)
    odd = detail + 0.5 * (even + shifted_in(even, -1, edge))
    return even, odd


def forward_wave(even, odd):
    detail = odd - 0.5 * (even + shifted_in(even, -1, 0.0))
    smooth = even + 0.25 * (shifted_in(detail, 1, 0.0) + detail)
    return smooth, detail


def by_kind(lane, base, *values):
    kind = lax.rem(lane - base + KINDS * LANES, KINDS)
    result = values[0]
    for k, value in enumerate(values[1:], 1):
        result = jnp.where(kind == k, value, result)
    return result


def pieces(x, count):
    result = []
    for _ in range(count):
        result.append(x.astype(BF16).astype(F32))
        x = x - result[-1]
    return result


def first_kernel(layers, wave_hbm, k_hbm, observed_hbm, packet_ref, wave_ref, k_ref, observed_ref, tile, arrived):
    rows = k_ref.shape[0]
    models = wave_ref.shape[0]
    loads = [
        pltpu.make_async_copy(source, target, arrived.at[i])
        for i, (source, target) in enumerate(
            ((wave_hbm, wave_ref), (k_hbm, k_ref), (observed_hbm, observed_ref))
        )
    ]
    for load, priority in zip(loads, (0, 1, 0)):
        load.start(priority=priority)
    loads[0].wait()
    even, odd = inverse_wave(*stacked(wave_ref, layers), 0.0)
    model = unstacked(even, odd, models).astype(BF16)
    tile[...] = edge_tile(lambda l: layer_tiles(wave_ref, l), layers, rows)
    loads[1].wait()
    loads[2].wait()
    edges = edge_tile(lambda l: tuple(t.astype(F32) for t in layer_tiles(k_ref, l)), layers, rows)
    packet_ref[:rows, :] = edges.astype(BF16)
    tile[:, :rows] = nt_dot(model, k_ref[...])
    parts = pieces(tile[...], 2)
    tile[...] = jnp.zeros_like(tile)
    tile[:, :rows] = observed_ref[...]
    parts += pieces(tile[...], 3) + [jnp.zeros_like(tile)]
    packet_ref[rows:, :] = jnp.concatenate(parts, axis=0).astype(BF16)


def joining_kernel(models, mine_ref, other_ref, k_in_ref, both_ref, observed_ref, k_ref):
    del k_in_ref, k_ref
    is_first = on_first_core()
    mine, other = mine_ref[...].astype(F32), other_ref[...].astype(F32)
    first, second = jnp.where(is_first, mine, other), jnp.where(is_first, other, mine)
    end = mine.shape[0] - 4 * models
    rows = end - 2 * models
    both_ref[...] = jnp.concatenate([first[:end], second[:end]], axis=0).astype(BF16)

    def observations(packet):
        high, middle, low = (packet[i : i + models] for i in range(end, end + 3 * models, models))
        return (high + middle) + low

    observed_ref[...] = observations(first) + turned(observations(second), rows)


def on_first_core():
    return lax.rem(lax.axis_index("dp"), 2) == 0


def applied_kernel(layers, k_ref, k_other_ref, kw_ref):
    core = lax.rem(lax.axis_index("dp"), 2)
    rows = k_ref.shape[0]
    kw_ref[2 * rows :, :] = jnp.zeros((kw_ref.shape[0] - 2 * rows, kw_ref.shape[1]), BF16)
    for which, source in ((core, k_ref), (1 - core, k_other_ref)):
        waves = forward_wave(*stacked(source, layers))
        kw_ref[pl.ds(pl.multiple_of(which * rows, 16), rows), :] = unstacked(*waves, rows).astype(BF16)


def transposing_kernel(k_ref, k_other_ref, kt_ref):
    is_first = on_first_core()
    rows = k_ref.shape[0]
    rest = jnp.zeros((LANES - 2 * rows, LANES), F32)
    for start in range(0, kt_ref.shape[0], LANES):
        mine, other = (ref[:, start : start + LANES].astype(F32) for ref in (k_ref, k_other_ref))
        both = [jnp.where(is_first, mine, other), jnp.where(is_first, other, mine), rest]
        kt_ref[start : start + LANES, :] = jnp.concatenate(both, axis=0).T.astype(BF16)


def spread_kernel(layers, base, threshold_ref, cut_ref, cut_halo_ref):
    models = cut_ref.shape[0]
    lane = lanes_of((models, LANES))
    halo = jnp.zeros((models, LANES), F32)
    for layer in range(layers):
        smooth, detail = (
            jnp.broadcast_to(threshold_ref[:, p, layer : layer + 1], (models, LANES)) for p in range(2)
        )
        start = 2 * LANES * layer
        cut_ref[:, start : start + LANES] = smooth
        cut_ref[:, start + LANES : start + 2 * LANES] = detail
        start = base + KINDS * layer
        here = (lane >= start) & (lane < start + KINDS)
        halo = jnp.where(here, jnp.where(lane == start + S_NEXT, smooth, detail), halo)
    cut_halo_ref[...] = halo


def back_projected(residual, kw_ref, columns, g_ref):
    width = kw_ref.shape[1]
    sent = residual.astype(BF16)
    g_ref[:, :width] = jnp.dot(sent, kw_ref[...], preferred_element_type=F32).astype(BF16)
    g_ref[:, width:] = jnp.dot(sent, columns, preferred_element_type=F32).astype(BF16)


def edge_terms(edge, base, layers):
    lane = lanes_of(edge[0].shape)
    inside = (lane >= base) & (lane < base + KINDS * layers)
    terms = []
    for z, own in enumerate(edge):
        before, after = edge[z - 1], edge[(z + 1) % len(edge)]
        next_smooth = turned(after, O_LAST - E_FIRST)
        next_detail = turned(after, O_LAST - O_FIRST)
        next_even = next_smooth - 0.25 * (own + next_detail)
        term = by_kind(
            lane,
            base,
            0.0,
            -0.25 * turned(before, E_FIRST - O_LAST),
            0.0,
            0.5 * next_even,
            -0.125 * turned(before, O_FIRST - O_LAST),
        )
        terms.append(jnp.where(inside, term, 0.0).astype(BF16))
    return jnp.concatenate(terms, axis=1)


def halo_columns(before, own, after, base):
    lane = lanes_of(own.shape)
    details = by_kind(
        lane,
        base,
        0.0,
        0.0,
        0.0,
        own - 0.5 * (turned(own, O_LAST - E_LAST) + turned(after, O_LAST - E_FIRST)),
        after - 0.5 * (turned(after, O_FIRST - E_FIRST) + turned(after, O_FIRST - E_SECOND)),
    )
    return by_kind(
        lane,
        base,
        turned(after, E_NEXT - E_FIRST),
        turned(before, D_BEFORE - O_LAST) - 0.5 * (turned(before, D_BEFORE - E_LAST) + own),
        turned(after, S_NEXT - E_FIRST) + 0.25 * (turned(details, S_NEXT - D_LAST) + turned(details, S_NEXT - D_NEXT)),
        details,
        details,
    )


def second_kernel(layers, n_vox, distances, observed_ref, kw_ref, *refs):
    (*packets, g_ref, columns_ref, halo_ref, held) = refs
    models = observed_ref.shape[0]
    size = held.shape[1] // 2
    rows = size - 2 * models
    me = lax.axis_index("vox")
    for distance, packet in zip(distances, packets):
        held[me ^ distance] = packet[...]
    left, right = lax.rem(me + n_vox - 1, n_vox), lax.rem(me + 1, n_vox)
    lane = lanes_of((models, LANES))

    def values(which, core):
        both = held[which, core * size + rows : (core + 1) * size, :].astype(F32)
        return both[:models] + both[models:]

    terms = edge_terms([values(z, 0) for z in range(n_vox)], rows, layers)
    edges, columns, shares = [], [], []
    for core in range(2):
        edges.append(
            jnp.concatenate([held[z, core * size : core * size + rows, :] for z in range(n_vox)], axis=1)
        )
        share = values(0, core)
        for z in range(1, n_vox):
            share = share + values(z, core)
        shares.append(jnp.where(lane < rows, share, 0.0))
        around = [held[z, core * size : core * size + rows, :].astype(F32) for z in (left, me, right)]
        columns.append(halo_columns(*around, rows))
    known = observed_ref[...] - (shares[0] + turned(shares[1], rows))
    residual = known[:, : 2 * rows] - nt_dot(terms, jnp.concatenate(edges, axis=0))
    columns = jnp.concatenate(columns, axis=0).astype(BF16)
    columns_ref[...] = jnp.zeros_like(columns_ref)
    columns_ref[: 2 * rows, :] = columns
    back_projected(residual, kw_ref.at[: 2 * rows], columns, g_ref)
    before, own, after = (values(z, 0) for z in (left, me, right))
    halo_ref[...] = by_kind(
        lane, rows, 0.0, turned(before, D_BEFORE - O_LAST), turned(after, S_NEXT - E_FIRST), own, after
    )


def added(shares):
    while len(shares) > 1:
        shares = [a + b for a, b in zip(shares[::2], shares[1::2])]
    return shares[0]


def at_ends(tile, layers, base):
    return jnp.concatenate([turned(tile, -(base + KINDS * layer + 1)) for layer in range(layers)], axis=0)


def halo_gradient(g_refs):
    return added([g[:, g.shape[1] - LANES :].astype(F32) for g in g_refs])


def stepped(layers, base, wave_ref, cut_ref, g_refs, edge):
    gradients = [stacked(g, layers) for g in g_refs]
    smooth_g, detail_g = (added([g[p] for g in gradients]) for p in range(2))
    ends = at_ends(edge, layers, base)
    lane = lanes_of(ends.shape)
    smooth_g += jnp.where(lane == 0, 0.25 * ends, jnp.where(lane == LANES - 1, -0.125 * ends, 0.0))
    detail_g += jnp.where(lane == LANES - 1, -0.5 * ends, 0.0)
    return tuple(
        shrink(w + step_size * g, cut)
        for w, g, cut in zip(stacked(wave_ref, layers), (smooth_g, detail_g), stacked(cut_ref, layers))
    )


def fourth_kernel(layers, base, wave_ref, cut_ref, halo_ref, cut_halo_ref, kt_ref, *refs):
    *g_refs, new_ref, pred_ref = refs
    models = wave_ref.shape[0]
    edge = halo_gradient(g_refs)
    smooth, detail = stepped(layers, base, wave_ref, cut_ref, g_refs, edge)
    new_ref[...] = unstacked(smooth, detail, models)
    halo = shrink(halo_ref[...] + step_size * edge, cut_halo_ref[...])
    next_even = turned(halo, E_NEXT - S_NEXT) - 0.25 * (turned(halo, E_NEXT - D_LAST) + turned(halo, E_NEXT - D_NEXT))
    ends = at_ends(by_kind(lanes_of(halo.shape), base, next_even, halo), layers, base)
    model = unstacked(*inverse_wave(smooth, detail, ends), models).astype(BF16)
    pred_ref[...] = jnp.dot(model, kt_ref[...], preferred_element_type=F32)


def fifth_kernel(kw_ref, columns_ref, observed_ref, *refs):
    *shares, g_ref, residual_ref = refs
    residual = observed_ref[...] - added([s[...] for s in shares])
    back_projected(residual, kw_ref, columns_ref[...], g_ref)
    residual_ref[...] = residual


def sixth_kernel(layers, base, residual_in_ref, wave_ref, cut_ref, *refs):
    *g_refs, new_ref, residual_ref = refs
    del residual_in_ref, residual_ref
    waves = stepped(layers, base, wave_ref, cut_ref, g_refs, halo_gradient(g_refs))
    new_ref[...] = unstacked(*waves, wave_ref.shape[0])


def seventh_kernel(wave_ref, other_wave_ref, residual_ref, other_residual_ref, out_ref, own_ref):
    rows = own_ref.shape[1]
    is_first = on_first_core()
    out_ref[...] = jnp.where(is_first, other_wave_ref[...], wave_ref[...])
    own_ref[...] = jnp.where(is_first, residual_ref[...], turned(other_residual_ref[...], -rows))[:, :rows]


def from_partner(x, axis, distance):
    return lax.ppermute(x, axis, [(i, i ^ distance) for i in range(lax.axis_size(axis))])


def from_same_core(x, chips, vox):
    n_vox = lax.axis_size("vox")
    places = [(d, z) for d in range(lax.axis_size("dp")) for z in range(n_vox)]
    return lax.ppermute(x, ("dp", "vox"), [(d * n_vox + z, (d ^ (2 * chips)) * n_vox + (z ^ vox)) for d, z in places])


def handed_over(x, sender, chips, vox):
    n_vox = lax.axis_size("vox")
    route = []
    for d in range(lax.axis_size("dp")):
        away = (chips, vox) if d % 2 == sender else (0, 0)
        route += [(d * n_vox + z, (d ^ 1 ^ (2 * away[0])) * n_vox + (z ^ away[1])) for z in range(n_vox)]
    return lax.ppermute(x, ("dp", "vox"), route)


def shares_over(x, size, step, sender):
    lowest = 1
    while size > 4:
        fours = [x] + [from_same_core(x, *step(lowest * n)) for n in (1, 2, 3)]
        x = added([f.astype(F32) for f in fours]).astype(x.dtype)
        lowest, size = lowest * 4, size // 4
    return [handed_over(x, sender, *step(lowest * n)) for n in reversed(range(size))]


def over_chips(x):
    return shares_over(x, lax.axis_size("dp") // 2, lambda n: (n, 0), 0)


def over_vox(x):
    return shares_over(x, lax.axis_size("vox"), lambda n: (0, n), 1)


def call(kernel, out_shape, *args, scratch=(), space=pltpu.VMEM, aliases=None):
    return pl.pallas_call(
        kernel,
        out_shape=out_shape,
        in_specs=[pl.BlockSpec(memory_space=space)] * len(args),
        out_specs=jax.tree.map(lambda _: pl.BlockSpec(memory_space=pltpu.VMEM), out_shape),
        scratch_shapes=list(scratch),
        input_output_aliases=aliases or {},
        compiler_params=pltpu.CompilerParams(vmem_limit_bytes=KERNEL_BYTES),
    )(*[pltpu.with_memory_space_constraint(arg, space) for arg in args])


def body(kernels, observed, initial, threshold):
    models, width = initial.shape
    rows = kernels.shape[0]
    layers = threshold.shape[1]
    n_vox = lax.axis_size("vox")
    assert width == 2 * layers * LANES and rows + KINDS * layers <= LANES and 2 * rows <= LANES
    g_shape = pltpu.VMEM((models, width + LANES), BF16)
    k_shape = pltpu.VMEM((rows, width), BF16)
    tile_shape = pltpu.VMEM((models, LANES), F32)
    both_shape = pltpu.VMEM((2 * (rows + 2 * models), LANES), BF16)

    packet, wavelets, k_mine = call(
        functools.partial(first_kernel, layers),
        (pltpu.VMEM((rows + 6 * models, LANES), BF16), pltpu.VMEM((models, width), F32), k_shape),
        initial,
        kernels,
        observed,
        scratch=[pltpu.VMEM((models, rows), F32), tile_shape, pltpu.SemaphoreType.DMA((3,))],
        space=pltpu.HBM,
    )
    both, observed_both, k_mine = call(
        functools.partial(joining_kernel, models),
        (both_shape, tile_shape, k_shape),
        packet,
        from_partner(packet, "dp", 1),
        k_mine,
        aliases={2: 2},
    )
    k_other = from_partner(k_mine, "dp", 1)
    distances = sorted(range(1, n_vox), key=lambda d: (d != n_vox // 2, -d))
    packets = [handed_over(both, 1, 0, d) for d in distances] + [both]
    kw = call(functools.partial(applied_kernel, layers), pltpu.VMEM((LANES, width), BF16), k_mine, k_other)
    kt = call(transposing_kernel, pltpu.VMEM((width, LANES), BF16), k_mine, k_other)
    cut, cut_halo = call(
        functools.partial(spread_kernel, layers, rows),
        (pltpu.VMEM((models, width), F32), tile_shape),
        jnp.swapaxes(threshold, 1, 2),
    )
    g, columns, halo = call(
        functools.partial(second_kernel, layers, n_vox, distances + [0]),
        (g_shape, pltpu.VMEM((LANES, LANES), BF16), tile_shape),
        observed_both,
        kw,
        *packets,
        scratch=[pltpu.VMEM((n_vox, *both_shape.shape), BF16)],
    )
    wavelets, predicted = call(
        functools.partial(fourth_kernel, layers, rows),
        (pltpu.VMEM((models, width), F32), tile_shape),
        wavelets,
        cut,
        from_partner(halo, "dp", 1),
        cut_halo,
        kt,
        *over_chips(g),
    )
    g, residual = call(fifth_kernel, (g_shape, tile_shape), kw, columns, observed_both, *over_vox(predicted))
    coefficients, residual_other = call(
        functools.partial(sixth_kernel, layers, rows),
        (pltpu.VMEM((models, width), F32), tile_shape),
        from_partner(residual, "dp", 1),
        wavelets,
        cut,
        *over_chips(g),
        aliases={0: 1},
    )
    return call(
        seventh_kernel,
        (jax.ShapeDtypeStruct((models, width), F32), jax.ShapeDtypeStruct((models, rows), F32)),
        coefficients,
        from_partner(coefficients, "dp", 1),
        residual,
        residual_other,
    )


def solution(mesh):
    return jax.shard_map(
        body,
        mesh=mesh,
        in_specs=(P("dp", "vox"), P(None, "dp"), P(None, "vox"), P()),
        out_specs=(P(None, "vox"), P(None, "dp")),
        check_vma=False,
    )
```
